128 devices in a mesh: chain: 32 (over x, y, core), seq: 4 (over z).
Axes of the slice: x: 4, y: 4, z: 4, core: 2. Of those that a mesh axis runs over, the one named last changes fastest.
Arguments:
- tokens: bfloat16 [32, 3, 512, 768], P('chain', None, 'seq'), may hold values from -6 to 6
- documents: int32 [32, 3, 512], P('chain', None, 'seq'), may hold values from 0 to 4, as said below
- resets: int32 [32, 2], P('chain'), may hold values 0 or 1
- cotangent: bfloat16 [32, 3, 512, 768], P('chain', None, 'seq'), may hold values from -6 to 6
- query_weight: bfloat16 [768, 768], replicated, may hold values from -0.21875 to 0.21875
- query_bias: bfloat16 [768], replicated, may hold values from -1.25 to 1.25
- key_weight: bfloat16 [768, 768], replicated, may hold values from -0.21875 to 0.21875
- value_weight: bfloat16 [768, 768], replicated, may hold values from -0.21875 to 0.21875
- value_bias: bfloat16 [768], replicated, may hold values from -1.25 to 1.25
- mixer_weight: bfloat16 [768, 768], replicated, may hold values from -1.75 to 1.75
- mixer_bias: bfloat16 [768], replicated, may hold values from -1.25 to 1.25
- first_gain: bfloat16 [768], replicated, may hold values from 0.5 to 1.5
- first_shift: bfloat16 [768], replicated, may hold values from -1.25 to 1.25
- inner_weight: bfloat16 [768, 3072], replicated, may hold values from -0.21875 to 0.21875
- inner_bias: bfloat16 [3072], replicated, may hold values from -1.25 to 1.25
- outer_weight: bfloat16 [3072, 768], replicated, may hold values from -0.109375 to 0.109375
- outer_bias: bfloat16 [768], replicated, may hold values from -1.25 to 1.25
- second_gain: bfloat16 [768], replicated, may hold values from 0.5 to 1.5
- second_shift: bfloat16 [768], replicated, may hold values from -1.25 to 1.25
- memory_init: bfloat16 [20, 768], replicated, may hold values from -6 to 6
- write_offset: bfloat16 [20, 768], replicated, may hold values from -3 to 3
Outputs:
- layer_output: bfloat16 [32, 3, 512, 768], P('chain', None, 'seq')
- input_grad: float32 [32, 3, 512, 768], P('chain', None, 'seq')
- query_weight_grad: float32 [768, 768], replicated
- query_bias_grad: float32 [768], replicated
- key_weight_grad: float32 [768, 768], replicated
- value_weight_grad: float32 [768, 768], replicated
- value_bias_grad: float32 [768], replicated
- mixer_weight_grad: float32 [768, 768], replicated
- mixer_bias_grad: float32 [768], replicated
- first_gain_grad: float32 [768], replicated
- first_shift_grad: float32 [768], replicated
- inner_weight_grad: float32 [768, 3072], replicated
- inner_bias_grad: float32 [3072], replicated
- outer_weight_grad: float32 [3072, 768], replicated
- outer_bias_grad: float32 [768], replicated
- second_gain_grad: float32 [768], replicated
- second_shift_grad: float32 [768], replicated
- memory_init_grad: float32 [20, 768], replicated
- write_offset_grad: float32 [20, 768], replicated
- memory_norm: float32 [], replicated
The draws below stay inside these ranges and needn't reach their ends.
Inputs may be any that keep to these rules, and one draw needn't show every extreme that they name: `documents`: within a segment the ids never fall; a segment's first token has id 0 and its last token id 4.
All inputs are finite; a program needn't handle non-finite values. No bound on the sum of `resets` on one device may be relied on, other than what follows from the above.
Results may differ from the reference program's by a relative error of at most 0.04.
Values may be sent and summed in bfloat16 or wider, within the bound.
A program may use at most 256 MiB of HBM per device.

```python
import jax
import jax.numpy as jnp
from jax import lax

D = 768
HEADS = 12
FF = 3072
MEM = 20
SEG_DEV = 128
SEGS = 3
SEG = 512
CHAINS = 32


def draw_documents(key, part):
    key = jax.random.fold_in(key, 7)
    streams = jax.random.split(key, 4)
    shape = (CHAINS, SEGS, 1)
    start = jax.random.randint(streams[0], shape, 2, SEG_DEV)
    opening = jax.random.randint(streams[1], shape, 1, start)
    finish = jax.random.randint(streams[2], shape, SEG - SEG_DEV + 1, SEG)
    ending = jax.random.randint(streams[3], shape, finish, SEG)
    position = jnp.arange(SEG, dtype=jnp.int32)[None, None, :]
    labels = (position >= opening).astype(jnp.int32) + (position >= start).astype(jnp.int32)
    labels = labels + (position >= finish).astype(jnp.int32) + (position >= ending).astype(jnp.int32)
    return labels


def draw_cotangent(key, part):
    key = jax.random.fold_in(key, 11)
    place = jnp.arange(CHAINS, dtype=jnp.float32) / max(CHAINS - 1, 1)
    shape = (CHAINS, SEGS, SEG, D)
    base = jnp.clip(jax.random.normal(key, shape, jnp.float32), -3.4, 3.4)
    factor = 3.0 ** (0.5 * place)
    return (base * factor[:, None, None, None]).astype(jnp.bfloat16)


def set_ends(drawn, own_key, least, largest):
    index_at = [jax.random.randint(jax.random.fold_in(own_key, axis), (), 0, length) for axis, length in enumerate(drawn.shape)]
    widest = drawn.shape.index(max(drawn.shape))
    neighbour = index_at[:widest] + [(index_at[widest] + 1) % drawn.shape[widest]] + index_at[widest + 1:]
    return drawn.at[tuple(index_at)].set(least).at[tuple(neighbour)].set(largest)


def levels(stream_key, shape, shards, smallest, top_value):
    level, own = 1.0, jax.random.fold_in(stream_key, 6)
    for dim, shards_of in shards:
        steps = jnp.exp(jax.random.uniform(jax.random.fold_in(own, dim), (shards_of,), jnp.float32, smallest / len(shards), top_value / len(shards)))
        level = level * jnp.repeat(steps, shape[dim] // shards_of).reshape([-1 if axis == dim else 1 for axis in range(len(shape))])
    return level


def gaussian(own_key, shape, scale, most, pieces=(), kind=jnp.bfloat16):
    entries = scale * jax.random.normal(own_key, shape, jnp.float32)
    if pieces:
        entries = entries * levels(own_key, shape, pieces, -0.22, 0.18)
    return jnp.clip(entries, -most, most).astype(kind)


def setup_inputs(seed: int = 0) -> dict:
    splits = jax.random.split(jax.random.key(seed), 22)
    return {
        "tokens": gaussian(splits[0], (CHAINS, SEGS, SEG, D), 1.0, 6.0, ((0, 32), (2, 4))),
        "documents": draw_documents(jax.random.fold_in(splits[21], 71), 0),
        "resets": set_ends((jax.random.randint(splits[2], (CHAINS, SEGS - 1), 0, 3) < 1).astype(jnp.int32), jax.random.fold_in(splits[2], 1), 0, 1),
        "cotangent": draw_cotangent(jax.random.fold_in(splits[21], 71), 0),
        "query_weight": gaussian(splits[4], (D, D), D ** -0.5, 0.21875),
        "query_bias": gaussian(splits[5], (D,), 0.2, 1.25),
        "key_weight": gaussian(splits[6], (D, D), D ** -0.5, 0.21875),
        "value_weight": gaussian(splits[7], (D, D), D ** -0.5, 0.21875),
        "value_bias": gaussian(splits[8], (D,), 0.2, 1.25),
        "mixer_weight": gaussian(splits[9], (D, D), (D // 64) ** -0.5, 1.75),
        "mixer_bias": gaussian(splits[10], (D,), 0.2, 1.25),
        "first_gain": jnp.clip(1.0 + 0.1 * jax.random.normal(splits[11], (D,), jnp.float32), 0.5, 1.5).astype(jnp.bfloat16),
        "first_shift": gaussian(splits[12], (D,), 0.2, 1.25),
        "inner_weight": gaussian(splits[13], (D, FF), D ** -0.5, 0.21875),
        "inner_bias": gaussian(splits[14], (FF,), 0.2, 1.25),
        "outer_weight": gaussian(splits[15], (FF, D), FF ** -0.5, 0.109375),
        "outer_bias": gaussian(splits[16], (D,), 0.2, 1.25),
        "second_gain": jnp.clip(1.0 + 0.1 * jax.random.normal(splits[17], (D,), jnp.float32), 0.5, 1.5).astype(jnp.bfloat16),
        "second_shift": gaussian(splits[18], (D,), 0.2, 1.25),
        "memory_init": gaussian(splits[19], (MEM, D), 1.0, 6.0),
        "write_offset": gaussian(splits[20], (MEM, D), 0.5, 3.0),
    }


EPS = 1e-12
HIGH = lax.Precision.HIGHEST

@jax.custom_vjp
def low(v):
    return lax.optimization_barrier(v.astype(jnp.bfloat16)).astype(jnp.float32)

@jax.custom_vjp
def low_back(v):
    return v

def low_keep(v):
    return (low(v), None)

def low_pass(kept, grad):
    return (grad,)

def back_keep(v):
    return (v, None)

def back_low(kept, grad):
    return (low(grad),)
low.defvjp(low_keep, low_pass)
low_back.defvjp(back_keep, back_low)

def matmul(left, right):
    return jnp.dot(left, right, precision=HIGH, preferred_element_type=jnp.float32)

def layer_norm(hidden, gain, shift):
    centre = hidden - lax.optimization_barrier(jnp.mean(hidden, axis=-1, keepdims=True))
    spread = lax.optimization_barrier(jnp.mean(centre * centre, axis=-1, keepdims=True))
    return centre * lax.rsqrt(spread + EPS) * gain + shift

def attention(queries, keys, values, visible):
    count = queries.shape[0]
    depth = D // HEADS
    query_heads = queries.reshape(count, HEADS, depth)
    key_heads = keys.reshape(count, HEADS, depth)
    value_heads = values.reshape(count, HEADS, depth)
    scores = jnp.einsum('rhd,khd->hrk', query_heads, key_heads, precision=HIGH) * depth ** (-0.5)
    scores = low_back(scores)
    masked = jnp.where(visible[None], scores, -jnp.inf)
    peak = lax.optimization_barrier(jnp.max(masked, axis=-1, keepdims=True))
    weights = jnp.exp(masked - peak)
    probs = weights / lax.optimization_barrier(jnp.sum(weights, axis=-1, keepdims=True))
    mixed = jnp.einsum('hrk,khd->rhd', low(probs), value_heads, precision=HIGH)
    return mixed.reshape(count, D)

def segment(params, tokens, labels, memory):
    query_weight, query_bias, key_weight, value_weight, value_bias, mixer_weight, mixer_bias, first_gain, first_shift, inner_weight, inner_bias, outer_weight, outer_bias, second_gain, second_shift, memory_init, write_offset = params
    written_in = low(memory + write_offset)
    rows = jnp.concatenate([memory, tokens, written_in], axis=0)
    memory_marks = jnp.full((MEM,), -1, jnp.int32)
    marks = jnp.concatenate([memory_marks, labels.astype(jnp.int32), memory_marks])
    visible = (marks[:, None] == marks[None, :]) | (marks[:, None] < 0) | (marks[None, :] < 0)
    queries = low_back(low(matmul(rows, query_weight) + query_bias))
    keys = low_back(low(matmul(rows, key_weight)))
    values = low_back(low(matmul(rows, value_weight) + value_bias))
    mixed = low_back(low(jax.checkpoint(attention)(queries, keys, values, visible)))
    branch = low_back(matmul(mixed, mixer_weight) + mixer_bias)
    upper = layer_norm(rows + branch, first_gain, first_shift)
    inner = low_back(matmul(low(upper), inner_weight) + inner_bias)
    activated = low(jax.nn.gelu(inner, approximate=False))
    outer = low_back(matmul(activated, outer_weight) + outer_bias)
    result = layer_norm(upper + outer, second_gain, second_shift)
    return (result[MEM:MEM + SEG], result[MEM + SEG:])

def forward(token_values, deltas, documents, resets, params):
    memory_init = params[15]

    def chain(inputs):
        chain_tokens, chain_deltas, chain_docs, chain_resets = inputs
        outputs = []
        memory = memory_init + chain_deltas[0]
        written = memory
        for step in range(SEGS):
            if step > 0:
                memory = jnp.where(chain_resets[step - 1] > 0, memory_init, low(written)) + chain_deltas[step]
            result, written = jax.checkpoint(segment)(params, chain_tokens[step], chain_docs[step], memory)
            outputs.append(result)
        return jnp.stack(outputs)
    return lax.map(chain, (token_values, deltas, documents, resets))

def reference(tokens, documents, resets, cotangent, query_weight, query_bias, key_weight, value_weight, value_bias, mixer_weight, mixer_bias, first_gain, first_shift, inner_weight, inner_bias, outer_weight, outer_bias, second_gain, second_shift, memory_init, write_offset):
    params = tuple((weight.astype(jnp.float32) for weight in (query_weight, query_bias, key_weight, value_weight, value_bias, mixer_weight, mixer_bias, first_gain, first_shift, inner_weight, inner_bias, outer_weight, outer_bias, second_gain, second_shift, memory_init, write_offset)))
    token_values = tokens.astype(jnp.float32)
    deltas = jnp.zeros((CHAINS, SEGS, MEM, D), jnp.float32)

    def run(token_values, deltas, params):
        return forward(token_values, deltas, documents, resets, params)
    result, pull = jax.vjp(run, token_values, deltas, params)
    input_grad, memory_grads, grads = pull(cotangent.astype(jnp.float32))
    memory_norm = jnp.sqrt(jnp.mean(memory_grads * memory_grads))
    return (result.astype(jnp.bfloat16), input_grad, grads[0], grads[1], grads[2], grads[3], grads[4], grads[5], grads[6], grads[7], grads[8], grads[9], grads[10], grads[11], grads[12], grads[13], grads[14], grads[15], grads[16], memory_norm)
```

```python
import functools

import jax
import jax.numpy as jnp
from jax import lax
from jax.experimental import pallas as pl
from jax.experimental.pallas import tpu as pltpu
from jax.sharding import PartitionSpec as P

MESH = pl.DeviceIdType.MESH
LOW = jnp.bfloat16
F32 = jnp.float32
SEGS = 3
BLOCK = 128
MODEL = 768
INNER = 3072
SLOTS = 20
PAD = 32
MEMORY = 2 * PAD
ROWS = SEGS * BLOCK
TOKENS = 512
KEYS = 640
QUERIES = TOKENS + PAD
HEAD = 64
MINE = 3
GROUP = MINE * HEAD
TRIPLE = 3 * GROUP
SCALE = HEAD ** (-0.5)
EPS = 1e-12
HIDDEN = -1e30


def dot(left, right):
    return jnp.dot(left, right, preferred_element_type=F32)


def dot_t(left, right):
    return lax.dot_general(left, right, (((1,), (1,)), ((), ())), preferred_element_type=F32)


def t_dot(left, right):
    return lax.dot_general(left, right, (((0,), (0,)), ((), ())), preferred_element_type=F32)


def norm_parts(hidden):
    centre = hidden - jnp.mean(hidden, axis=-1, keepdims=True)
    spread = jnp.mean(centre * centre, axis=-1, keepdims=True)
    inverse = lax.rsqrt(spread + EPS)
    return centre * inverse, inverse


def norm_back(upstream, unit, inverse, gain):
    scaled = upstream * gain
    first = jnp.mean(scaled, axis=-1, keepdims=True)
    second = jnp.mean(scaled * unit, axis=-1, keepdims=True)
    return (scaled - first - unit * second) * inverse


def gelu_parts(values):
    below = 0.5 * (1.0 + lax.erf(values * (0.5**0.5)))
    density = jnp.exp(-0.5 * values * values) * 0.3989422804014327
    return values * below, below + values * density


def column_sum(values):
    return jnp.sum(values.astype(F32), axis=0, keepdims=True)


def ring(off):
    return lax.rem(lax.axis_index("seq") + off + 4, 4)


def ring_barrier():
    barrier = pltpu.get_barrier_semaphore()
    for off in (1, 2, 3):
        pl.semaphore_signal(
            barrier, inc=1, device_id=(lax.axis_index("chain"), ring(off)), device_id_type=MESH
        )
    pl.semaphore_wait(barrier, 3)


def push(started, src, dst, s_sem, r_sem, off):
    copy = pltpu.make_async_remote_copy(
        src_ref=src,
        dst_ref=dst,
        send_sem=s_sem,
        recv_sem=r_sem,
        device_id=(lax.axis_index("chain"), ring(off)),
        device_id_type=MESH,
    )
    copy.start()
    started.append(copy)
    return copy


def fetch(pairs, sems):
    copies = [pltpu.make_async_copy(src, dst, sems.at[i]) for i, (src, dst) in enumerate(pairs)]
    for copy in copies:
        copy.start()
    return copies


QUERY_B, VALUE_B, MIXER_B, GAIN_1, SHIFT_1, OUTER_B, GAIN_2, SHIFT_2 = range(8)


def forward_kernel(
    resets, tok, docs, init, offset, vec, inner_b,
    wq_h, wk_h, wv_h, wm_h, wi_h, wo_h,
    kv, probs, orow, ow, h1w, zw, h2w, xm,
    wq, wk, wv, wm, wi, wo, wown, vown, sbuf, lab, bias, osend, owsend,
    w_sem, q_s, q_r, o_s, o_r, m_s, m_r, l_s, l_r,
):
    z = lax.axis_index("seq")
    fetched = fetch(
        [(wq_h, wq), (wk_h, wk), (wv_h, wv), (wm_h, wm), (wi_h, wi), (wo_h, wo)], w_sem
    )
    started = []
    ring_barrier()
    lab[pl.ds(z, 1)] = docs[...][None]
    label_copies = [
        push(started, docs, lab.at[z], l_s.at[d - 1], l_r.at[d - 1], d) for d in (1, 2, 3)
    ]
    tokens = tok[...].reshape(ROWS, MODEL)
    fetched[0].wait()
    queries = ((dot(tokens, wq[...]) + vec[QUERY_B : QUERY_B + 1, :]) * SCALE).astype(LOW)
    for g in range(4):
        for s in range(SEGS):
            sbuf[g, s, :, 0:GROUP] = queries[
                s * BLOCK : (s + 1) * BLOCK, g * GROUP : (g + 1) * GROUP
            ]
    fetched[1].wait()
    keys = dot(tokens, wk[...]).astype(LOW)
    for g in range(4):
        for s in range(SEGS):
            sbuf[g, s, :, GROUP : 2 * GROUP] = keys[
                s * BLOCK : (s + 1) * BLOCK, g * GROUP : (g + 1) * GROUP
            ]
    fetched[2].wait()
    values = (dot(tokens, wv[...]) + vec[VALUE_B : VALUE_B + 1, :]).astype(LOW)
    for g in range(4):
        for s in range(SEGS):
            sbuf[g, s, :, 2 * GROUP :] = values[
                s * BLOCK : (s + 1) * BLOCK, g * GROUP : (g + 1) * GROUP
            ]
    here = pl.ds(pl.multiple_of(z * BLOCK, BLOCK), BLOCK)
    row_copies = []
    for s in range(SEGS):
        row_copies.append(
            [
                push(
                    started, sbuf.at[ring(d), s], kv.at[s, here],
                    q_s.at[s, d - 1], q_r.at[s, d - 1], d,
                )
                for d in (1, 2, 3)
            ]
        )
    for s in range(SEGS):
        kv[s, here, :] = sbuf[z, s]
        kv[s, TOKENS + MEMORY :, :] = jnp.zeros((KEYS - TOKENS - MEMORY, TRIPLE), LOW)
    for g in range(4):

        @pl.when(z == g)
        def _():
            cut = slice(g * GROUP, (g + 1) * GROUP)
            wown[:, 0:GROUP] = wq[:, cut]
            wown[:, GROUP : 2 * GROUP] = wk[:, cut]
            wown[:, 2 * GROUP :] = wv[:, cut]
            vown[0:1, 0:GROUP] = vec[QUERY_B : QUERY_B + 1, cut]
            vown[0:1, GROUP : 2 * GROUP] = jnp.zeros((1, GROUP), F32)
            vown[0:1, 2 * GROUP :] = vec[VALUE_B : VALUE_B + 1, cut]

    lane = lax.broadcasted_iota(jnp.int32, (1, TRIPLE), 1)
    factor = jnp.where(lane < GROUP, SCALE, 1.0)
    slot = lax.broadcasted_iota(jnp.int32, (PAD, MODEL), 0)
    key_lane = lax.broadcasted_iota(jnp.int32, (PAD, KEYS), 1)
    filled = (key_lane < TOKENS + SLOTS) | (
        (key_lane >= TOKENS + PAD) & (key_lane < TOKENS + PAD + SLOTS)
    )
    write_bias = jnp.where(filled, 0.0, HIDDEN)

    def attend(query_rows, mask, s, row_at, rows):
        parts = []
        for h in range(MINE):
            key_head = kv[s, :, GROUP + h * HEAD : GROUP + (h + 1) * HEAD]
            value_head = kv[s, :, 2 * GROUP + h * HEAD : 2 * GROUP + (h + 1) * HEAD]
            scores = dot_t(query_rows[:, h * HEAD : (h + 1) * HEAD], key_head) + mask
            weights = jnp.exp(scores - jnp.max(scores, axis=-1, keepdims=True))
            total = jnp.sum(weights, axis=-1, keepdims=True)
            prob = (weights * (1.0 / total)).astype(LOW)
            probs[s, h, pl.ds(row_at, rows), :] = prob
            parts.append(dot(prob, value_head))
        return jnp.concatenate(parts, axis=1).astype(LOW)

    memory = init[...]
    for copy in label_copies:
        copy.wait_recv()
    out_copies = []
    for s in range(SEGS):
        written_in = (memory.astype(F32) + offset[...].astype(F32)).astype(LOW)
        xm[s, 0:PAD, :] = written_in
        xm[s, PAD:, :] = memory
        kv[s, TOKENS : TOKENS + MEMORY, :] = (
            (dot(xm[s], wown[...]) + vown[0:1, :]) * factor
        ).astype(LOW)
        for i in range(4):
            column = jnp.transpose(jnp.broadcast_to(lab[i, s : s + 1, :].astype(F32), (BLOCK, BLOCK)))
            for j in range(4):
                row = jnp.broadcast_to(lab[j, s : s + 1, :].astype(F32), (BLOCK, BLOCK))
                bias[i * BLOCK : (i + 1) * BLOCK, j * BLOCK : (j + 1) * BLOCK] = jnp.where(
                    column == row, 0.0, HIDDEN
                )
            bias[i * BLOCK : (i + 1) * BLOCK, TOKENS:] = jnp.broadcast_to(
                write_bias[0:1, TOKENS:], (BLOCK, BLOCK)
            )
        for copy in row_copies[s]:
            copy.wait_recv()
        if s < SEGS - 1:
            mixed = attend(kv[s, TOKENS : TOKENS + PAD, :], write_bias, s, TOKENS, PAD)
            owsend[s] = mixed
            ow[s, pl.ds(z, 1)] = mixed[None]
            write_copies = [
                push(started, owsend.at[s], ow.at[s, z], m_s.at[s, d - 1], m_r.at[s, d - 1], d)
                for d in (1, 2, 3)
            ]

        def block(i, carry):
            row_at = pl.multiple_of(i * BLOCK, BLOCK)
            rows = pl.ds(row_at, BLOCK)
            osend[s, i] = attend(kv[s, rows, :], bias[rows, :], s, row_at, BLOCK)
            return carry

        lax.fori_loop(0, 4, block, 0)
        part = slice(s * BLOCK, (s + 1) * BLOCK)
        out_copies += [
            push(
                started, osend.at[s, ring(d)], orow.at[z, part],
                o_s.at[s, d - 1], o_r.at[s, d - 1], d,
            )
            for d in (1, 2, 3)
        ]
        orow[z, part, :] = osend[s, z]
        if s < SEGS - 1:
            if s == 0:
                for copy in fetched[3:]:
                    copy.wait()
            for copy in write_copies:
                copy.wait_recv()
            hidden = xm[s, 0:PAD, :].astype(F32) + vec[MIXER_B : MIXER_B + 1, :]
            for g in range(4):
                hidden = hidden + dot(ow[s, g], wm[g * GROUP : (g + 1) * GROUP, :])
            h1w[s] = hidden
            unit, _ = norm_parts(hidden)
            upper = unit * vec[GAIN_1 : GAIN_1 + 1, :] + vec[SHIFT_1 : SHIFT_1 + 1, :]
            inner = dot(upper.astype(LOW), wi[...]) + inner_b[...]
            zw[s] = inner
            active, _ = gelu_parts(inner)
            hidden = upper + dot(active.astype(LOW), wo[...]) + vec[OUTER_B : OUTER_B + 1, :]
            h2w[s] = hidden
            unit, _ = norm_parts(hidden)
            result = unit * vec[GAIN_2 : GAIN_2 + 1, :] + vec[SHIFT_2 : SHIFT_2 + 1, :]
            flag = jnp.full((PAD, MODEL), resets[0, s], jnp.int32)
            result = jnp.where(flag > 0, init[...].astype(F32), result)
            memory = jnp.where(slot < SLOTS, result, 0.0).astype(LOW)
    for copy in out_copies:
        copy.wait_recv()
    for copy in started:
        copy.wait_send()


def shape(dims, kind=LOW):
    return jax.ShapeDtypeStruct(dims, kind)


VMEM = pl.BlockSpec(memory_space=pltpu.VMEM)
ANY = pl.BlockSpec(memory_space=pl.ANY)
DMA = pltpu.SemaphoreType.DMA


def weight_buffers():
    return [pltpu.VMEM((MODEL, MODEL), LOW) for _ in range(4)] + [
        pltpu.VMEM((MODEL, INNER), LOW),
        pltpu.VMEM((INNER, MODEL), LOW),
    ]


def forward(resets, tok, docs, init, offset, vec, inner_b, weights):
    return pl.pallas_call(
        forward_kernel,
        out_shape=(
            shape((SEGS, KEYS, TRIPLE)),
            shape((SEGS, MINE, QUERIES, KEYS)),
            shape((4, ROWS, GROUP)),
            shape((2, 4, PAD, GROUP)),
            shape((2, PAD, MODEL), F32),
            shape((2, PAD, INNER), F32),
            shape((2, PAD, MODEL), F32),
            shape((SEGS, MEMORY, MODEL)),
        ),
        in_specs=[pl.BlockSpec(memory_space=pltpu.SMEM)] + [VMEM] * 6 + [ANY] * 6,
        out_specs=(VMEM,) * 8,
        scratch_shapes=weight_buffers()
        + [
            pltpu.VMEM((MODEL, TRIPLE), LOW),
            pltpu.VMEM((8, TRIPLE), F32),
            pltpu.VMEM((4, SEGS, BLOCK, TRIPLE), LOW),
            pltpu.VMEM((4, SEGS, BLOCK), jnp.int32),
            pltpu.VMEM((TOKENS, KEYS), F32),
            pltpu.VMEM((SEGS, 4, BLOCK, GROUP), LOW),
            pltpu.VMEM((2, PAD, GROUP), LOW),
            DMA((6,)),
            DMA((SEGS, 3)),
            DMA((SEGS, 3)),
            DMA((SEGS, 3)),
            DMA((SEGS, 3)),
            DMA((2, 3)),
            DMA((2, 3)),
            DMA((3,)),
            DMA((3,)),
        ],
        compiler_params=pltpu.CompilerParams(
            collective_id=1, has_side_effects=True, vmem_limit_bytes=60 << 20
        ),
        name="forward_attention",
    )(resets, tok, docs, init, offset, vec, inner_b, *weights)


WIDE = 768
HALF = 4608
PART = 1536
CHUNK = 384
SUB = 96
ORDERS = (("x", "y", "z"), ("y", "z", "x"), ("z", "x", "y"))


def places():
    chain = lax.axis_index("chain")
    return {
        "x": chain // 8,
        "y": lax.rem(chain // 2, 4),
        "z": lax.axis_index("seq"),
        "core": lax.rem(chain, 2),
    }


def peer(at, axis, off):
    at = dict(at)
    size = 2 if axis == "core" else 4
    at[axis] = lax.rem(at[axis] + off + size, size)
    return ((at["x"] * 4 + at["y"]) * 2 + at["core"], at["z"])


def greet(at, peers):
    barrier = pltpu.get_barrier_semaphore()
    for axis, off in peers:
        pl.semaphore_signal(barrier, inc=1, device_id=peer(at, axis, off), device_id_type=MESH)
    pl.semaphore_wait(barrier, len(peers))


ALL_PEERS = [("core", 1)] + [(axis, off) for axis in "xyz" for off in (1, 2, 3)]


def add_rows(out, out_start, terms, rows, step=48):
    def body(i, carry):
        base = i * step
        total = None
        for ref, start in terms:
            term = ref[pl.ds(pl.multiple_of(start + base, 16), step), :].astype(jnp.float32)
            total = term if total is None else total + term
        out[pl.ds(pl.multiple_of(out_start + base, 16), step), :] = total.astype(out.dtype)
        return carry

    lax.fori_loop(0, rows // step, body, 0)


def sum_kernel(
    g, ext, w, e, crecv, r1, r2, r3, r4, ecore, ex, ey, ez,
    c_s, c_r, a1_s, a1_r, a2_s, a2_r, b_s, b_r, d_s, d_r,
    gd_s, gd_r, gb_s, gb_r, g1_s, g1_r, g2_s, g2_r, gc_s, gc_r,
    e_s, e_r,
):
    at = places()
    greet(at, ALL_PEERS)
    started = []

    def send(src, dst, s_sem, r_sem, axis, off):
        copy = pltpu.make_async_remote_copy(
            src_ref=src, dst_ref=dst, send_sem=s_sem, recv_sem=r_sem,
            device_id=peer(at, axis, off), device_id_type=MESH,
        )
        copy.start()
        started.append(copy)
        return copy

    core = at["core"]
    mine = core * HALF
    theirs = (1 - core) * HALF

    def turn(value, off):
        return lax.rem(value + off + 4, 4)

    def ds(start, size):
        return pl.ds(pl.multiple_of(start, 16), size)

    place1 = [at[order[0]] for order in ORDERS]
    place2 = [at[order[1]] for order in ORDERS]
    place3 = [at[order[2]] for order in ORDERS]

    def rel(p, off):
        return p * PART + turn(place1[p], off) * CHUNK

    core_copies = {}
    e_core = send(
        ext.at[pl.ds(pl.multiple_of((1 - core) * 32, 8), 32)], ecore, e_s.at[0], e_r.at[0], "core", 1
    )
    for j, off in enumerate((2, 1, 3, 0)):
        for p in range(3):
            start = rel(p, off)
            core_copies[p, off] = send(
                g.at[ds(theirs + start, CHUNK)], crecv.at[ds(start, CHUNK)],
                c_s.at[p, j], c_r.at[p, j], "core", 1,
            )

    def own(p, off):
        core_copies[p, off].wait_recv()
        start = rel(p, off)
        add_rows(crecv, start, [(g, mine + start), (crecv, start)], CHUNK)

    e_core.wait_recv()
    ecore[...] = ext[pl.ds(pl.multiple_of(core * 32, 8), 32), :] + ecore[...]
    e_x = [
        send(
            ecore.at[pl.ds(pl.multiple_of(turn(at["x"], d) * 8, 8), 8)],
            ex.at[d - 1], e_s.at[d], e_r.at[d], "x", d,
        )
        for d in (1, 2, 3)
    ]
    first = {}
    for p in range(3):
        own(p, 2)
        start = rel(p, 2)
        axis = ORDERS[p][0]
        first[p] = (
            send(crecv.at[ds(start, CHUNK // 2)], r1.at[p, 0], a1_s.at[p, 0], a1_r.at[p, 0], axis, 1),
            send(
                crecv.at[ds(start + CHUNK // 2, CHUNK // 2)], r1.at[p, 1],
                a1_s.at[p, 1], a1_r.at[p, 1], axis, 3,
            ),
        )
    for off in (1, 3, 0):
        for p in range(3):
            own(p, off)
    second = {}
    for p in range(3):
        axis = ORDERS[p][0]
        start = rel(p, 1)
        first[p][0].wait_recv()
        add_rows(crecv, start, [(crecv, start), (r1.at[p, 0], 0)], CHUNK // 2)
        right = send(crecv.at[ds(start, CHUNK)], r2.at[p, 0], a2_s.at[p, 0], a2_r.at[p, 0], axis, 1)
        start = rel(p, 3)
        first[p][1].wait_recv()
        add_rows(
            crecv, start + CHUNK // 2, [(crecv, start + CHUNK // 2), (r1.at[p, 1], 0)], CHUNK // 2
        )
        left = send(crecv.at[ds(start, CHUNK)], r2.at[p, 1], a2_s.at[p, 1], a2_r.at[p, 1], axis, 3)
        second[p] = (right, left)
    e_own = pl.ds(pl.multiple_of(core * 32 + at["x"] * 8, 8), 8)
    for copy in e_x:
        copy.wait_recv()
    ey[pl.ds(at["y"], 1)] = (ecore[pl.ds(pl.multiple_of(at["x"] * 8, 8), 8), :] + ex[0] + ex[1] + ex[2])[None]
    e_y = [
        send(ey.at[at["y"]], ey.at[at["y"]], e_s.at[3 + d], e_r.at[3 + d], "y", d)
        for d in (1, 2, 3)
    ]
    third = {}
    for p in range(3):
        start = rel(p, 0)
        for copy in second[p]:
            copy.wait_recv()
        add_rows(crecv, start, [(crecv, start), (r2.at[p, 0], 0), (r2.at[p, 1], 0)], CHUNK)
        third[p] = [
            send(
                crecv.at[ds(start + turn(place2[p], d) * SUB, SUB)], r3.at[p, d - 1],
                b_s.at[p, d - 1], b_r.at[p, d - 1], ORDERS[p][1], d,
            )
            for d in (1, 2, 3)
        ]
    for copy in e_y:
        copy.wait_recv()
    ez[pl.ds(at["z"], 1)] = (ey[0] + ey[1] + ey[2] + ey[3])[None]
    e_z = [
        send(ez.at[at["z"]], ez.at[at["z"]], e_s.at[6 + d], e_r.at[6 + d], "z", d)
        for d in (1, 2, 3)
    ]
    fourth = {}

    def quarter(ref, start, c):
        return ref.at[ds(start + (c // 2) * (SUB // 2), SUB // 2), pl.ds(pl.multiple_of(lax.rem(c, 2) * (WIDE // 2), 128), WIDE // 2)]

    for p in range(3):
        start = rel(p, 0) + place2[p] * SUB
        for copy in third[p]:
            copy.wait_recv()
        add_rows(crecv, start, [(crecv, start)] + [(r3.at[p, d], 0) for d in range(3)], SUB)
        fourth[p] = [
            send(
                quarter(crecv, start, turn(place3[p], d)), r4.at[p, d - 1],
                d_s.at[p, d - 1], d_r.at[p, d - 1], ORDERS[p][2], d,
            )
            for d in (1, 2, 3)
        ]
    for copy in e_z:
        copy.wait_recv()
    e[e_own, :] = ez[0] + ez[1] + ez[2] + ez[3]
    e_back = [
        send(e.at[e_own], e.at[e_own], e_s.at[9 + d], e_r.at[9 + d], "x", d) for d in (1, 2, 3)
    ]
    fifth = {}
    for p in range(3):
        start = rel(p, 0) + place2[p] * SUB
        for copy in fourth[p]:
            copy.wait_recv()
        total = quarter(crecv, start, place3[p])[...].astype(jnp.float32)
        for d in range(3):
            total = total + r4[p, d].astype(jnp.float32)
        piece = quarter(w, mine + start, place3[p])
        piece[...] = total.astype(w.dtype)
        fifth[p] = [
            send(piece, piece, gd_s.at[p, d - 1], gd_r.at[p, d - 1], ORDERS[p][2], d)
            for d in (1, 2, 3)
        ]
    sixth = {}
    for p in range(3):
        start = mine + rel(p, 0) + place2[p] * SUB
        for copy in fifth[p]:
            copy.wait_recv()
        piece = w.at[ds(start, SUB)]
        sixth[p] = [
            send(piece, piece, gb_s.at[p, d - 1], gb_r.at[p, d - 1], ORDERS[p][1], d)
            for d in (1, 2, 3)
        ]
    for copy in e_back:
        copy.wait_recv()
    e_half = e.at[pl.ds(pl.multiple_of(core * 32, 8), 32)]
    e_last = send(e_half, e_half, e_s.at[13], e_r.at[13], "core", 1)
    seventh = {}
    last = []

    def across(p, j, start, rows):
        piece = w.at[ds(start, rows)]
        last.append(send(piece, piece, gc_s.at[p, j], gc_r.at[p, j], "core", 1))

    for p in range(3):
        start = mine + rel(p, 0)
        for copy in sixth[p]:
            copy.wait_recv()
        piece = w.at[ds(start, CHUNK)]
        axis = ORDERS[p][0]
        seventh[p] = (
            send(piece, piece, g1_s.at[p, 0], g1_r.at[p, 0], axis, 1),
            send(piece, piece, g1_s.at[p, 1], g1_r.at[p, 1], axis, 3),
        )
        across(p, 0, start, CHUNK)
    eighth = {}
    for p in range(3):
        axis = ORDERS[p][0]
        seventh[p][0].wait_recv()
        start = mine + rel(p, 3)
        piece = w.at[ds(start, CHUNK // 2)]
        right = send(piece, piece, g2_s.at[p, 0], g2_r.at[p, 0], axis, 1)
        across(p, 1, start, CHUNK)
        seventh[p][1].wait_recv()
        start = mine + rel(p, 1)
        piece = w.at[ds(start + CHUNK // 2, CHUNK // 2)]
        left = send(piece, piece, g2_s.at[p, 1], g2_r.at[p, 1], axis, 3)
        across(p, 2, start, CHUNK)
        eighth[p] = (right, left)
    for p in range(3):
        start = mine + rel(p, 2)
        for i in range(2):
            eighth[p][i].wait_recv()
            across(p, 3 + i, start + i * (CHUNK // 2), CHUNK // 2)
    e_last.wait_recv()
    for copy in last:
        copy.wait_recv()
    for copy in started:
        copy.wait_send()


def sum_all(g, ext):
    dma = pltpu.SemaphoreType.DMA
    pairs = [(3, 4), (3, 2), (3, 2), (3, 3), (3, 3), (3, 3), (3, 3), (3, 2), (3, 2), (3, 5), (14,)]
    sems = [dma(shape) for shape in pairs for _ in range(2)]
    vmem = pl.BlockSpec(memory_space=pltpu.VMEM)
    return pl.pallas_call(
        sum_kernel,
        out_shape=(
            jax.ShapeDtypeStruct((2 * HALF, WIDE), jnp.bfloat16),
            jax.ShapeDtypeStruct((64, WIDE), jnp.float32),
        ),
        in_specs=[vmem, vmem],
        out_specs=(vmem, vmem),
        scratch_shapes=[
            pltpu.VMEM((HALF, WIDE), jnp.bfloat16),
            pltpu.VMEM((3, 2, CHUNK // 2, WIDE), jnp.bfloat16),
            pltpu.VMEM((3, 2, CHUNK, WIDE), jnp.bfloat16),
            pltpu.VMEM((3, 3, SUB, WIDE), jnp.bfloat16),
            pltpu.VMEM((3, 3, SUB // 2, WIDE // 2), jnp.bfloat16),
            pltpu.VMEM((32, WIDE), jnp.float32),
            pltpu.VMEM((3, 8, WIDE), jnp.float32),
            pltpu.VMEM((4, 8, WIDE), jnp.float32),
            pltpu.VMEM((4, 8, WIDE), jnp.float32),
        ] + sems,
        compiler_params=pltpu.CompilerParams(
            collective_id=7, has_side_effects=True, vmem_limit_bytes=60 << 20
        ),
        name="sum_all",
    )(g, ext)


def middle_kernel(
    tok, orow, cot, vec, inner_b, wm_h, wi_h, wo_h,
    out, ub, act, dz, df, da, dh1, dout, sums, inner_sum,
    wm, wi, wo, slope, total, unit_1, inverse_1, w_sem,
):
    fetched = fetch([(wm_h, wm), (wi_h, wi), (wo_h, wo)], w_sem)
    gain_1 = vec[GAIN_1 : GAIN_1 + 1, :]
    gain_2 = vec[GAIN_2 : GAIN_2 + 1, :]
    hidden = tok[...].reshape(ROWS, MODEL).astype(F32) + vec[MIXER_B : MIXER_B + 1, :]
    fetched[0].wait()
    for g in range(4):
        hidden = hidden + dot(orow[g], wm[g * GROUP : (g + 1) * GROUP, :])
    unit, inverse = norm_parts(hidden)
    unit_1[...] = unit
    inverse_1[...] = inverse
    upper = unit * gain_1 + vec[SHIFT_1 : SHIFT_1 + 1, :]
    ub[...] = upper.astype(LOW)
    total[...] = upper + vec[OUTER_B : OUTER_B + 1, :]
    for copy in fetched[1:]:
        copy.wait()

    def ahead(j, carry):
        cut = pl.ds(pl.multiple_of(j * MODEL, MODEL), MODEL)
        inner = dot(ub[...], wi[:, cut]) + inner_b[:, cut]
        active, slant = gelu_parts(inner)
        active = active.astype(LOW)
        act[:, cut] = active
        slope[:, cut] = slant
        total[...] += dot(active, wo[cut, :])
        return carry

    lax.fori_loop(0, INNER // MODEL, ahead, 0)
    unit, inverse = norm_parts(total[...])
    result = unit * gain_2 + vec[SHIFT_2 : SHIFT_2 + 1, :]
    out[...] = result.astype(LOW).reshape(1, SEGS, BLOCK, MODEL)
    upstream = cot[...].reshape(ROWS, MODEL).astype(F32)
    sums[GAIN_2 : GAIN_2 + 1, :] = column_sum(upstream * unit)
    sums[SHIFT_2 : SHIFT_2 + 1, :] = column_sum(upstream)
    d_hidden = norm_back(upstream, unit, inverse, gain_2)
    total[...] = d_hidden
    d_low = d_hidden.astype(LOW)
    df[...] = d_low
    sums[OUTER_B : OUTER_B + 1, :] = column_sum(d_low)

    def back(j, carry):
        cut = pl.ds(pl.multiple_of(j * MODEL, MODEL), MODEL)
        d_inner = (dot_t(df[...], wo[cut, :]) * slope[:, cut]).astype(LOW)
        dz[:, cut] = d_inner
        inner_sum[:, cut] = column_sum(d_inner)
        total[...] += dot_t(d_inner, wi[:, cut])
        return carry

    lax.fori_loop(0, INNER // MODEL, back, 0)
    upstream = total[...]
    unit = unit_1[...]
    sums[GAIN_1 : GAIN_1 + 1, :] = column_sum(upstream * unit)
    sums[SHIFT_1 : SHIFT_1 + 1, :] = column_sum(upstream)
    d_hidden = norm_back(upstream, unit, inverse_1[...], gain_1)
    dh1[...] = d_hidden
    d_low = d_hidden.astype(LOW)
    da[...] = d_low
    sums[MIXER_B : MIXER_B + 1, :] = column_sum(d_low)
    sums[QUERY_B : QUERY_B + 2, :] = jnp.zeros((2, MODEL), F32)
    for g in range(4):
        dout[g] = dot_t(d_low, wm[g * GROUP : (g + 1) * GROUP, :]).astype(LOW)


def middle(tok, orow, cot, vec, inner_b, weights):
    return pl.pallas_call(
        middle_kernel,
        out_shape=(
            shape((1, SEGS, BLOCK, MODEL)),
            shape((ROWS, MODEL)),
            shape((ROWS, INNER)),
            shape((ROWS, INNER)),
            shape((ROWS, MODEL)),
            shape((ROWS, MODEL)),
            shape((ROWS, MODEL), F32),
            shape((4, ROWS, GROUP)),
            shape((8, MODEL), F32),
            shape((1, INNER), F32),
        ),
        in_specs=[VMEM] * 5 + [ANY] * 3,
        out_specs=(VMEM,) * 10,
        scratch_shapes=[
            pltpu.VMEM((MODEL, MODEL), LOW),
            pltpu.VMEM((MODEL, INNER), LOW),
            pltpu.VMEM((INNER, MODEL), LOW),
            pltpu.VMEM((ROWS, INNER), F32),
            pltpu.VMEM((ROWS, MODEL), F32),
            pltpu.VMEM((ROWS, MODEL), F32),
            pltpu.VMEM((ROWS, 1), F32),
            DMA((3,)),
        ],
        compiler_params=pltpu.CompilerParams(vmem_limit_bytes=60 << 20),
        name="token_layer",
    )(tok, orow, cot, vec, inner_b, *weights[3:])


def backward_kernel(
    resets, dout, kv, probs, h1w, zw, h2w, vec,
    wq_h, wk_h, wv_h, wm_h, wi_h, wo_h,
    drow, dmem, ubw, gw, dzw, dfw, daw, small,
    wq, wk, wv, wm, wi, wo, doh, dow, ds, acc, dsend, msend, wide,
    w_sem, d_s, d_r, x_s, x_r, m_s, m_r,
):
    z = lax.axis_index("seq")
    fetched = fetch(
        [(wq_h, wq), (wk_h, wk), (wv_h, wv), (wm_h, wm), (wi_h, wi), (wo_h, wo)], w_sem
    )
    started = []
    ring_barrier()
    here = pl.ds(pl.multiple_of(z * BLOCK, BLOCK), BLOCK)
    in_copies = {}
    for s in reversed(range(SEGS)):
        part = slice(s * BLOCK, (s + 1) * BLOCK)
        in_copies[s] = [
            push(
                started, dout.at[ring(d), part], doh.at[s, here],
                d_s.at[s, d - 1], d_r.at[s, d - 1], d,
            )
            for d in (1, 2, 3)
        ]
        doh[s, here, :] = dout[z, part, :]
    gain_1 = vec[GAIN_1 : GAIN_1 + 1, :]
    gain_2 = vec[GAIN_2 : GAIN_2 + 1, :]

    def head_back(s, h, d_rows, rows):
        cut = slice(h * HEAD, (h + 1) * HEAD)
        key_head = kv[s, :, GROUP + h * HEAD : GROUP + (h + 1) * HEAD]
        value_head = kv[s, :, 2 * GROUP + h * HEAD : 2 * GROUP + (h + 1) * HEAD]
        d_head = d_rows[:, cut]
        prob = probs[s, h, rows, :]
        wide_prob = prob.astype(F32)
        product = wide_prob * dot_t(d_head, value_head)
        delta = jnp.sum(product, axis=-1, keepdims=True)
        d_scores = (product - wide_prob * delta).astype(LOW)
        d_query = (dot(d_scores, key_head) * SCALE).astype(LOW)
        d_key = t_dot(d_scores, kv[s, rows, cut])
        d_value = t_dot(prob, d_head)
        return d_query, d_key, d_value

    def tokens_back(s):
        for copy in in_copies[s]:
            copy.wait_recv()
        rows = slice(0, TOKENS)
        for h in range(MINE):
            cut = slice(h * HEAD, (h + 1) * HEAD)
            d_query, d_key, d_value = head_back(s, h, doh[s], rows)
            dsend[s, :, cut] = d_query
            acc[s, :, cut] = d_key
            acc[s, :, GROUP + h * HEAD : GROUP + (h + 1) * HEAD] = d_value

    def writes_back(s):
        rows = slice(TOKENS, TOKENS + PAD)
        for h in range(MINE):
            cut = slice(h * HEAD, (h + 1) * HEAD)
            d_query, d_key, d_value = head_back(s, h, dow[...], rows)
            msend[s, 0:PAD, cut] = d_query
            acc[s, :, cut] += d_key
            acc[s, :, GROUP + h * HEAD : GROUP + (h + 1) * HEAD] += d_value

    mem_copies = {}
    row_copies = []

    def finish(s):
        if s == SEGS - 1:
            msend[s, :, 0:GROUP] = jnp.zeros((MEMORY, GROUP), LOW)
        else:
            msend[s, PAD:, 0:GROUP] = jnp.zeros((PAD, GROUP), LOW)
        msend[s, :, GROUP:] = acc[s, TOKENS : TOKENS + MEMORY, :].astype(LOW)
        mem_copies[s] = [
            push(started, msend.at[s], dmem.at[s, z], m_s.at[s, d - 1], m_r.at[s, d - 1], d)
            for d in (1, 2, 3)
        ]
        dmem[s, z] = msend[s]
        dsend[s, :, GROUP:] = acc[s, 0:TOKENS, :].astype(LOW)
        part = slice(s * BLOCK, (s + 1) * BLOCK)
        for d in (1, 2, 3):
            there = pl.ds(pl.multiple_of(ring(d) * BLOCK, BLOCK), BLOCK)
            row_copies.append(
                push(
                    started, dsend.at[s, there], drow.at[z, part],
                    x_s.at[s, d - 1], x_r.at[s, d - 1], d,
                )
            )
        drow[z, part, :] = dsend[s, here, :]

    sums = {}

    def add(name, value):
        sums[name] = value if name not in sums else sums[name] + value

    saved = {}

    def memory_back(s):
        for copy in mem_copies[s]:
            copy.wait_recv()
        for g in range(4):
            for t in range(3):
                wide[t, :, g * GROUP : (g + 1) * GROUP] = dmem[
                    s, g, :, t * GROUP : (t + 1) * GROUP
                ]
        if s == SEGS - 1:
            for copy in fetched:
                copy.wait()
        d_rows = dot_t(wide[0], wq[...]) + dot_t(wide[1], wk[...]) + dot_t(wide[2], wv[...])
        write = d_rows[0:PAD]
        if s < SEGS - 1:
            write = write + saved[s]
        grad = write + d_rows[PAD:]
        add("offset", write)
        add("norm", jnp.sum(jnp.sum(grad * grad, axis=0, keepdims=True), axis=1, keepdims=True))
        if s == 0:
            add("init", grad)
            return None
        flag = jnp.full((PAD, MODEL), resets[0, s - 1], jnp.int32) > 0
        add("init", jnp.where(flag, grad, 0.0))
        return jnp.where(flag, 0.0, grad)

    def layer_back(s, upstream):
        unit, inverse = norm_parts(h2w[s])
        add("gain_2", column_sum(upstream * unit))
        add("shift_2", column_sum(upstream))
        d_second = norm_back(upstream, unit, inverse, gain_2)
        d_low = d_second.astype(LOW)
        dfw[s] = d_low
        add("outer", column_sum(d_low))
        active, slant = gelu_parts(zw[s])
        gw[s] = active.astype(LOW)
        d_inner = (dot_t(d_low, wo[...]) * slant).astype(LOW)
        dzw[s] = d_inner
        add("inner", column_sum(d_inner))
        unit, inverse = norm_parts(h1w[s])
        ubw[s] = (unit * gain_1 + vec[SHIFT_1 : SHIFT_1 + 1, :]).astype(LOW)
        d_upper = dot_t(d_inner, wi[...]) + d_second
        add("gain_1", column_sum(d_upper * unit))
        add("shift_1", column_sum(d_upper))
        d_first = norm_back(d_upper, unit, inverse, gain_1)
        saved[s] = d_first
        d_low = d_first.astype(LOW)
        daw[s] = d_low
        add("mixer", column_sum(d_low))
        own = pl.ds(pl.multiple_of(z * GROUP, HEAD), GROUP)
        dow[...] = dot_t(d_low, wm[own, :]).astype(LOW)

    tokens_back(2)
    finish(2)
    tokens_back(1)
    layer_back(1, memory_back(2))
    writes_back(1)
    finish(1)
    tokens_back(0)
    layer_back(0, memory_back(1))
    writes_back(0)
    finish(0)
    memory_back(0)
    quarter = 0.25
    row = lax.broadcasted_iota(jnp.int32, (24, MODEL), 0)
    zero = jnp.zeros((1, MODEL), F32)
    small[0:8, :] = quarter * jnp.concatenate(
        [zero, zero]
        + [sums[n] for n in ("mixer", "gain_1", "shift_1", "outer", "gain_2", "shift_2")],
        axis=0,
    )
    small[8:16, :] = quarter * jnp.concatenate(
        [sums["inner"][:, i * MODEL : (i + 1) * MODEL] for i in range(4)] + [zero] * 4, axis=0
    )
    small[16:40, :] = quarter * sums["init"][0:24]
    small[40:64, :] = quarter * (
        sums["offset"][0:24]
        + jnp.where(row >= SLOTS, jnp.broadcast_to(sums["norm"], (24, MODEL)), 0.0)
    )
    for copy in row_copies:
        copy.wait_recv()
    for copy in started:
        copy.wait_send()


def backward(resets, dout, kv, probs, h1w, zw, h2w, vec, weights):
    return pl.pallas_call(
        backward_kernel,
        out_shape=(
            shape((4, ROWS, TRIPLE)),
            shape((SEGS, 4, MEMORY, TRIPLE)),
            shape((2, PAD, MODEL)),
            shape((2, PAD, INNER)),
            shape((2, PAD, INNER)),
            shape((2, PAD, MODEL)),
            shape((2, PAD, MODEL)),
            shape((64, MODEL), F32),
        ),
        in_specs=[pl.BlockSpec(memory_space=pltpu.SMEM)] + [VMEM] * 7 + [ANY] * 6,
        out_specs=(VMEM,) * 8,
        scratch_shapes=weight_buffers()
        + [
            pltpu.VMEM((SEGS, TOKENS, GROUP), LOW),
            pltpu.VMEM((PAD, GROUP), LOW),
            pltpu.VMEM((TOKENS, KEYS), LOW),
            pltpu.VMEM((SEGS, KEYS, 2 * GROUP), F32),
            pltpu.VMEM((SEGS, TOKENS, TRIPLE), LOW),
            pltpu.VMEM((SEGS, MEMORY, TRIPLE), LOW),
            pltpu.VMEM((3, MEMORY, MODEL), LOW),
            DMA((6,)),
            DMA((SEGS, 3)),
            DMA((SEGS, 3)),
            DMA((SEGS, 3)),
            DMA((SEGS, 3)),
            DMA((SEGS, 3)),
            DMA((SEGS, 3)),
        ],
        compiler_params=pltpu.CompilerParams(
            collective_id=2, has_side_effects=True, vmem_limit_bytes=60 << 20
        ),
        name="backward_attention",
    )(resets, dout, kv, probs, h1w, zw, h2w, vec, *weights)


FULL = ROWS + MEMORY
MOST = ROWS + PAD


def weight_kernel(
    tok, xm, drow, dmem, orow, ow, dh1, sums, inner_sum, small, ubw, gw, dzw, dfw, daw,
    ub_h, act_h, dz_h, df_h, da_h, wq_h, wk_h, wv_h,
    packed, input_grad, ext,
    ub, act, dz, df, da, wq, wk, wv, rows, triple, mixed, w_sem,
):
    z = lax.axis_index("seq")
    top = pl.ds(0, ROWS)
    fetched = fetch(
        [
            (wq_h, wq), (wk_h, wk), (wv_h, wv), (da_h, da.at[top]), (ub_h, ub.at[top]),
            (dz_h, dz.at[top]), (df_h, df.at[top]), (act_h, act.at[top]),
        ],
        w_sem,
    )
    at = jnp.minimum(z, 2)
    keep = (z < SEGS).astype(F32).astype(LOW)
    low_at = jnp.minimum(z, 1)
    low_keep = (z < 2).astype(F32).astype(LOW)
    rows[0:ROWS, :] = tok[...].reshape(ROWS, MODEL)
    rows[ROWS:, :] = xm[at]
    for g in range(4):
        for t in range(3):
            cut = slice(g * GROUP, (g + 1) * GROUP)
            part = slice(t * GROUP, (t + 1) * GROUP)
            triple[t, 0:ROWS, cut] = drow[g, :, part]
            triple[t, ROWS:, cut] = dmem[at, g, :, part] * keep
        mixed[g, 0:ROWS, :] = orow[g]
        mixed[g, ROWS:, :] = ow[low_at, g]
    ub[ROWS:, :] = ubw[low_at]
    act[ROWS:, :] = gw[low_at]
    dz[ROWS:, :] = dzw[low_at] * low_keep
    df[ROWS:, :] = dfw[low_at] * low_keep
    da[ROWS:, :] = daw[low_at] * low_keep
    ext[...] = small[...]
    ext[0:8, :] += sums[...]
    ext[8:12, :] += jnp.concatenate(
        [inner_sum[:, i * MODEL : (i + 1) * MODEL] for i in range(4)], axis=0
    )
    ext[QUERY_B : QUERY_B + 1, :] += column_sum(triple[0])
    ext[VALUE_B : VALUE_B + 1, :] += column_sum(triple[2])
    for t in range(3):
        packed[t * MODEL : (t + 1) * MODEL, :] = t_dot(rows[...], triple[t]).astype(LOW)
    for copy in fetched[:4]:
        copy.wait()
    for g in range(4):
        start = 3 * MODEL + g * GROUP
        packed[start : start + GROUP, :] = t_dot(mixed[g], da[...]).astype(LOW)
    input_grad[...] = (
        dh1[...]
        + dot_t(triple[0, 0:ROWS, :], wq[...])
        + dot_t(triple[1, 0:ROWS, :], wk[...])
        + dot_t(triple[2, 0:ROWS, :], wv[...])
    ).reshape(1, SEGS, BLOCK, MODEL)
    for copy in fetched[4:]:
        copy.wait()

    def inner(j, carry):
        cut = pl.ds(pl.multiple_of(j * MODEL, MODEL), MODEL)
        there = pl.ds(pl.multiple_of((4 + j) * MODEL, MODEL), MODEL)
        packed[there, :] = t_dot(ub[...], dz[:, cut]).astype(LOW)
        there = pl.ds(pl.multiple_of((8 + j) * MODEL, MODEL), MODEL)
        packed[there, :] = t_dot(act[:, cut], df[...]).astype(LOW)
        return carry

    lax.fori_loop(0, 4, inner, 0)


def weight_sums(
    tok, xm, drow, dmem, orow, ow, dh1, sums, inner_sum, small, ubw, gw, dzw, dfw, daw,
    ub, act, dz, df, da, weights,
):
    return pl.pallas_call(
        weight_kernel,
        out_shape=(
            shape((12 * MODEL, MODEL)),
            shape((1, SEGS, BLOCK, MODEL), F32),
            shape((64, MODEL), F32),
        ),
        in_specs=[VMEM] * 15 + [ANY] * 8,
        out_specs=(VMEM,) * 3,
        scratch_shapes=[
            pltpu.VMEM((MOST, MODEL), LOW),
            pltpu.VMEM((MOST, INNER), LOW),
            pltpu.VMEM((MOST, INNER), LOW),
            pltpu.VMEM((MOST, MODEL), LOW),
            pltpu.VMEM((MOST, MODEL), LOW),
            pltpu.VMEM((MODEL, MODEL), LOW),
            pltpu.VMEM((MODEL, MODEL), LOW),
            pltpu.VMEM((MODEL, MODEL), LOW),
            pltpu.VMEM((FULL, MODEL), LOW),
            pltpu.VMEM((3, FULL, MODEL), LOW),
            pltpu.VMEM((4, MOST, GROUP), LOW),
            DMA((8,)),
        ],
        compiler_params=pltpu.CompilerParams(vmem_limit_bytes=60 << 20),
        name="weight_sums",
    )(
        tok, xm, drow, dmem, orow, ow, dh1, sums, inner_sum, small, ubw, gw, dzw, dfw, daw,
        ub, act, dz, df, da, *weights[:3],
    )


def shards(
    tokens, documents, resets, cotangent, query_weight, query_bias, key_weight, value_weight,
    value_bias, mixer_weight, mixer_bias, first_gain, first_shift, inner_weight, inner_bias,
    outer_weight, outer_bias, second_gain, second_shift, memory_init, write_offset,
):
    weights = (query_weight, key_weight, value_weight, mixer_weight, inner_weight, outer_weight)
    vec = jnp.stack(
        [
            query_bias, value_bias, mixer_bias, first_gain, first_shift, outer_bias, second_gain,
            second_shift,
        ]
    ).astype(F32)
    inner_b = inner_bias.astype(F32)[None]
    tok = tokens[0]
    spare = ((0, PAD - SLOTS), (0, 0))
    init = jnp.pad(memory_init, spare)
    offset = jnp.pad(write_offset, spare)
    kv, probs, orow, ow, h1w, zw, h2w, xm = forward(
        resets, tok, documents[0], init, offset, vec, inner_b, weights
    )
    layer_output, ub, act, dz, df, da, dh1, dout, sums, inner_sum = middle(
        tok, orow, cotangent[0], vec, inner_b, weights
    )
    drow, dmem, ubw, gw, dzw, dfw, daw, small = backward(
        resets, dout, kv, probs, h1w, zw, h2w, vec, weights
    )
    packed, input_grad, ext = weight_sums(
        tok, xm, drow, dmem, orow, ow, dh1, sums, inner_sum, small, ubw, gw, dzw, dfw, daw,
        ub, act, dz, df, da, weights,
    )
    packed, ext = sum_all(packed, ext)
    query_w, key_w, value_w, mixer_w = (
        packed[i * MODEL : (i + 1) * MODEL].astype(F32) for i in range(4)
    )
    inner_w = jnp.concatenate(
        [packed[i * MODEL : (i + 1) * MODEL] for i in range(4, 8)], axis=1
    ).astype(F32)
    outer_w = packed[8 * MODEL :].astype(F32)
    chains = lax.axis_size("chain")
    memory_norm = jnp.sqrt(ext[60, 0] / (chains * SEGS * SLOTS * MODEL))
    return (
        layer_output,
        input_grad,
        query_w,
        ext[QUERY_B],
        key_w,
        value_w,
        ext[VALUE_B],
        mixer_w,
        ext[MIXER_B],
        ext[GAIN_1],
        ext[SHIFT_1],
        inner_w,
        ext[8:12].reshape(-1),
        outer_w,
        ext[OUTER_B],
        ext[GAIN_2],
        ext[SHIFT_2],
        ext[16:36],
        ext[40:60],
        memory_norm,
    )


def solution(mesh):
    tokens = P("chain", None, "seq", None)
    in_specs = (tokens, P("chain", None, "seq"), P("chain", None), tokens) + (P(),) * 17
    out_specs = (tokens, tokens) + (P(),) * 18
    return jax.shard_map(shards, mesh=mesh, in_specs=in_specs, out_specs=out_specs, check_vma=False)
```

```python
import functools

import jax
import jax.numpy as jnp
from jax import lax
from jax.experimental import pallas as pl
from jax.experimental.pallas import tpu as pltpu
from jax.sharding import PartitionSpec as P

MESH = pl.DeviceIdType.MESH
LOW = jnp.bfloat16
F32 = jnp.float32
SEGS = 3
BLOCK = 128
MODEL = 768
INNER = 3072
SLOTS = 20
PAD = 32
MEMORY = 2 * PAD
ROWS = SEGS * BLOCK
TOKENS = 512
KEYS = 640
QUERIES = TOKENS + PAD
HEAD = 64
MINE = 3
GROUP = MINE * HEAD
TRIPLE = 3 * GROUP
SCALE = HEAD ** (-0.5)
EPS = 1e-12
HIDDEN = -1e30


def dot(left, right):
    return jnp.dot(left, right, preferred_element_type=F32)


def dot_t(left, right):
    return lax.dot_general(left, right, (((1,), (1,)), ((), ())), preferred_element_type=F32)


def t_dot(left, right):
    return lax.dot_general(left, right, (((0,), (0,)), ((), ())), preferred_element_type=F32)


def norm_parts(hidden):
    centre = hidden - jnp.mean(hidden, axis=-1, keepdims=True)
    spread = jnp.mean(centre * centre, axis=-1, keepdims=True)
    inverse = lax.rsqrt(spread + EPS)
    return centre * inverse, inverse


def norm_back(upstream, unit, inverse, gain):
    scaled = upstream * gain
    first = jnp.mean(scaled, axis=-1, keepdims=True)
    second = jnp.mean(scaled * unit, axis=-1, keepdims=True)
    return (scaled - first - unit * second) * inverse


def gelu_parts(values):
    below = 0.5 * (1.0 + lax.erf(values * (0.5**0.5)))
    density = jnp.exp(-0.5 * values * values) * 0.3989422804014327
    return values * below, below + values * density


def column_sum(values):
    return jnp.sum(values.astype(F32), axis=0, keepdims=True)


def ring(off):
    return lax.rem(lax.axis_index("seq") + off + 4, 4)


def ring_barrier():
    barrier = pltpu.get_barrier_semaphore()
    for off in (1, 2, 3):
        pl.semaphore_signal(
            barrier, inc=1, device_id=(lax.axis_index("chain"), ring(off)), device_id_type=MESH
        )
    pl.semaphore_wait(barrier, 3)


def push(started, src, dst, s_sem, r_sem, off):
    copy = pltpu.make_async_remote_copy(
        src_ref=src,
        dst_ref=dst,
        send_sem=s_sem,
        recv_sem=r_sem,
        device_id=(lax.axis_index("chain"), ring(off)),
        device_id_type=MESH,
    )
    copy.start()
    started.append(copy)
    return copy


def fetch(pairs, sems):
    copies = [pltpu.make_async_copy(src, dst, sems.at[i]) for i, (src, dst) in enumerate(pairs)]
    for copy in copies:
        copy.start()
    return copies


QUERY_B, VALUE_B, MIXER_B, GAIN_1, SHIFT_1, OUTER_B, GAIN_2, SHIFT_2 = range(8)


def forward_kernel(
    resets, tok, docs, init_in, offset_in, query_b, value_b, mixer_b, gain_1, shift_1, outer_b,
    gain_2, shift_2, inner_in, wq_h, wk_h, wv_h, wm_h, wi_h, wo_h,
    kv, probs, orow, ow, h1w, zw, h2w, xm, vec, inner_b,
    wq, wk, wv, wm, wi, wo, wown, vown, sbuf, lab, bias, osend, owsend, init, offset,
    w_sem, q_s, q_r, o_s, o_r, m_s, m_r, l_s, l_r,
):
    z = lax.axis_index("seq")
    fetched = fetch(
        [(wq_h, wq), (wk_h, wk), (wv_h, wv), (wm_h, wm), (wi_h, wi), (wo_h, wo)], w_sem
    )
    started = []
    vectors = (query_b, value_b, mixer_b, gain_1, shift_1, outer_b, gain_2, shift_2)
    for i, ref in enumerate(vectors):
        vec[i : i + 1, :] = ref[...].astype(F32).reshape(1, MODEL)
    inner_b[...] = inner_in[...].astype(F32).reshape(1, INNER)
    for wide, ref in ((init, init_in), (offset, offset_in)):
        wide[...] = jnp.zeros((PAD, MODEL), LOW)
        wide[0:SLOTS, :] = ref[...]
    ring_barrier()
    lab[pl.ds(z, 1)] = docs[...][None]
    label_copies = [
        push(started, docs, lab.at[z], l_s.at[d - 1], l_r.at[d - 1], d) for d in (1, 2, 3)
    ]
    tokens = tok[...].reshape(ROWS, MODEL)
    fetched[0].wait()
    queries = ((dot(tokens, wq[...]) + vec[QUERY_B : QUERY_B + 1, :]) * SCALE).astype(LOW)
    for g in range(4):
        for s in range(SEGS):
            sbuf[g, s, :, 0:GROUP] = queries[
                s * BLOCK : (s + 1) * BLOCK, g * GROUP : (g + 1) * GROUP
            ]
    fetched[1].wait()
    keys = dot(tokens, wk[...]).astype(LOW)
    for g in range(4):
        for s in range(SEGS):
            sbuf[g, s, :, GROUP : 2 * GROUP] = keys[
                s * BLOCK : (s + 1) * BLOCK, g * GROUP : (g + 1) * GROUP
            ]
    fetched[2].wait()
    values = (dot(tokens, wv[...]) + vec[VALUE_B : VALUE_B + 1, :]).astype(LOW)
    for g in range(4):
        for s in range(SEGS):
            sbuf[g, s, :, 2 * GROUP :] = values[
                s * BLOCK : (s + 1) * BLOCK, g * GROUP : (g + 1) * GROUP
            ]
    here = pl.ds(pl.multiple_of(z * BLOCK, BLOCK), BLOCK)
    row_copies = []
    for s in range(SEGS):
        row_copies.append(
            [
                push(
                    started, sbuf.at[ring(d), s], kv.at[s, here],
                    q_s.at[s, d - 1], q_r.at[s, d - 1], d,
                )
                for d in (1, 2, 3)
            ]
        )
    for s in range(SEGS):
        kv[s, here, :] = sbuf[z, s]
        kv[s, TOKENS + MEMORY :, :] = jnp.zeros((KEYS - TOKENS - MEMORY, TRIPLE), LOW)
    for g in range(4):

        @pl.when(z == g)
        def _():
            cut = slice(g * GROUP, (g + 1) * GROUP)
            wown[:, 0:GROUP] = wq[:, cut]
            wown[:, GROUP : 2 * GROUP] = wk[:, cut]
            wown[:, 2 * GROUP :] = wv[:, cut]
            vown[0:1, 0:GROUP] = vec[QUERY_B : QUERY_B + 1, cut]
            vown[0:1, GROUP : 2 * GROUP] = jnp.zeros((1, GROUP), F32)
            vown[0:1, 2 * GROUP :] = vec[VALUE_B : VALUE_B + 1, cut]

    lane = lax.broadcasted_iota(jnp.int32, (1, TRIPLE), 1)
    factor = jnp.where(lane < GROUP, SCALE, 1.0)
    slot = lax.broadcasted_iota(jnp.int32, (PAD, MODEL), 0)
    key_lane = lax.broadcasted_iota(jnp.int32, (PAD, KEYS), 1)
    filled = (key_lane < TOKENS + SLOTS) | (
        (key_lane >= TOKENS + PAD) & (key_lane < TOKENS + PAD + SLOTS)
    )
    write_bias = jnp.where(filled, 0.0, HIDDEN)

    def attend(query_rows, mask, s, row_at, rows):
        parts = []
        for h in range(MINE):
            key_head = kv[s, :, GROUP + h * HEAD : GROUP + (h + 1) * HEAD]
            value_head = kv[s, :, 2 * GROUP + h * HEAD : 2 * GROUP + (h + 1) * HEAD]
            scores = dot_t(query_rows[:, h * HEAD : (h + 1) * HEAD], key_head) + mask
            weights = jnp.exp(scores - jnp.max(scores, axis=-1, keepdims=True))
            total = jnp.sum(weights, axis=-1, keepdims=True)
            prob = (weights * (1.0 / total)).astype(LOW)
            probs[s, h, pl.ds(row_at, rows), :] = prob
            parts.append(dot(prob, value_head))
        return jnp.concatenate(parts, axis=1).astype(LOW)

    memory = init[...]
    for copy in label_copies:
        copy.wait_recv()
    for s in range(SEGS):
        for i in range(4):
            column = jnp.transpose(jnp.broadcast_to(lab[i, s : s + 1, :].astype(F32), (BLOCK, BLOCK)))
            for j in range(4):
                row = jnp.broadcast_to(lab[j, s : s + 1, :].astype(F32), (BLOCK, BLOCK))
                bias[s, i * BLOCK : (i + 1) * BLOCK, j * BLOCK : (j + 1) * BLOCK] = jnp.where(
                    column == row, 0.0, HIDDEN
                )
            bias[s, i * BLOCK : (i + 1) * BLOCK, TOKENS:] = jnp.broadcast_to(
                write_bias[0:1, TOKENS:], (BLOCK, BLOCK)
            )
    out_copies = []
    for s in range(SEGS):
        written_in = (memory.astype(F32) + offset[...].astype(F32)).astype(LOW)
        xm[s, 0:PAD, :] = written_in
        xm[s, PAD:, :] = memory
        kv[s, TOKENS : TOKENS + MEMORY, :] = (
            (dot(xm[s], wown[...]) + vown[0:1, :]) * factor
        ).astype(LOW)
        for copy in row_copies[s]:
            copy.wait_recv()
        if s < SEGS - 1:
            mixed = attend(kv[s, TOKENS : TOKENS + PAD, :], write_bias, s, TOKENS, PAD)
            owsend[s] = mixed
            ow[s, pl.ds(z, 1)] = mixed[None]
            write_copies = [
                push(started, owsend.at[s], ow.at[s, z], m_s.at[s, d - 1], m_r.at[s, d - 1], d)
                for d in (1, 2, 3)
            ]

        def block(i, carry):
            row_at = pl.multiple_of(i * BLOCK, BLOCK)
            rows = pl.ds(row_at, BLOCK)
            osend[s, i] = attend(kv[s, rows, :], bias[s, rows, :], s, row_at, BLOCK)
            return carry

        lax.fori_loop(0, 4, block, 0)
        part = slice(s * BLOCK, (s + 1) * BLOCK)
        out_copies += [
            push(
                started, osend.at[s, ring(d)], orow.at[z, part],
                o_s.at[s, d - 1], o_r.at[s, d - 1], d,
            )
            for d in (1, 2, 3)
        ]
        orow[z, part, :] = osend[s, z]
        if s < SEGS - 1:
            if s == 0:
                for copy in fetched[3:]:
                    copy.wait()
            for copy in write_copies:
                copy.wait_recv()
            hidden = xm[s, 0:PAD, :].astype(F32) + vec[MIXER_B : MIXER_B + 1, :]
            for g in range(4):
                hidden = hidden + dot(ow[s, g], wm[g * GROUP : (g + 1) * GROUP, :])
            h1w[s] = hidden
            unit, _ = norm_parts(hidden)
            upper = unit * vec[GAIN_1 : GAIN_1 + 1, :] + vec[SHIFT_1 : SHIFT_1 + 1, :]
            inner = dot(upper.astype(LOW), wi[...]) + inner_b[...]
            zw[s] = inner
            active, _ = gelu_parts(inner)
            hidden = upper + dot(active.astype(LOW), wo[...]) + vec[OUTER_B : OUTER_B + 1, :]
            h2w[s] = hidden
            unit, _ = norm_parts(hidden)
            result = unit * vec[GAIN_2 : GAIN_2 + 1, :] + vec[SHIFT_2 : SHIFT_2 + 1, :]
            flag = jnp.full((PAD, MODEL), resets[0, s], jnp.int32)
            result = jnp.where(flag > 0, init[...].astype(F32), result)
            memory = jnp.where(slot < SLOTS, result, 0.0).astype(LOW)
    for copy in out_copies:
        copy.wait_recv()
    for copy in started:
        copy.wait_send()


def shape(dims, kind=LOW):
    return jax.ShapeDtypeStruct(dims, kind)


VMEM = pl.BlockSpec(memory_space=pltpu.VMEM)
ANY = pl.BlockSpec(memory_space=pl.ANY)
DMA = pltpu.SemaphoreType.DMA


def weight_buffers():
    return [pltpu.VMEM((MODEL, MODEL), LOW) for _ in range(4)] + [
        pltpu.VMEM((MODEL, INNER), LOW),
        pltpu.VMEM((INNER, MODEL), LOW),
    ]


def forward(resets, tok, docs, init, offset, vectors, inner_b, weights):
    return pl.pallas_call(
        forward_kernel,
        out_shape=(
            shape((SEGS, KEYS, TRIPLE)),
            shape((SEGS, MINE, QUERIES, KEYS)),
            shape((4, ROWS, GROUP)),
            shape((2, 4, PAD, GROUP)),
            shape((2, PAD, MODEL), F32),
            shape((2, PAD, INNER), F32),
            shape((2, PAD, MODEL), F32),
            shape((SEGS, MEMORY, MODEL)),
            shape((8, MODEL), F32),
            shape((1, INNER), F32),
        ),
        in_specs=[pl.BlockSpec(memory_space=pltpu.SMEM)] + [VMEM] * 13 + [ANY] * 6,
        out_specs=(VMEM,) * 10,
        scratch_shapes=weight_buffers()
        + [
            pltpu.VMEM((MODEL, TRIPLE), LOW),
            pltpu.VMEM((8, TRIPLE), F32),
            pltpu.VMEM((4, SEGS, BLOCK, TRIPLE), LOW),
            pltpu.VMEM((4, SEGS, BLOCK), jnp.int32),
            pltpu.VMEM((SEGS, TOKENS, KEYS), F32),
            pltpu.VMEM((SEGS, 4, BLOCK, GROUP), LOW),
            pltpu.VMEM((2, PAD, GROUP), LOW),
            pltpu.VMEM((PAD, MODEL), LOW),
            pltpu.VMEM((PAD, MODEL), LOW),
            DMA((6,)),
            DMA((SEGS, 3)),
            DMA((SEGS, 3)),
            DMA((SEGS, 3)),
            DMA((SEGS, 3)),
            DMA((2, 3)),
            DMA((2, 3)),
            DMA((3,)),
            DMA((3,)),
        ],
        compiler_params=pltpu.CompilerParams(
            collective_id=1, has_side_effects=True, vmem_limit_bytes=60 << 20
        ),
        name="forward_attention",
    )(resets, tok, docs, init, offset, *vectors, inner_b, *weights)


WIDE = 768
HALF = 4608
PART = 1536
CHUNK = 384
SUB = 96
ORDERS = (("x", "y", "z"), ("y", "z", "x"), ("z", "x", "y"))


def places():
    chain = lax.axis_index("chain")
    return {
        "x": chain // 8,
        "y": lax.rem(chain // 2, 4),
        "z": lax.axis_index("seq"),
        "core": lax.rem(chain, 2),
    }


def peer(at, axis, off):
    at = dict(at)
    size = 2 if axis == "core" else 4
    at[axis] = lax.rem(at[axis] + off + size, size)
    return ((at["x"] * 4 + at["y"]) * 2 + at["core"], at["z"])


def greet(at, peers):
    barrier = pltpu.get_barrier_semaphore()
    for axis, off in peers:
        pl.semaphore_signal(barrier, inc=1, device_id=peer(at, axis, off), device_id_type=MESH)
    pl.semaphore_wait(barrier, len(peers))


ALL_PEERS = [("core", 1)] + [(axis, off) for axis in "xyz" for off in (1, 2, 3)]


def add_rows(out, out_start, terms, rows, step=48):
    def body(i, carry):
        base = i * step
        total = None
        for ref, start in terms:
            term = ref[pl.ds(pl.multiple_of(start + base, 16), step), :].astype(jnp.float32)
            total = term if total is None else total + term
        out[pl.ds(pl.multiple_of(out_start + base, 16), step), :] = total.astype(out.dtype)
        return carry

    lax.fori_loop(0, rows // step, body, 0)


def sum_kernel(
    g, ext, w, e, crecv, r1, r2, r3, r4, ecore, ex, ey, ez,
    c_s, c_r, a1_s, a1_r, a2_s, a2_r, b_s, b_r, d_s, d_r,
    gd_s, gd_r, gb_s, gb_r, g1_s, g1_r, g2_s, g2_r, gc_s, gc_r,
    e_s, e_r,
):
    at = places()
    greet(at, ALL_PEERS)
    started = []

    def send(src, dst, s_sem, r_sem, axis, off):
        copy = pltpu.make_async_remote_copy(
            src_ref=src, dst_ref=dst, send_sem=s_sem, recv_sem=r_sem,
            device_id=peer(at, axis, off), device_id_type=MESH,
        )
        copy.start()
        started.append(copy)
        return copy

    core = at["core"]
    mine = core * HALF
    theirs = (1 - core) * HALF

    def turn(value, off):
        return lax.rem(value + off + 4, 4)

    def ds(start, size):
        return pl.ds(pl.multiple_of(start, 16), size)

    place1 = [at[order[0]] for order in ORDERS]
    place2 = [at[order[1]] for order in ORDERS]
    place3 = [at[order[2]] for order in ORDERS]

    def rel(p, off):
        return p * PART + turn(place1[p], off) * CHUNK

    core_copies = {}
    e_core = send(
        ext.at[pl.ds(pl.multiple_of((1 - core) * 32, 8), 32)], ecore, e_s.at[0], e_r.at[0], "core", 1
    )
    for j, off in enumerate((2, 1, 3, 0)):
        for p in range(3):
            start = rel(p, off)
            core_copies[p, off] = send(
                g.at[ds(theirs + start, CHUNK)], crecv.at[ds(start, CHUNK)],
                c_s.at[p, j], c_r.at[p, j], "core", 1,
            )

    def own(p, off):
        core_copies[p, off].wait_recv()
        start = rel(p, off)
        add_rows(crecv, start, [(g, mine + start), (crecv, start)], CHUNK)

    e_core.wait_recv()
    ecore[...] = ext[pl.ds(pl.multiple_of(core * 32, 8), 32), :] + ecore[...]
    e_x = [
        send(
            ecore.at[pl.ds(pl.multiple_of(turn(at["x"], d) * 8, 8), 8)],
            ex.at[d - 1], e_s.at[d], e_r.at[d], "x", d,
        )
        for d in (1, 2, 3)
    ]
    first = {}
    for p in range(3):
        own(p, 2)
        start = rel(p, 2)
        axis = ORDERS[p][0]
        first[p] = (
            send(crecv.at[ds(start, CHUNK // 2)], r1.at[p, 0], a1_s.at[p, 0], a1_r.at[p, 0], axis, 1),
            send(
                crecv.at[ds(start + CHUNK // 2, CHUNK // 2)], r1.at[p, 1],
                a1_s.at[p, 1], a1_r.at[p, 1], axis, 3,
            ),
        )
    for off in (1, 3, 0):
        for p in range(3):
            own(p, off)
    second = {}
    for p in range(3):
        axis = ORDERS[p][0]
        start = rel(p, 1)
        first[p][0].wait_recv()
        add_rows(crecv, start, [(crecv, start), (r1.at[p, 0], 0)], CHUNK // 2)
        right = send(crecv.at[ds(start, CHUNK)], r2.at[p, 0], a2_s.at[p, 0], a2_r.at[p, 0], axis, 1)
        start = rel(p, 3)
        first[p][1].wait_recv()
        add_rows(
            crecv, start + CHUNK // 2, [(crecv, start + CHUNK // 2), (r1.at[p, 1], 0)], CHUNK // 2
        )
        left = send(crecv.at[ds(start, CHUNK)], r2.at[p, 1], a2_s.at[p, 1], a2_r.at[p, 1], axis, 3)
        second[p] = (right, left)
    e_own = pl.ds(pl.multiple_of(core * 32 + at["x"] * 8, 8), 8)
    for copy in e_x:
        copy.wait_recv()
    ey[pl.ds(at["y"], 1)] = (ecore[pl.ds(pl.multiple_of(at["x"] * 8, 8), 8), :] + ex[0] + ex[1] + ex[2])[None]
    e_y = [
        send(ey.at[at["y"]], ey.at[at["y"]], e_s.at[3 + d], e_r.at[3 + d], "y", d)
        for d in (1, 2, 3)
    ]
    third = {}
    for p in range(3):
        start = rel(p, 0)
        for copy in second[p]:
            copy.wait_recv()
        add_rows(crecv, start, [(crecv, start), (r2.at[p, 0], 0), (r2.at[p, 1], 0)], CHUNK)
        third[p] = [
            send(
                crecv.at[ds(start + turn(place2[p], d) * SUB, SUB)], r3.at[p, d - 1],
                b_s.at[p, d - 1], b_r.at[p, d - 1], ORDERS[p][1], d,
            )
            for d in (1, 2, 3)
        ]
    for copy in e_y:
        copy.wait_recv()
    ez[pl.ds(at["z"], 1)] = (ey[0] + ey[1] + ey[2] + ey[3])[None]
    e_z = [
        send(ez.at[at["z"]], ez.at[at["z"]], e_s.at[6 + d], e_r.at[6 + d], "z", d)
        for d in (1, 2, 3)
    ]
    fourth = {}

    def quarter(ref, start, c):
        return ref.at[ds(start + (c // 2) * (SUB // 2), SUB // 2), pl.ds(pl.multiple_of(lax.rem(c, 2) * (WIDE // 2), 128), WIDE // 2)]

    for p in range(3):
        start = rel(p, 0) + place2[p] * SUB
        for copy in third[p]:
            copy.wait_recv()
        add_rows(crecv, start, [(crecv, start)] + [(r3.at[p, d], 0) for d in range(3)], SUB)
        fourth[p] = [
            send(
                quarter(crecv, start, turn(place3[p], d)), r4.at[p, d - 1],
                d_s.at[p, d - 1], d_r.at[p, d - 1], ORDERS[p][2], d,
            )
            for d in (1, 2, 3)
        ]
    for copy in e_z:
        copy.wait_recv()
    e[e_own, :] = ez[0] + ez[1] + ez[2] + ez[3]
    e_back = [
        send(e.at[e_own], e.at[e_own], e_s.at[9 + d], e_r.at[9 + d], "x", d) for d in (1, 2, 3)
    ]
    fifth = {}
    for p in range(3):
        start = rel(p, 0) + place2[p] * SUB
        for copy in fourth[p]:
            copy.wait_recv()
        total = quarter(crecv, start, place3[p])[...].astype(jnp.float32)
        for d in range(3):
            total = total + r4[p, d].astype(jnp.float32)
        piece = quarter(w, mine + start, place3[p])
        piece[...] = total.astype(w.dtype)
        fifth[p] = [
            send(piece, piece, gd_s.at[p, d - 1], gd_r.at[p, d - 1], ORDERS[p][2], d)
            for d in (1, 2, 3)
        ]
    sixth = {}
    for p in range(3):
        start = mine + rel(p, 0) + place2[p] * SUB
        for copy in fifth[p]:
            copy.wait_recv()
        piece = w.at[ds(start, SUB)]
        sixth[p] = [
            send(piece, piece, gb_s.at[p, d - 1], gb_r.at[p, d - 1], ORDERS[p][1], d)
            for d in (1, 2, 3)
        ]
    for copy in e_back:
        copy.wait_recv()
    e_half = e.at[pl.ds(pl.multiple_of(core * 32, 8), 32)]
    e_last = send(e_half, e_half, e_s.at[13], e_r.at[13], "core", 1)
    seventh = {}
    last = []

    def across(p, j, start, rows):
        piece = w.at[ds(start, rows)]
        last.append(send(piece, piece, gc_s.at[p, j], gc_r.at[p, j], "core", 1))

    for p in range(3):
        start = mine + rel(p, 0)
        for copy in sixth[p]:
            copy.wait_recv()
        piece = w.at[ds(start, CHUNK)]
        axis = ORDERS[p][0]
        seventh[p] = (
            send(piece, piece, g1_s.at[p, 0], g1_r.at[p, 0], axis, 1),
            send(piece, piece, g1_s.at[p, 1], g1_r.at[p, 1], axis, 3),
        )
        across(p, 0, start, CHUNK)
    eighth = {}
    for p in range(3):
        axis = ORDERS[p][0]
        seventh[p][0].wait_recv()
        start = mine + rel(p, 3)
        piece = w.at[ds(start, CHUNK // 2)]
        right = send(piece, piece, g2_s.at[p, 0], g2_r.at[p, 0], axis, 1)
        across(p, 1, start, CHUNK)
        seventh[p][1].wait_recv()
        start = mine + rel(p, 1)
        piece = w.at[ds(start + CHUNK // 2, CHUNK // 2)]
        left = send(piece, piece, g2_s.at[p, 1], g2_r.at[p, 1], axis, 3)
        across(p, 2, start, CHUNK)
        eighth[p] = (right, left)
    for p in range(3):
        start = mine + rel(p, 2)
        for i in range(2):
            eighth[p][i].wait_recv()
            across(p, 3 + i, start + i * (CHUNK // 2), CHUNK // 2)
    e_last.wait_recv()
    for copy in last:
        copy.wait_recv()
    for copy in started:
        copy.wait_send()


def sum_all(g, ext):
    dma = pltpu.SemaphoreType.DMA
    pairs = [(3, 4), (3, 2), (3, 2), (3, 3), (3, 3), (3, 3), (3, 3), (3, 2), (3, 2), (3, 5), (14,)]
    sems = [dma(shape) for shape in pairs for _ in range(2)]
    vmem = pl.BlockSpec(memory_space=pltpu.VMEM)
    return pl.pallas_call(
        sum_kernel,
        out_shape=(
            jax.ShapeDtypeStruct((2 * HALF, WIDE), jnp.bfloat16),
            jax.ShapeDtypeStruct((64, WIDE), jnp.float32),
        ),
        in_specs=[vmem, vmem],
        out_specs=(vmem, vmem),
        scratch_shapes=[
            pltpu.VMEM((HALF, WIDE), jnp.bfloat16),
            pltpu.VMEM((3, 2, CHUNK // 2, WIDE), jnp.bfloat16),
            pltpu.VMEM((3, 2, CHUNK, WIDE), jnp.bfloat16),
            pltpu.VMEM((3, 3, SUB, WIDE), jnp.bfloat16),
            pltpu.VMEM((3, 3, SUB // 2, WIDE // 2), jnp.bfloat16),
            pltpu.VMEM((32, WIDE), jnp.float32),
            pltpu.VMEM((3, 8, WIDE), jnp.float32),
            pltpu.VMEM((4, 8, WIDE), jnp.float32),
            pltpu.VMEM((4, 8, WIDE), jnp.float32),
        ] + sems,
        compiler_params=pltpu.CompilerParams(
            collective_id=7, has_side_effects=True, vmem_limit_bytes=60 << 20
        ),
        name="sum_all",
    )(g, ext)


def middle_kernel(
    tok, orow, cot, vec, inner_b, wm_h, wi_h, wo_h,
    out, ub, act, dz, df, da, dh1, dout, sums, inner_sum,
    wm, wi, wo, slope, total, unit_1, inverse_1, w_sem,
):
    fetched = fetch([(wm_h, wm), (wi_h, wi), (wo_h, wo)], w_sem)
    gain_1 = vec[GAIN_1 : GAIN_1 + 1, :]
    gain_2 = vec[GAIN_2 : GAIN_2 + 1, :]
    hidden = tok[...].reshape(ROWS, MODEL).astype(F32) + vec[MIXER_B : MIXER_B + 1, :]
    fetched[0].wait()
    for g in range(4):
        hidden = hidden + dot(orow[g], wm[g * GROUP : (g + 1) * GROUP, :])
    unit, inverse = norm_parts(hidden)
    unit_1[...] = unit
    inverse_1[...] = inverse
    upper = unit * gain_1 + vec[SHIFT_1 : SHIFT_1 + 1, :]
    ub[...] = upper.astype(LOW)
    total[...] = upper + vec[OUTER_B : OUTER_B + 1, :]
    for copy in fetched[1:]:
        copy.wait()

    def ahead(j, carry):
        cut = pl.ds(pl.multiple_of(j * MODEL, MODEL), MODEL)
        inner = dot(ub[...], wi[:, cut]) + inner_b[:, cut]
        active, slant = gelu_parts(inner)
        active = active.astype(LOW)
        act[:, cut] = active
        slope[:, cut] = slant
        total[...] += dot(active, wo[cut, :])
        return carry

    lax.fori_loop(0, INNER // MODEL, ahead, 0)
    unit, inverse = norm_parts(total[...])
    result = unit * gain_2 + vec[SHIFT_2 : SHIFT_2 + 1, :]
    out[...] = result.astype(LOW).reshape(1, SEGS, BLOCK, MODEL)
    upstream = cot[...].reshape(ROWS, MODEL).astype(F32)
    sums[GAIN_2 : GAIN_2 + 1, :] = column_sum(upstream * unit)
    sums[SHIFT_2 : SHIFT_2 + 1, :] = column_sum(upstream)
    d_hidden = norm_back(upstream, unit, inverse, gain_2)
    total[...] = d_hidden
    d_low = d_hidden.astype(LOW)
    df[...] = d_low
    sums[OUTER_B : OUTER_B + 1, :] = column_sum(d_low)

    def back(j, carry):
        cut = pl.ds(pl.multiple_of(j * MODEL, MODEL), MODEL)
        d_inner = (dot_t(df[...], wo[cut, :]) * slope[:, cut]).astype(LOW)
        dz[:, cut] = d_inner
        inner_sum[:, cut] = column_sum(d_inner)
        total[...] += dot_t(d_inner, wi[:, cut])
        return carry

    lax.fori_loop(0, INNER // MODEL, back, 0)
    upstream = total[...]
    unit = unit_1[...]
    sums[GAIN_1 : GAIN_1 + 1, :] = column_sum(upstream * unit)
    sums[SHIFT_1 : SHIFT_1 + 1, :] = column_sum(upstream)
    d_hidden = norm_back(upstream, unit, inverse_1[...], gain_1)
    dh1[...] = d_hidden
    d_low = d_hidden.astype(LOW)
    da[...] = d_low
    sums[MIXER_B : MIXER_B + 1, :] = column_sum(d_low)
    sums[QUERY_B : QUERY_B + 2, :] = jnp.zeros((2, MODEL), F32)
    for g in range(4):
        dout[g] = dot_t(d_low, wm[g * GROUP : (g + 1) * GROUP, :]).astype(LOW)


def middle(tok, orow, cot, vec, inner_b, weights):
    return pl.pallas_call(
        middle_kernel,
        out_shape=(
            shape((1, SEGS, BLOCK, MODEL)),
            shape((ROWS, MODEL)),
            shape((ROWS, INNER)),
            shape((ROWS, INNER)),
            shape((ROWS, MODEL)),
            shape((ROWS, MODEL)),
            shape((ROWS, MODEL), F32),
            shape((4, ROWS, GROUP)),
            shape((8, MODEL), F32),
            shape((1, INNER), F32),
        ),
        in_specs=[VMEM] * 5 + [ANY] * 3,
        out_specs=(VMEM,) * 10,
        scratch_shapes=[
            pltpu.VMEM((MODEL, MODEL), LOW),
            pltpu.VMEM((MODEL, INNER), LOW),
            pltpu.VMEM((INNER, MODEL), LOW),
            pltpu.VMEM((ROWS, INNER), F32),
            pltpu.VMEM((ROWS, MODEL), F32),
            pltpu.VMEM((ROWS, MODEL), F32),
            pltpu.VMEM((ROWS, 1), F32),
            DMA((3,)),
        ],
        compiler_params=pltpu.CompilerParams(vmem_limit_bytes=60 << 20),
        name="token_layer",
    )(tok, orow, cot, vec, inner_b, *weights[3:])


def backward_kernel(
    resets, dout, kv, probs, h1w, zw, h2w, vec,
    wq_h, wk_h, wv_h, wm_h, wi_h, wo_h,
    drow, dmem, ubw, gw, dzw, dfw, daw, small,
    wq, wk, wv, wm, wi, wo, doh, dow, ds, acc, dsend, msend, wide,
    w_sem, d_s, d_r, x_s, x_r, m_s, m_r,
):
    z = lax.axis_index("seq")
    fetched = fetch(
        [(wq_h, wq), (wk_h, wk), (wv_h, wv), (wm_h, wm), (wi_h, wi), (wo_h, wo)], w_sem
    )
    started = []
    ring_barrier()
    here = pl.ds(pl.multiple_of(z * BLOCK, BLOCK), BLOCK)
    in_copies = {}
    for s in reversed(range(SEGS)):
        part = slice(s * BLOCK, (s + 1) * BLOCK)
        in_copies[s] = [
            push(
                started, dout.at[ring(d), part], doh.at[s, here],
                d_s.at[s, d - 1], d_r.at[s, d - 1], d,
            )
            for d in (1, 2, 3)
        ]
        doh[s, here, :] = dout[z, part, :]
    gain_1 = vec[GAIN_1 : GAIN_1 + 1, :]
    gain_2 = vec[GAIN_2 : GAIN_2 + 1, :]

    def head_back(s, h, d_rows, rows):
        cut = slice(h * HEAD, (h + 1) * HEAD)
        key_head = kv[s, :, GROUP + h * HEAD : GROUP + (h + 1) * HEAD]
        value_head = kv[s, :, 2 * GROUP + h * HEAD : 2 * GROUP + (h + 1) * HEAD]
        d_head = d_rows[:, cut]
        prob = probs[s, h, rows, :]
        wide_prob = prob.astype(F32)
        product = wide_prob * dot_t(d_head, value_head)
        delta = jnp.sum(product, axis=-1, keepdims=True)
        d_scores = (product - wide_prob * delta).astype(LOW)
        d_query = (dot(d_scores, key_head) * SCALE).astype(LOW)
        d_key = t_dot(d_scores, kv[s, rows, cut])
        d_value = t_dot(prob, d_head)
        return d_query, d_key, d_value

    def tokens_back(s):
        for copy in in_copies[s]:
            copy.wait_recv()
        rows = slice(0, TOKENS)
        for h in range(MINE):
            cut = slice(h * HEAD, (h + 1) * HEAD)
            d_query, d_key, d_value = head_back(s, h, doh[s], rows)
            dsend[s, :, cut] = d_query
            acc[s, :, cut] = d_key
            acc[s, :, GROUP + h * HEAD : GROUP + (h + 1) * HEAD] = d_value

    def writes_back(s):
        rows = slice(TOKENS, TOKENS + PAD)
        for h in range(MINE):
            cut = slice(h * HEAD, (h + 1) * HEAD)
            d_query, d_key, d_value = head_back(s, h, dow[...], rows)
            msend[s, 0:PAD, cut] = d_query
            acc[s, :, cut] += d_key
            acc[s, :, GROUP + h * HEAD : GROUP + (h + 1) * HEAD] += d_value

    mem_copies = {}
    row_copies = []

    def finish(s):
        if s == SEGS - 1:
            msend[s, :, 0:GROUP] = jnp.zeros((MEMORY, GROUP), LOW)
        else:
            msend[s, PAD:, 0:GROUP] = jnp.zeros((PAD, GROUP), LOW)
        msend[s, :, GROUP:] = acc[s, TOKENS : TOKENS + MEMORY, :].astype(LOW)
        mem_copies[s] = [
            push(started, msend.at[s], dmem.at[s, z], m_s.at[s, d - 1], m_r.at[s, d - 1], d)
            for d in (1, 2, 3)
        ]
        dmem[s, z] = msend[s]
        dsend[s, :, GROUP:] = acc[s, 0:TOKENS, :].astype(LOW)
        part = slice(s * BLOCK, (s + 1) * BLOCK)
        for d in (1, 2, 3):
            there = pl.ds(pl.multiple_of(ring(d) * BLOCK, BLOCK), BLOCK)
            row_copies.append(
                push(
                    started, dsend.at[s, there], drow.at[z, part],
                    x_s.at[s, d - 1], x_r.at[s, d - 1], d,
                )
            )
        drow[z, part, :] = dsend[s, here, :]

    sums = {}

    def add(name, value):
        sums[name] = value if name not in sums else sums[name] + value

    saved = {}

    def memory_back(s):
        for copy in mem_copies[s]:
            copy.wait_recv()
        for g in range(4):
            for t in range(3):
                wide[t, :, g * GROUP : (g + 1) * GROUP] = dmem[
                    s, g, :, t * GROUP : (t + 1) * GROUP
                ]
        if s == SEGS - 1:
            for copy in fetched:
                copy.wait()
        d_rows = dot_t(wide[0], wq[...]) + dot_t(wide[1], wk[...]) + dot_t(wide[2], wv[...])
        write = d_rows[0:PAD]
        if s < SEGS - 1:
            write = write + saved[s]
        grad = write + d_rows[PAD:]
        add("offset", write)
        add("norm", jnp.sum(jnp.sum(grad * grad, axis=0, keepdims=True), axis=1, keepdims=True))
        if s == 0:
            add("init", grad)
            return None
        flag = jnp.full((PAD, MODEL), resets[0, s - 1], jnp.int32) > 0
        add("init", jnp.where(flag, grad, 0.0))
        return jnp.where(flag, 0.0, grad)

    def layer_back(s, upstream):
        unit, inverse = norm_parts(h2w[s])
        add("gain_2", column_sum(upstream * unit))
        add("shift_2", column_sum(upstream))
        d_second = norm_back(upstream, unit, inverse, gain_2)
        d_low = d_second.astype(LOW)
        dfw[s] = d_low
        add("outer", column_sum(d_low))
        active, slant = gelu_parts(zw[s])
        gw[s] = active.astype(LOW)
        d_inner = (dot_t(d_low, wo[...]) * slant).astype(LOW)
        dzw[s] = d_inner
        add("inner", column_sum(d_inner))
        unit, inverse = norm_parts(h1w[s])
        ubw[s] = (unit * gain_1 + vec[SHIFT_1 : SHIFT_1 + 1, :]).astype(LOW)
        d_upper = dot_t(d_inner, wi[...]) + d_second
        add("gain_1", column_sum(d_upper * unit))
        add("shift_1", column_sum(d_upper))
        d_first = norm_back(d_upper, unit, inverse, gain_1)
        saved[s] = d_first
        d_low = d_first.astype(LOW)
        daw[s] = d_low
        add("mixer", column_sum(d_low))
        own = pl.ds(pl.multiple_of(z * GROUP, HEAD), GROUP)
        dow[...] = dot_t(d_low, wm[own, :]).astype(LOW)

    tokens_back(2)
    finish(2)
    tokens_back(1)
    layer_back(1, memory_back(2))
    writes_back(1)
    finish(1)
    tokens_back(0)
    layer_back(0, memory_back(1))
    writes_back(0)
    finish(0)
    memory_back(0)
    quarter = 0.25
    row = lax.broadcasted_iota(jnp.int32, (24, MODEL), 0)
    zero = jnp.zeros((1, MODEL), F32)
    small[0:8, :] = quarter * jnp.concatenate(
        [zero, zero]
        + [sums[n] for n in ("mixer", "gain_1", "shift_1", "outer", "gain_2", "shift_2")],
        axis=0,
    )
    small[8:16, :] = quarter * jnp.concatenate(
        [sums["inner"][:, i * MODEL : (i + 1) * MODEL] for i in range(4)] + [zero] * 4, axis=0
    )
    small[16:40, :] = quarter * sums["init"][0:24]
    small[40:64, :] = quarter * (
        sums["offset"][0:24]
        + jnp.where(row >= SLOTS, jnp.broadcast_to(sums["norm"], (24, MODEL)), 0.0)
    )
    for copy in row_copies:
        copy.wait_recv()
    for copy in started:
        copy.wait_send()


def backward(resets, dout, kv, probs, h1w, zw, h2w, vec, weights):
    return pl.pallas_call(
        backward_kernel,
        out_shape=(
            shape((4, ROWS, TRIPLE)),
            shape((SEGS, 4, MEMORY, TRIPLE)),
            shape((2, PAD, MODEL)),
            shape((2, PAD, INNER)),
            shape((2, PAD, INNER)),
            shape((2, PAD, MODEL)),
            shape((2, PAD, MODEL)),
            shape((64, MODEL), F32),
        ),
        in_specs=[pl.BlockSpec(memory_space=pltpu.SMEM)] + [VMEM] * 7 + [ANY] * 6,
        out_specs=(VMEM,) * 8,
        scratch_shapes=weight_buffers()
        + [
            pltpu.VMEM((SEGS, TOKENS, GROUP), LOW),
            pltpu.VMEM((PAD, GROUP), LOW),
            pltpu.VMEM((TOKENS, KEYS), LOW),
            pltpu.VMEM((SEGS, KEYS, 2 * GROUP), F32),
            pltpu.VMEM((SEGS, TOKENS, TRIPLE), LOW),
            pltpu.VMEM((SEGS, MEMORY, TRIPLE), LOW),
            pltpu.VMEM((3, MEMORY, MODEL), LOW),
            DMA((6,)),
            DMA((SEGS, 3)),
            DMA((SEGS, 3)),
            DMA((SEGS, 3)),
            DMA((SEGS, 3)),
            DMA((SEGS, 3)),
            DMA((SEGS, 3)),
        ],
        compiler_params=pltpu.CompilerParams(
            collective_id=2, has_side_effects=True, vmem_limit_bytes=60 << 20
        ),
        name="backward_attention",
    )(resets, dout, kv, probs, h1w, zw, h2w, vec, *weights)


FULL = ROWS + MEMORY
MOST = ROWS + PAD


def weight_kernel(
    tok, xm, drow, dmem, orow, ow, dh1, sums, inner_sum, small, ubw, gw, dzw, dfw, daw,
    ub_h, act_h, dz_h, df_h, da_h, wq_h, wk_h, wv_h,
    packed, input_grad, ext,
    ub, act, dz, df, da, wq, wk, wv, rows, triple, mixed, w_sem,
):
    z = lax.axis_index("seq")
    top = pl.ds(0, ROWS)
    fetched = fetch(
        [
            (wq_h, wq), (wk_h, wk), (wv_h, wv), (da_h, da.at[top]), (ub_h, ub.at[top]),
            (dz_h, dz.at[top]), (df_h, df.at[top]), (act_h, act.at[top]),
        ],
        w_sem,
    )
    at = jnp.minimum(z, 2)
    keep = (z < SEGS).astype(F32).astype(LOW)
    low_at = jnp.minimum(z, 1)
    low_keep = (z < 2).astype(F32).astype(LOW)
    rows[0:ROWS, :] = tok[...].reshape(ROWS, MODEL)
    rows[ROWS:, :] = xm[at]
    for g in range(4):
        for t in range(3):
            cut = slice(g * GROUP, (g + 1) * GROUP)
            part = slice(t * GROUP, (t + 1) * GROUP)
            triple[t, 0:ROWS, cut] = drow[g, :, part]
            triple[t, ROWS:, cut] = dmem[at, g, :, part] * keep
        mixed[g, 0:ROWS, :] = orow[g]
        mixed[g, ROWS:, :] = ow[low_at, g]
    ub[ROWS:, :] = ubw[low_at]
    act[ROWS:, :] = gw[low_at]
    dz[ROWS:, :] = dzw[low_at] * low_keep
    df[ROWS:, :] = dfw[low_at] * low_keep
    da[ROWS:, :] = daw[low_at] * low_keep
    ext[...] = small[...]
    ext[0:8, :] += sums[...]
    ext[8:12, :] += jnp.concatenate(
        [inner_sum[:, i * MODEL : (i + 1) * MODEL] for i in range(4)], axis=0
    )
    ext[QUERY_B : QUERY_B + 1, :] += column_sum(triple[0])
    ext[VALUE_B : VALUE_B + 1, :] += column_sum(triple[2])
    for t in range(3):
        packed[t * MODEL : (t + 1) * MODEL, :] = t_dot(rows[...], triple[t]).astype(LOW)
    for copy in fetched[:4]:
        copy.wait()
    for g in range(4):
        start = 3 * MODEL + g * GROUP
        packed[start : start + GROUP, :] = t_dot(mixed[g], da[...]).astype(LOW)
    input_grad[...] = (
        dh1[...]
        + dot_t(triple[0, 0:ROWS, :], wq[...])
        + dot_t(triple[1, 0:ROWS, :], wk[...])
        + dot_t(triple[2, 0:ROWS, :], wv[...])
    ).reshape(1, SEGS, BLOCK, MODEL)
    for copy in fetched[4:]:
        copy.wait()

    def inner(j, carry):
        cut = pl.ds(pl.multiple_of(j * MODEL, MODEL), MODEL)
        there = pl.ds(pl.multiple_of((4 + j) * MODEL, MODEL), MODEL)
        packed[there, :] = t_dot(ub[...], dz[:, cut]).astype(LOW)
        there = pl.ds(pl.multiple_of((8 + j) * MODEL, MODEL), MODEL)
        packed[there, :] = t_dot(act[:, cut], df[...]).astype(LOW)
        return carry

    lax.fori_loop(0, 4, inner, 0)


def weight_sums(
    tok, xm, drow, dmem, orow, ow, dh1, sums, inner_sum, small, ubw, gw, dzw, dfw, daw,
    ub, act, dz, df, da, weights,
):
    return pl.pallas_call(
        weight_kernel,
        out_shape=(
            shape((12 * MODEL, MODEL)),
            shape((1, SEGS, BLOCK, MODEL), F32),
            shape((64, MODEL), F32),
        ),
        in_specs=[VMEM] * 15 + [ANY] * 8,
        out_specs=(VMEM,) * 3,
        scratch_shapes=[
            pltpu.VMEM((MOST, MODEL), LOW),
            pltpu.VMEM((MOST, INNER), LOW),
            pltpu.VMEM((MOST, INNER), LOW),
            pltpu.VMEM((MOST, MODEL), LOW),
            pltpu.VMEM((MOST, MODEL), LOW),
            pltpu.VMEM((MODEL, MODEL), LOW),
            pltpu.VMEM((MODEL, MODEL), LOW),
            pltpu.VMEM((MODEL, MODEL), LOW),
            pltpu.VMEM((FULL, MODEL), LOW),
            pltpu.VMEM((3, FULL, MODEL), LOW),
            pltpu.VMEM((4, MOST, GROUP), LOW),
            DMA((8,)),
        ],
        compiler_params=pltpu.CompilerParams(vmem_limit_bytes=60 << 20),
        name="weight_sums",
    )(
        tok, xm, drow, dmem, orow, ow, dh1, sums, inner_sum, small, ubw, gw, dzw, dfw, daw,
        ub, act, dz, df, da, *weights[:3],
    )


def widen_kernel(
    count, packed, ext,
    query_w, key_w, value_w, mixer_w, inner_w, outer_w, query_b, value_b, mixer_b, gain_1, shift_1,
    inner_b, outer_b, gain_2, shift_2, init, offset, norm,
    low, wide, in_sem, out_sem,
):
    def rows(i):
        return pl.ds(i * MODEL, MODEL)

    loads = [pltpu.make_async_copy(packed.at[rows(i)], low.at[i], in_sem.at[i]) for i in range(12)]
    for copy in loads:
        copy.start()
    targets = [query_w, key_w, value_w, mixer_w]
    targets += [inner_w.at[:, rows(i)] for i in range(4)]
    targets += [outer_w.at[rows(i)] for i in range(4)]
    stores = []
    for i in range(12):
        loads[i].wait()

        def body(j, carry):
            part = pl.ds(pl.multiple_of(j * 96, 96), 96)
            wide[i, part, :] = low[i, part, :].astype(F32)
            return carry

        lax.fori_loop(0, 8, body, 0)
        stores.append(pltpu.make_async_copy(wide.at[i], targets[i], out_sem.at[i]))
        stores[-1].start()
    singles = (
        (query_b, QUERY_B), (value_b, VALUE_B), (mixer_b, MIXER_B), (gain_1, GAIN_1),
        (shift_1, SHIFT_1), (outer_b, OUTER_B), (gain_2, GAIN_2), (shift_2, SHIFT_2),
    )
    for ref, row in singles:
        ref[...] = ext[row : row + 1, :].reshape(MODEL)
    inner_b[...] = jnp.concatenate([ext[8 + i : 9 + i, :] for i in range(4)], axis=1).reshape(INNER)
    init[...] = ext[16 : 16 + SLOTS, :]
    offset[...] = ext[40 : 40 + SLOTS, :]
    norm[...] = jnp.sqrt(ext[60:61, 0:1] * (1.0 / count))
    for copy in stores:
        copy.wait()


def widen(packed, ext, chains):
    square = shape((MODEL, MODEL), F32)
    line = shape((MODEL,), F32)
    slots = shape((SLOTS, MODEL), F32)
    return pl.pallas_call(
        functools.partial(widen_kernel, chains * SEGS * SLOTS * MODEL),
        out_shape=(
            square, square, square, square, shape((MODEL, INNER), F32), shape((INNER, MODEL), F32),
            line, line, line, line, line, shape((INNER,), F32), line, line, line, slots, slots,
            shape((1, 1), F32),
        ),
        in_specs=[ANY, VMEM],
        out_specs=(ANY,) * 6 + (VMEM,) * 12,
        scratch_shapes=[
            pltpu.VMEM((12, MODEL, MODEL), LOW),
            pltpu.VMEM((12, MODEL, MODEL), F32),
            DMA((12,)),
            DMA((12,)),
        ],
        compiler_params=pltpu.CompilerParams(vmem_limit_bytes=60 << 20),
        name="widen",
    )(packed, ext)


def shards(
    tokens, documents, resets, cotangent, query_weight, query_bias, key_weight, value_weight,
    value_bias, mixer_weight, mixer_bias, first_gain, first_shift, inner_weight, inner_bias,
    outer_weight, outer_bias, second_gain, second_shift, memory_init, write_offset,
):
    weights = (query_weight, key_weight, value_weight, mixer_weight, inner_weight, outer_weight)
    vectors = (
        query_bias, value_bias, mixer_bias, first_gain, first_shift, outer_bias, second_gain,
        second_shift,
    )
    tok = tokens[0]
    kv, probs, orow, ow, h1w, zw, h2w, xm, vec, inner_b = forward(
        resets, tok, documents[0], memory_init, write_offset, vectors, inner_bias, weights
    )
    layer_output, ub, act, dz, df, da, dh1, dout, sums, inner_sum = middle(
        tok, orow, cotangent[0], vec, inner_b, weights
    )
    drow, dmem, ubw, gw, dzw, dfw, daw, small = backward(
        resets, dout, kv, probs, h1w, zw, h2w, vec, weights
    )
    packed, input_grad, ext = weight_sums(
        tok, xm, drow, dmem, orow, ow, dh1, sums, inner_sum, small, ubw, gw, dzw, dfw, daw,
        ub, act, dz, df, da, weights,
    )
    packed, ext = sum_all(packed, ext)
    (
        query_w, key_w, value_w, mixer_w, inner_w, outer_w, query_b, value_b, mixer_b, gain_1,
        shift_1, inner_b, outer_b, gain_2, shift_2, init, offset, memory_norm,
    ) = widen(packed, ext, lax.axis_size("chain"))
    return (
        layer_output, input_grad, query_w, query_b, key_w, value_w, value_b, mixer_w, mixer_b,
        gain_1, shift_1, inner_w, inner_b, outer_w, outer_b, gain_2, shift_2, init, offset,
        memory_norm.reshape(()),
    )


def solution(mesh):
    tokens = P("chain", None, "seq", None)
    in_specs = (tokens, P("chain", None, "seq"), P("chain", None), tokens) + (P(),) * 17
    out_specs = (tokens, tokens) + (P(),) * 18
    return jax.shard_map(shards, mesh=mesh, in_specs=in_specs, out_specs=out_specs, check_vma=False)
```

```python
import functools

import jax
import jax.numpy as jnp
from jax import lax
from jax.experimental import pallas as pl
from jax.experimental.pallas import tpu as pltpu
from jax.sharding import PartitionSpec as P

MESH = pl.DeviceIdType.MESH
LOW = jnp.bfloat16
F32 = jnp.float32
SEGS = 3
BLOCK = 128
MODEL = 768
INNER = 3072
SLOTS = 20
PAD = 32
MEMORY = 2 * PAD
ROWS = SEGS * BLOCK
TOKENS = 512
KEYS = 640
QUERIES = TOKENS + PAD
HEAD = 64
MINE = 3
GROUP = MINE * HEAD
TRIPLE = 3 * GROUP
SCALE = HEAD ** (-0.5)
EPS = 1e-12
HIDDEN = -1e30


def dot(left, right):
    return jnp.dot(left, right, preferred_element_type=F32)


def dot_t(left, right):
    return lax.dot_general(left, right, (((1,), (1,)), ((), ())), preferred_element_type=F32)


def t_dot(left, right):
    return lax.dot_general(left, right, (((0,), (0,)), ((), ())), preferred_element_type=F32)


def norm_parts(hidden):
    centre = hidden - jnp.mean(hidden, axis=-1, keepdims=True)
    spread = jnp.mean(centre * centre, axis=-1, keepdims=True)
    inverse = lax.rsqrt(spread + EPS)
    return centre * inverse, inverse


def norm_back(upstream, unit, inverse, gain):
    scaled = upstream * gain
    first = jnp.mean(scaled, axis=-1, keepdims=True)
    second = jnp.mean(scaled * unit, axis=-1, keepdims=True)
    return (scaled - first - unit * second) * inverse


def gelu_parts(values):
    below = 0.5 * (1.0 + lax.erf(values * (0.5**0.5)))
    density = jnp.exp(-0.5 * values * values) * 0.3989422804014327
    return values * below, below + values * density


def column_sum(values):
    return jnp.sum(values.astype(F32), axis=0, keepdims=True)


def ring(off):
    return lax.rem(lax.axis_index("seq") + off + 4, 4)


def ring_barrier():
    barrier = pltpu.get_barrier_semaphore()
    for off in (1, 2, 3):
        pl.semaphore_signal(
            barrier, inc=1, device_id=(lax.axis_index("chain"), ring(off)), device_id_type=MESH
        )
    pl.semaphore_wait(barrier, 3)


def push(started, src, dst, s_sem, r_sem, off):
    copy = pltpu.make_async_remote_copy(
        src_ref=src,
        dst_ref=dst,
        send_sem=s_sem,
        recv_sem=r_sem,
        device_id=(lax.axis_index("chain"), ring(off)),
        device_id_type=MESH,
    )
    copy.start()
    started.append(copy)
    return copy


def fetch(pairs, sems):
    copies = [pltpu.make_async_copy(src, dst, sems.at[i]) for i, (src, dst) in enumerate(pairs)]
    for copy in copies:
        copy.start()
    return copies


QUERY_B, VALUE_B, MIXER_B, GAIN_1, SHIFT_1, OUTER_B, GAIN_2, SHIFT_2 = range(8)


def forward_kernel(
    resets, tok, docs, init_in, offset_in, query_b, value_b, mixer_b, gain_1, shift_1, outer_b,
    gain_2, shift_2, inner_in, wq_h, wk_h, wv_h, wm_h, wi_h, wo_h,
    kv, probs, orow, ow, h1w, zw, h2w, xm, vec, inner_b,
    wq, wk, wv, wm, wi, wo, wown, vown, sbuf, lab, bias, osend, owsend, init, offset,
    w_sem, q_s, q_r, o_s, o_r, m_s, m_r, l_s, l_r,
):
    z = lax.axis_index("seq")
    fetched = fetch(
        [(wq_h, wq), (wk_h, wk), (wv_h, wv), (wm_h, wm), (wi_h, wi), (wo_h, wo)], w_sem
    )
    started = []
    vectors = (query_b, value_b, mixer_b, gain_1, shift_1, outer_b, gain_2, shift_2)
    for i, ref in enumerate(vectors):
        vec[i : i + 1, :] = ref[...].astype(F32).reshape(1, MODEL)
    inner_b[...] = inner_in[...].astype(F32).reshape(1, INNER)
    for wide, ref in ((init, init_in), (offset, offset_in)):
        wide[...] = jnp.zeros((PAD, MODEL), LOW)
        wide[0:SLOTS, :] = ref[...]
    ring_barrier()
    lab[pl.ds(z, 1)] = docs[...][None]
    label_copies = [
        push(started, docs, lab.at[z], l_s.at[d - 1], l_r.at[d - 1], d) for d in (1, 2, 3)
    ]
    tokens = tok[...].reshape(ROWS, MODEL)
    fetched[0].wait()
    queries = ((dot(tokens, wq[...]) + vec[QUERY_B : QUERY_B + 1, :]) * SCALE).astype(LOW)
    for g in range(4):
        for s in range(SEGS):
            sbuf[g, s, :, 0:GROUP] = queries[
                s * BLOCK : (s + 1) * BLOCK, g * GROUP : (g + 1) * GROUP
            ]
    fetched[1].wait()
    keys = dot(tokens, wk[...]).astype(LOW)
    for g in range(4):
        for s in range(SEGS):
            sbuf[g, s, :, GROUP : 2 * GROUP] = keys[
                s * BLOCK : (s + 1) * BLOCK, g * GROUP : (g + 1) * GROUP
            ]
    fetched[2].wait()
    values = (dot(tokens, wv[...]) + vec[VALUE_B : VALUE_B + 1, :]).astype(LOW)
    for g in range(4):
        for s in range(SEGS):
            sbuf[g, s, :, 2 * GROUP :] = values[
                s * BLOCK : (s + 1) * BLOCK, g * GROUP : (g + 1) * GROUP
            ]
    here = pl.ds(pl.multiple_of(z * BLOCK, BLOCK), BLOCK)
    row_copies = []
    for s in range(SEGS):
        row_copies.append(
            [
                push(
                    started, sbuf.at[ring(d), s], kv.at[s, here],
                    q_s.at[s, d - 1], q_r.at[s, d - 1], d,
                )
                for d in (1, 2, 3)
            ]
        )
    for s in range(SEGS):
        kv[s, here, :] = sbuf[z, s]
        kv[s, TOKENS + MEMORY :, :] = jnp.zeros((KEYS - TOKENS - MEMORY, TRIPLE), LOW)
    for g in range(4):

        @pl.when(z == g)
        def _():
            cut = slice(g * GROUP, (g + 1) * GROUP)
            wown[:, 0:GROUP] = wq[:, cut]
            wown[:, GROUP : 2 * GROUP] = wk[:, cut]
            wown[:, 2 * GROUP :] = wv[:, cut]
            vown[0:1, 0:GROUP] = vec[QUERY_B : QUERY_B + 1, cut]
            vown[0:1, GROUP : 2 * GROUP] = jnp.zeros((1, GROUP), F32)
            vown[0:1, 2 * GROUP :] = vec[VALUE_B : VALUE_B + 1, cut]

    lane = lax.broadcasted_iota(jnp.int32, (1, TRIPLE), 1)
    factor = jnp.where(lane < GROUP, SCALE, 1.0)
    slot = lax.broadcasted_iota(jnp.int32, (PAD, MODEL), 0)
    key_lane = lax.broadcasted_iota(jnp.int32, (PAD, KEYS), 1)
    filled = (key_lane < TOKENS + SLOTS) | (
        (key_lane >= TOKENS + PAD) & (key_lane < TOKENS + PAD + SLOTS)
    )
    write_bias = jnp.where(filled, 0.0, HIDDEN)

    def attend(query_rows, mask, s, row_at, rows):
        parts = []
        for h in range(MINE):
            key_head = kv[s, :, GROUP + h * HEAD : GROUP + (h + 1) * HEAD]
            value_head = kv[s, :, 2 * GROUP + h * HEAD : 2 * GROUP + (h + 1) * HEAD]
            scores = dot_t(query_rows[:, h * HEAD : (h + 1) * HEAD], key_head) + mask
            weights = jnp.exp(scores - jnp.max(scores, axis=-1, keepdims=True))
            total = jnp.sum(weights, axis=-1, keepdims=True)
            prob = (weights * (1.0 / total)).astype(LOW)
            probs[s, h, pl.ds(row_at, rows), :] = prob
            parts.append(dot(prob, value_head))
        return jnp.concatenate(parts, axis=1).astype(LOW)

    memory = init[...]
    for copy in label_copies:
        copy.wait_recv()
    for s in range(SEGS):
        for i in range(4):
            column = jnp.transpose(jnp.broadcast_to(lab[i, s : s + 1, :].astype(F32), (BLOCK, BLOCK)))
            for j in range(4):
                row = jnp.broadcast_to(lab[j, s : s + 1, :].astype(F32), (BLOCK, BLOCK))
                bias[s, i * BLOCK : (i + 1) * BLOCK, j * BLOCK : (j + 1) * BLOCK] = jnp.where(
                    column == row, 0.0, HIDDEN
                )
            bias[s, i * BLOCK : (i + 1) * BLOCK, TOKENS:] = jnp.broadcast_to(
                write_bias[0:1, TOKENS:], (BLOCK, BLOCK)
            )
    out_copies = []
    for s in range(SEGS):
        written_in = (memory.astype(F32) + offset[...].astype(F32)).astype(LOW)
        xm[s, 0:PAD, :] = written_in
        xm[s, PAD:, :] = memory
        kv[s, TOKENS : TOKENS + MEMORY, :] = (
            (dot(xm[s], wown[...]) + vown[0:1, :]) * factor
        ).astype(LOW)
        for copy in row_copies[s]:
            copy.wait_recv()
        if s < SEGS - 1:
            mixed = attend(kv[s, TOKENS : TOKENS + PAD, :], write_bias, s, TOKENS, PAD)
            owsend[s] = mixed
            ow[s, pl.ds(z, 1)] = mixed[None]
            write_copies = [
                push(started, owsend.at[s], ow.at[s, z], m_s.at[s, d - 1], m_r.at[s, d - 1], d)
                for d in (1, 2, 3)
            ]

        def block(i, carry):
            row_at = pl.multiple_of(i * BLOCK, BLOCK)
            rows = pl.ds(row_at, BLOCK)
            osend[s, i] = attend(kv[s, rows, :], bias[s, rows, :], s, row_at, BLOCK)
            return carry

        lax.fori_loop(0, 4, block, 0)
        part = slice(s * BLOCK, (s + 1) * BLOCK)
        out_copies += [
            push(
                started, osend.at[s, ring(d)], orow.at[z, part],
                o_s.at[s, d - 1], o_r.at[s, d - 1], d,
            )
            for d in (1, 2, 3)
        ]
        orow[z, part, :] = osend[s, z]
        if s < SEGS - 1:
            if s == 0:
                for copy in fetched[3:]:
                    copy.wait()
            for copy in write_copies:
                copy.wait_recv()
            hidden = xm[s, 0:PAD, :].astype(F32) + vec[MIXER_B : MIXER_B + 1, :]
            for g in range(4):
                hidden = hidden + dot(ow[s, g], wm[g * GROUP : (g + 1) * GROUP, :])
            h1w[s] = hidden
            unit, _ = norm_parts(hidden)
            upper = unit * vec[GAIN_1 : GAIN_1 + 1, :] + vec[SHIFT_1 : SHIFT_1 + 1, :]
            inner = dot(upper.astype(LOW), wi[...]) + inner_b[...]
            zw[s] = inner
            active, _ = gelu_parts(inner)
            hidden = upper + dot(active.astype(LOW), wo[...]) + vec[OUTER_B : OUTER_B + 1, :]
            h2w[s] = hidden
            unit, _ = norm_parts(hidden)
            result = unit * vec[GAIN_2 : GAIN_2 + 1, :] + vec[SHIFT_2 : SHIFT_2 + 1, :]
            flag = jnp.full((PAD, MODEL), resets[0, s], jnp.int32)
            result = jnp.where(flag > 0, init[...].astype(F32), result)
            memory = jnp.where(slot < SLOTS, result, 0.0).astype(LOW)
    for copy in out_copies:
        copy.wait_recv()
    for copy in started:
        copy.wait_send()


def shape(dims, kind=LOW):
    return jax.ShapeDtypeStruct(dims, kind)


VMEM = pl.BlockSpec(memory_space=pltpu.VMEM)
ANY = pl.BlockSpec(memory_space=pl.ANY)
DMA = pltpu.SemaphoreType.DMA


def weight_buffers():
    return [pltpu.VMEM((MODEL, MODEL), LOW) for _ in range(4)] + [
        pltpu.VMEM((MODEL, INNER), LOW),
        pltpu.VMEM((INNER, MODEL), LOW),
    ]


def forward(resets, tok, docs, init, offset, vectors, inner_b, weights):
    return pl.pallas_call(
        forward_kernel,
        out_shape=(
            shape((SEGS, KEYS, TRIPLE)),
            shape((SEGS, MINE, QUERIES, KEYS)),
            shape((4, ROWS, GROUP)),
            shape((2, 4, PAD, GROUP)),
            shape((2, PAD, MODEL), F32),
            shape((2, PAD, INNER), F32),
            shape((2, PAD, MODEL), F32),
            shape((SEGS, MEMORY, MODEL)),
            shape((8, MODEL), F32),
            shape((1, INNER), F32),
        ),
        in_specs=[pl.BlockSpec(memory_space=pltpu.SMEM)] + [VMEM] * 13 + [ANY] * 6,
        out_specs=(VMEM,) * 10,
        scratch_shapes=weight_buffers()
        + [
            pltpu.VMEM((MODEL, TRIPLE), LOW),
            pltpu.VMEM((8, TRIPLE), F32),
            pltpu.VMEM((4, SEGS, BLOCK, TRIPLE), LOW),
            pltpu.VMEM((4, SEGS, BLOCK), jnp.int32),
            pltpu.VMEM((SEGS, TOKENS, KEYS), F32),
            pltpu.VMEM((SEGS, 4, BLOCK, GROUP), LOW),
            pltpu.VMEM((2, PAD, GROUP), LOW),
            pltpu.VMEM((PAD, MODEL), LOW),
            pltpu.VMEM((PAD, MODEL), LOW),
            DMA((6,)),
            DMA((SEGS, 3)),
            DMA((SEGS, 3)),
            DMA((SEGS, 3)),
            DMA((SEGS, 3)),
            DMA((2, 3)),
            DMA((2, 3)),
            DMA((3,)),
            DMA((3,)),
        ],
        compiler_params=pltpu.CompilerParams(
            collective_id=1, has_side_effects=True, vmem_limit_bytes=60 << 20
        ),
        name="forward_attention",
    )(resets, tok, docs, init, offset, *vectors, inner_b, *weights)


HALF = 384
CHUNK = 96
SUB = 48
SIDE = 384
ORDERS = (("x", "y", "z"), ("y", "z", "x"), ("z", "x", "y"))


def places():
    chain = lax.axis_index("chain")
    return {
        "x": chain // 8,
        "y": lax.rem(chain // 2, 4),
        "z": lax.axis_index("seq"),
        "core": lax.rem(chain, 2),
    }


def peer(at, axis, off):
    at = dict(at)
    size = 2 if axis == "core" else 4
    at[axis] = lax.rem(at[axis] + off + size, size)
    return ((at["x"] * 4 + at["y"]) * 2 + at["core"], at["z"])


def greet(at, peers):
    barrier = pltpu.get_barrier_semaphore()
    for axis, off in peers:
        pl.semaphore_signal(barrier, inc=1, device_id=peer(at, axis, off), device_id_type=MESH)
    pl.semaphore_wait(barrier, len(peers))


ALL_PEERS = [("core", 1)] + [(axis, off) for axis in "xyz" for off in (1, 2, 3)]


def add_rows(out, out_start, terms, rows, step=48):
    def body(i, carry):
        base = i * step
        total = None
        for ref, start in terms:
            term = ref[pl.ds(pl.multiple_of(start + base, 16), step), :].astype(jnp.float32)
            total = term if total is None else total + term
        out[pl.ds(pl.multiple_of(out_start + base, 16), step), :] = total.astype(out.dtype)
        return carry

    lax.fori_loop(0, rows // step, body, 0)


def middle_kernel(
    tok, orow, cot, vec, inner_b, wm_h, wi_h, wo_h,
    out, ub, act, dz, df, da, dh1, dout, sums, inner_sum,
    wm, wi, wo, slope, total, unit_1, inverse_1, w_sem,
):
    fetched = fetch([(wm_h, wm), (wi_h, wi), (wo_h, wo)], w_sem)
    gain_1 = vec[GAIN_1 : GAIN_1 + 1, :]
    gain_2 = vec[GAIN_2 : GAIN_2 + 1, :]
    hidden = tok[...].reshape(ROWS, MODEL).astype(F32) + vec[MIXER_B : MIXER_B + 1, :]
    fetched[0].wait()
    for g in range(4):
        hidden = hidden + dot(orow[g], wm[g * GROUP : (g + 1) * GROUP, :])
    unit, inverse = norm_parts(hidden)
    unit_1[...] = unit
    inverse_1[...] = inverse
    upper = unit * gain_1 + vec[SHIFT_1 : SHIFT_1 + 1, :]
    ub[...] = upper.astype(LOW)
    total[...] = upper + vec[OUTER_B : OUTER_B + 1, :]
    for copy in fetched[1:]:
        copy.wait()

    def ahead(j, carry):
        cut = pl.ds(pl.multiple_of(j * MODEL, MODEL), MODEL)
        inner = dot(ub[...], wi[:, cut]) + inner_b[:, cut]
        active, slant = gelu_parts(inner)
        active = active.astype(LOW)
        act[:, cut] = active
        slope[:, cut] = slant
        total[...] += dot(active, wo[cut, :])
        return carry

    lax.fori_loop(0, INNER // MODEL, ahead, 0)
    unit, inverse = norm_parts(total[...])
    result = unit * gain_2 + vec[SHIFT_2 : SHIFT_2 + 1, :]
    out[...] = result.astype(LOW).reshape(1, SEGS, BLOCK, MODEL)
    upstream = cot[...].reshape(ROWS, MODEL).astype(F32)
    sums[GAIN_2 : GAIN_2 + 1, :] = column_sum(upstream * unit)
    sums[SHIFT_2 : SHIFT_2 + 1, :] = column_sum(upstream)
    d_hidden = norm_back(upstream, unit, inverse, gain_2)
    total[...] = d_hidden
    d_low = d_hidden.astype(LOW)
    df[...] = d_low
    sums[OUTER_B : OUTER_B + 1, :] = column_sum(d_low)

    def back(j, carry):
        cut = pl.ds(pl.multiple_of(j * MODEL, MODEL), MODEL)
        d_inner = (dot_t(df[...], wo[cut, :]) * slope[:, cut]).astype(LOW)
        dz[:, cut] = d_inner
        inner_sum[:, cut] = column_sum(d_inner)
        total[...] += dot_t(d_inner, wi[:, cut])
        return carry

    lax.fori_loop(0, INNER // MODEL, back, 0)
    upstream = total[...]
    unit = unit_1[...]
    sums[GAIN_1 : GAIN_1 + 1, :] = column_sum(upstream * unit)
    sums[SHIFT_1 : SHIFT_1 + 1, :] = column_sum(upstream)
    d_hidden = norm_back(upstream, unit, inverse_1[...], gain_1)
    dh1[...] = d_hidden
    d_low = d_hidden.astype(LOW)
    da[...] = d_low
    sums[MIXER_B : MIXER_B + 1, :] = column_sum(d_low)
    sums[QUERY_B : QUERY_B + 2, :] = jnp.zeros((2, MODEL), F32)
    for g in range(4):
        dout[g] = dot_t(d_low, wm[g * GROUP : (g + 1) * GROUP, :]).astype(LOW)


def middle(tok, orow, cot, vec, inner_b, weights):
    return pl.pallas_call(
        middle_kernel,
        out_shape=(
            shape((1, SEGS, BLOCK, MODEL)),
            shape((ROWS, MODEL)),
            shape((ROWS, INNER)),
            shape((ROWS, INNER)),
            shape((ROWS, MODEL)),
            shape((ROWS, MODEL)),
            shape((ROWS, MODEL), F32),
            shape((4, ROWS, GROUP)),
            shape((8, MODEL), F32),
            shape((1, INNER), F32),
        ),
        in_specs=[VMEM] * 5 + [ANY] * 3,
        out_specs=(VMEM,) * 10,
        scratch_shapes=[
            pltpu.VMEM((MODEL, MODEL), LOW),
            pltpu.VMEM((MODEL, INNER), LOW),
            pltpu.VMEM((INNER, MODEL), LOW),
            pltpu.VMEM((ROWS, INNER), F32),
            pltpu.VMEM((ROWS, MODEL), F32),
            pltpu.VMEM((ROWS, MODEL), F32),
            pltpu.VMEM((ROWS, 1), F32),
            DMA((3,)),
        ],
        compiler_params=pltpu.CompilerParams(vmem_limit_bytes=60 << 20),
        name="token_layer",
    )(tok, orow, cot, vec, inner_b, *weights[3:])


def backward_kernel(
    resets, dout, kv, probs, h1w, zw, h2w, vec,
    wq_h, wk_h, wv_h, wm_h, wi_h, wo_h,
    drow, dmem, ubw, gw, dzw, dfw, daw, small, doh, dow, dh1w,
    wq, wk, wv, wm, wi, wo, acc, dsend, msend, wide,
    w_sem, d_s, d_r, x_s, x_r, m_s, m_r,
):
    z = lax.axis_index("seq")
    fetched = fetch(
        [(wq_h, wq), (wk_h, wk), (wv_h, wv), (wm_h, wm), (wi_h, wi), (wo_h, wo)], w_sem
    )
    started = []
    ring_barrier()
    here = pl.ds(pl.multiple_of(z * BLOCK, BLOCK), BLOCK)
    in_copies = {}
    for s in reversed(range(SEGS)):
        part = slice(s * BLOCK, (s + 1) * BLOCK)
        in_copies[s] = [
            push(
                started, dout.at[ring(d), part], doh.at[s, here],
                d_s.at[s, d - 1], d_r.at[s, d - 1], d,
            )
            for d in (1, 2, 3)
        ]
        doh[s, here, :] = dout[z, part, :]
    gain_1 = vec[GAIN_1 : GAIN_1 + 1, :]
    gain_2 = vec[GAIN_2 : GAIN_2 + 1, :]

    def head_back(s, h, d_rows, rows):
        cut = slice(h * HEAD, (h + 1) * HEAD)
        key_head = kv[s, :, GROUP + h * HEAD : GROUP + (h + 1) * HEAD]
        value_head = kv[s, :, 2 * GROUP + h * HEAD : 2 * GROUP + (h + 1) * HEAD]
        d_head = d_rows[:, cut]
        prob = probs[s, h, rows, :]
        wide_prob = prob.astype(F32)
        product = wide_prob * dot_t(d_head, value_head)
        delta = jnp.sum(product, axis=-1, keepdims=True)
        d_scores = (product - wide_prob * delta).astype(LOW)
        d_query = (dot(d_scores, key_head) * SCALE).astype(LOW)
        d_key = t_dot(d_scores, kv[s, rows, cut])
        d_value = t_dot(prob, d_head)
        return d_query, d_key, d_value

    def tokens_back(s):
        for copy in in_copies[s]:
            copy.wait_recv()
        rows = slice(0, TOKENS)
        for h in range(MINE):
            cut = slice(h * HEAD, (h + 1) * HEAD)
            d_query, d_key, d_value = head_back(s, h, doh[s], rows)
            dsend[s, :, cut] = d_query
            acc[s, :, cut] = d_key
            acc[s, :, GROUP + h * HEAD : GROUP + (h + 1) * HEAD] = d_value

    def writes_back(s):
        rows = slice(TOKENS, TOKENS + PAD)
        for h in range(MINE):
            cut = slice(h * HEAD, (h + 1) * HEAD)
            d_query, d_key, d_value = head_back(s, h, dow[...], rows)
            msend[s, 0:PAD, cut] = d_query
            acc[s, :, cut] += d_key
            acc[s, :, GROUP + h * HEAD : GROUP + (h + 1) * HEAD] += d_value

    mem_copies = {}
    row_copies = []

    def finish(s):
        if s == SEGS - 1:
            msend[s, :, 0:GROUP] = jnp.zeros((MEMORY, GROUP), LOW)
        else:
            msend[s, PAD:, 0:GROUP] = jnp.zeros((PAD, GROUP), LOW)
        msend[s, :, GROUP:] = acc[s, TOKENS : TOKENS + MEMORY, :].astype(LOW)
        mem_copies[s] = [
            push(started, msend.at[s], dmem.at[s - 1, z], m_s.at[s, d - 1], m_r.at[s, d - 1], d)
            for d in (1, 2, 3)
        ]
        dmem[s - 1, z] = msend[s]
        dsend[s, :, GROUP:] = acc[s, 0:TOKENS, :].astype(LOW)
        kept = slice((s - 1) * BLOCK, s * BLOCK)
        for d in (1, 2, 3):
            there = pl.ds(pl.multiple_of(ring(d) * BLOCK, BLOCK), BLOCK)
            row_copies.append(
                push(
                    started, dsend.at[s, there], drow.at[z, kept],
                    x_s.at[s, d - 1], x_r.at[s, d - 1], d,
                )
            )
        drow[z, kept, :] = dsend[s, here, :]

    sums = {}

    def add(name, value):
        sums[name] = value if name not in sums else sums[name] + value

    saved = {}

    def memory_back(s):
        for copy in mem_copies[s]:
            copy.wait_recv()
        for g in range(4):
            for t in range(3):
                wide[t, :, g * GROUP : (g + 1) * GROUP] = dmem[
                    s - 1, g, :, t * GROUP : (t + 1) * GROUP
                ]
        if s == SEGS - 1:
            for copy in fetched:
                copy.wait()
        d_rows = dot_t(wide[0], wq[...]) + dot_t(wide[1], wk[...]) + dot_t(wide[2], wv[...])
        write = d_rows[0:PAD]
        if s < SEGS - 1:
            write = write + saved[s]
        grad = write + d_rows[PAD:]
        add("offset", write)
        add("norm", jnp.sum(jnp.sum(grad * grad, axis=0, keepdims=True), axis=1, keepdims=True))
        flag = jnp.full((PAD, MODEL), resets[0, s - 1], jnp.int32) > 0
        add("init", jnp.where(flag, grad, 0.0))
        return jnp.where(flag, 0.0, grad)

    def layer_back(s, upstream):
        unit, inverse = norm_parts(h2w[s])
        add("gain_2", column_sum(upstream * unit))
        add("shift_2", column_sum(upstream))
        d_second = norm_back(upstream, unit, inverse, gain_2)
        d_low = d_second.astype(LOW)
        dfw[s] = d_low
        add("outer", column_sum(d_low))
        active, slant = gelu_parts(zw[s])
        gw[s] = active.astype(LOW)
        d_inner = (dot_t(d_low, wo[...]) * slant).astype(LOW)
        dzw[s] = d_inner
        add("inner", column_sum(d_inner))
        unit, inverse = norm_parts(h1w[s])
        ubw[s] = (unit * gain_1 + vec[SHIFT_1 : SHIFT_1 + 1, :]).astype(LOW)
        d_upper = dot_t(d_inner, wi[...]) + d_second
        add("gain_1", column_sum(d_upper * unit))
        add("shift_1", column_sum(d_upper))
        d_first = norm_back(d_upper, unit, inverse, gain_1)
        saved[s] = d_first
        if s == 0:
            dh1w[...] = d_first
        d_low = d_first.astype(LOW)
        daw[s] = d_low
        add("mixer", column_sum(d_low))
        own = pl.ds(pl.multiple_of(z * GROUP, HEAD), GROUP)
        dow[...] = dot_t(d_low, wm[own, :]).astype(LOW)

    tokens_back(2)
    finish(2)
    tokens_back(1)
    layer_back(1, memory_back(2))
    writes_back(1)
    finish(1)
    layer_back(0, memory_back(1))
    quarter = 0.25
    row = lax.broadcasted_iota(jnp.int32, (24, MODEL), 0)
    zero = jnp.zeros((1, MODEL), F32)
    small[0:8, :] = quarter * jnp.concatenate(
        [zero, zero]
        + [sums[n] for n in ("mixer", "gain_1", "shift_1", "outer", "gain_2", "shift_2")],
        axis=0,
    )
    small[8:16, :] = quarter * jnp.concatenate(
        [sums["inner"][:, i * MODEL : (i + 1) * MODEL] for i in range(4)] + [zero] * 4, axis=0
    )
    small[16:40, :] = quarter * sums["init"][0:24]
    small[40:64, :] = quarter * (
        sums["offset"][0:24]
        + jnp.where(row >= SLOTS, jnp.broadcast_to(sums["norm"], (24, MODEL)), 0.0)
    )
    for copy in in_copies[0] + row_copies:
        copy.wait_recv()
    for copy in started:
        copy.wait_send()


def backward(resets, dout, kv, probs, h1w, zw, h2w, vec, weights):
    return pl.pallas_call(
        backward_kernel,
        out_shape=(
            shape((4, ROWS - BLOCK, TRIPLE)),
            shape((SEGS - 1, 4, MEMORY, TRIPLE)),
            shape((2, PAD, MODEL)),
            shape((2, PAD, INNER)),
            shape((2, PAD, INNER)),
            shape((2, PAD, MODEL)),
            shape((2, PAD, MODEL)),
            shape((64, MODEL), F32),
            shape((SEGS, TOKENS, GROUP)),
            shape((PAD, GROUP)),
            shape((PAD, MODEL), F32),
        ),
        in_specs=[pl.BlockSpec(memory_space=pltpu.SMEM)] + [VMEM] * 7 + [ANY] * 6,
        out_specs=(VMEM,) * 11,
        scratch_shapes=weight_buffers()
        + [
            pltpu.VMEM((SEGS, KEYS, 2 * GROUP), F32),
            pltpu.VMEM((SEGS, TOKENS, TRIPLE), LOW),
            pltpu.VMEM((SEGS, MEMORY, TRIPLE), LOW),
            pltpu.VMEM((3, MEMORY, MODEL), LOW),
            DMA((6,)),
            DMA((SEGS, 3)),
            DMA((SEGS, 3)),
            DMA((SEGS, 3)),
            DMA((SEGS, 3)),
            DMA((SEGS, 3)),
            DMA((SEGS, 3)),
        ],
        compiler_params=pltpu.CompilerParams(
            collective_id=2, has_side_effects=True, vmem_limit_bytes=60 << 20
        ),
        name="backward_attention",
    )(resets, dout, kv, probs, h1w, zw, h2w, vec, *weights)


FULL = ROWS + MEMORY
MOST = ROWS + PAD
UNITS = ((4, 5, 6), (7, 8, 9), (10, 11, 3), (0, 1, 2))


def finish_kernel(
    tok, xm, drow, dmem, orow, ow, dh1, sums, inner_sum, small, ubw, gw, dzw, dfw, daw, dow, dh1w,
    kv_h, probs_h, doh_h, ub_h, act_h, dz_h, df_h, da_h, wq_h, wk_h, wv_h,
    packed, input_grad, ext,
    kv, probs, doh, ub, act, dz, df, da, wq, wk, wv, rows, triple, mixed, acc, dsend, msend,
    drow0, dmall, wide, g, crecv, r1, r2, r3, slots, own_ext, ecore, ex, ey, ez,
    w_sem, x_s, x_r, m_s, m_r, c_s, c_r, a_s, a_r, b_s, b_r, d_s, d_r, e_s, e_r, f_s, f_r,
    loc, free, n_s, n_r, o_s, o_r, gc_s, gc_r, t_s, t_r,
):
    at = places()
    z = at["z"]
    core = at["core"]
    top = pl.ds(0, ROWS)
    fetched = fetch(
        [
            (ub_h, ub.at[top]), (dz_h, dz.at[top]), (kv_h.at[0], kv), (probs_h.at[0], probs),
            (doh_h.at[0], doh), (act_h, act.at[top]), (df_h, df.at[top]), (da_h, da.at[top]),
            (wq_h, wq), (wk_h, wk), (wv_h, wv),
        ],
        w_sem,
    )
    started = []

    def send(src, dst, s_sem, r_sem, axis, off):
        copy = pltpu.make_async_remote_copy(
            src_ref=src, dst_ref=dst, send_sem=s_sem, recv_sem=r_sem,
            device_id=peer(at, axis, off), device_id_type=MESH,
        )
        copy.start()
        started.append(copy)
        return copy

    def turn(value, off):
        return lax.rem(value + off + 4, 4)

    def ds(start, size):
        return pl.ds(pl.multiple_of(start, 16), size)

    place1 = [at[order[0]] for order in ORDERS]
    place2 = [at[order[1]] for order in ORDERS]
    place3 = [at[order[2]] for order in ORDERS]
    live = {}

    def sub_of(ref, start, n):
        side = pl.ds(pl.multiple_of(lax.rem(n, 2) * SIDE, 128), SIDE)
        return ref.at[ds(start + (n // 2) * SUB, SUB), side]

    def home(p, off):
        return core * HALF + turn(place1[p], off) * CHUNK

    def block_done(u, p):
        b = UNITS[u][p]
        live["core", u, p] = send(
            g.at[b, ds((1 - core) * HALF, HALF)], crecv.at[u, p],
            c_s.at[u, p], c_r.at[u, p], "core", 1,
        )
        started.pop()

    def stage1(u):
        for p in range(3):
            b = UNITS[u][p]
            live["core", u, p].wait_recv()
            held = crecv.at[u, p]
            start = turn(place1[p], 2) * CHUNK
            add_rows(held, start, [(g.at[b], core * HALF + start), (held, start)], CHUNK)
            live["a", u, p] = [
                send(
                    held.at[ds(start + i * SUB, SUB)], r1.at[u, p, i],
                    a_s.at[u, p, i], a_r.at[u, p, i], ORDERS[p][0], 1 + 2 * i,
                )
                for i in range(2)
            ]
        for p in range(3):
            b = UNITS[u][p]
            held = crecv.at[u, p]
            for off in (1, 3, 0):
                start = turn(place1[p], off) * CHUNK
                add_rows(held, start, [(g.at[b], core * HALF + start), (held, start)], CHUNK)
            live["core", u, p].wait_send()
        pl.semaphore_signal(
            free.at[u], inc=1, device_id=peer(at, "core", 1), device_id_type=MESH
        )

    def stage2(u):
        for p in range(3):
            held = crecv.at[u, p]
            live["b", u, p] = []
            for i in range(2):
                start = turn(place1[p], 1 + 2 * i) * CHUNK
                live["a", u, p][i].wait_recv()
                half = start + i * SUB
                add_rows(held, half, [(held, half), (r1.at[u, p, i], 0)], SUB)
                live["b", u, p].append(
                    send(
                        held.at[ds(start, CHUNK)], r2.at[u, p, i],
                        b_s.at[u, p, i], b_r.at[u, p, i], ORDERS[p][0], 1 + 2 * i,
                    )
                )

    def stage3(u):
        for p in range(3):
            held = crecv.at[u, p]
            start = place1[p] * CHUNK
            for copy in live["b", u, p]:
                copy.wait_recv()
            add_rows(held, start, [(held, start), (r2.at[u, p, 0], 0), (r2.at[u, p, 1], 0)], CHUNK)
            live["d", u, p] = [
                send(
                    sub_of(held, start, turn(place2[p], d)), r3.at[u, p, d - 1],
                    d_s.at[u, p, d - 1], d_r.at[u, p, d - 1], ORDERS[p][1], d,
                )
                for d in (1, 2, 3)
            ]

    def stage4(u):
        for p in range(3):
            for copy in live["d", u, p]:
                copy.wait_recv()
            total = sub_of(crecv.at[u, p], place1[p] * CHUNK, place2[p])[...].astype(F32)
            for d in range(3):
                total = total + r3[u, p, d].astype(F32)
            slots[u, p, pl.ds(place3[p], 1)] = total.astype(LOW)[None]
            live["e", u, p] = [
                send(
                    slots.at[u, p, place3[p]], slots.at[u, p, place3[p]],
                    e_s.at[u, p, d - 1], e_r.at[u, p, d - 1], ORDERS[p][2], d,
                )
                for d in (1, 2, 3)
            ]

    def stage5(u):
        for p in range(3):
            for copy in live["e", u, p]:
                copy.wait_recv()
            total = slots[u, p, 0].astype(F32)
            for i in range(1, 4):
                total = total + slots[u, p, i].astype(F32)
            target = sub_of(g.at[UNITS[u][p]], home(p, 0), place2[p])
            target[...] = total.astype(LOW)
            live["f", u, p] = [
                send(target, target, f_s.at[u, p, d - 1], f_r.at[u, p, d - 1], ORDERS[p][1], d)
                for d in (1, 2, 3)
            ]

    def across(u, p, j, start, count):
        piece = g.at[UNITS[u][p], ds(start, count)]
        live["gc", u, p, j] = send(piece, piece, gc_s.at[u, p, j], gc_r.at[u, p, j], "core", 1)

    def stage6(u):
        pl.semaphore_wait(free.at[u], 1)
        for p in range(3):
            for copy in live["f", u, p]:
                copy.wait_recv()
            piece = g.at[UNITS[u][p], ds(home(p, 0), CHUNK)]
            live["n", u, p] = [
                send(piece, piece, n_s.at[u, p, i], n_r.at[u, p, i], ORDERS[p][0], 1 + 2 * i)
                for i in range(2)
            ]
            across(u, p, 0, home(p, 0), CHUNK)

    def stage7(u):
        for p in range(3):
            live["o", u, p] = []
            for i in range(2):
                live["n", u, p][i].wait_recv()
                start = home(p, 3 - 2 * i)
                piece = g.at[UNITS[u][p], ds(start + i * SUB, SUB)]
                live["o", u, p].append(
                    send(piece, piece, o_s.at[u, p, i], o_r.at[u, p, i], ORDERS[p][0], 1 + 2 * i)
                )
                across(u, p, 1 + i, start, CHUNK)

    def stage8(u):
        for p in range(3):
            for i in range(2):
                live["o", u, p][i].wait_recv()
                across(u, p, 3 + i, home(p, 2) + i * SUB, SUB)

    stores = []

    def stage9(u):
        for p in range(3):
            for j in range(5):
                live["gc", u, p, j].wait_recv()
            b = UNITS[u][p]
            stores.append(
                pltpu.make_async_copy(
                    g.at[b], packed.at[pl.ds(b * MODEL, MODEL)], loc.at[u, p]
                )
            )
            stores[-1].start()

    stages = {
        1: stage1, 2: stage2, 3: stage3, 4: stage4, 5: stage5, 6: stage6, 7: stage7, 8: stage8,
        9: stage9,
    }

    def wave(*pairs):
        for u, k in pairs:
            stages[k](u)

    low_at = jnp.minimum(z, 1)
    low_keep = (z < 2).astype(F32).astype(LOW)
    at_seg = jnp.minimum(z, 2)
    keep = (z < SEGS).astype(F32).astype(LOW)

    def inner_block(j):
        g[4 + j] = t_dot(ub[...], dz[:, j * MODEL : (j + 1) * MODEL]).astype(LOW)

    def outer_block(j):
        g[8 + j] = t_dot(act[:, j * MODEL : (j + 1) * MODEL], df[...]).astype(LOW)

    def mixer_block():
        for i in range(4):
            mixed[i, 0:ROWS, :] = orow[i]
            mixed[i, ROWS:, :] = ow[low_at, i]
        for i in range(4):
            g[3, i * GROUP : (i + 1) * GROUP, :] = t_dot(mixed[i], da[...]).astype(LOW)

    def head_back(h, d_rows, part):
        cut = slice(h * HEAD, (h + 1) * HEAD)
        key_head = kv[:, GROUP + h * HEAD : GROUP + (h + 1) * HEAD]
        value_head = kv[:, 2 * GROUP + h * HEAD : 2 * GROUP + (h + 1) * HEAD]
        d_head = d_rows[:, cut]
        prob = probs[h, part, :]
        wide_prob = prob.astype(F32)
        product = wide_prob * dot_t(d_head, value_head)
        delta = jnp.sum(product, axis=-1, keepdims=True)
        d_scores = (product - wide_prob * delta).astype(LOW)
        d_query = (dot(d_scores, key_head) * SCALE).astype(LOW)
        return d_query, t_dot(d_scores, kv[part, cut]), t_dot(prob, d_head)

    def head_tokens(h):
        cut = slice(h * HEAD, (h + 1) * HEAD)
        d_query, d_key, d_value = head_back(h, doh[...], slice(0, TOKENS))
        dsend[:, cut] = d_query
        acc[:, cut] = d_key
        acc[:, GROUP + h * HEAD : GROUP + (h + 1) * HEAD] = d_value

    def head_writes(h):
        cut = slice(h * HEAD, (h + 1) * HEAD)
        d_query, d_key, d_value = head_back(h, dow[...], slice(TOKENS, TOKENS + PAD))
        msend[0:PAD, cut] = d_query
        acc[:, cut] += d_key
        acc[:, GROUP + h * HEAD : GROUP + (h + 1) * HEAD] += d_value

    greet(at, ALL_PEERS)
    ub[ROWS:, :] = ubw[low_at]
    act[ROWS:, :] = gw[low_at]
    dz[ROWS:, :] = dzw[low_at] * low_keep
    df[ROWS:, :] = dfw[low_at] * low_keep
    da[ROWS:, :] = daw[low_at] * low_keep
    for copy in fetched[:2]:
        copy.wait()
    for j in range(3):
        inner_block(j)
        block_done(0, j)
    for copy in fetched[2:5]:
        copy.wait()
    head_tokens(0)
    wave((0, 1))
    head_tokens(1)
    head_tokens(2)
    for h in range(MINE):
        head_writes(h)
    msend[PAD:, 0:GROUP] = jnp.zeros((PAD, GROUP), LOW)
    msend[:, GROUP:] = acc[TOKENS : TOKENS + MEMORY, :].astype(LOW)
    dsend[:, GROUP:] = acc[0:TOKENS, :].astype(LOW)
    row_copies = []
    for d in (1, 2, 3):
        there = ds(ring(d) * BLOCK, BLOCK)
        row_copies.append(
            send(dsend.at[there], drow0.at[z], x_s.at[d - 1], x_r.at[d - 1], "z", d)
        )
        row_copies.append(
            send(msend, dmall.at[0, z], m_s.at[d - 1], m_r.at[d - 1], "z", d)
        )
    drow0[z] = dsend[ds(z * BLOCK, BLOCK), :]
    dmall[0, z] = msend[...]
    dmall[1:] = dmem[...]
    wave((0, 2))
    inner_block(3)
    block_done(1, 0)
    for copy in fetched[5:7]:
        copy.wait()
    for j in range(2):
        outer_block(j)
        block_done(1, 1 + j)
    wave((0, 3), (1, 1))
    for j in range(2, 4):
        outer_block(j)
        block_done(2, j - 2)
    fetched[7].wait()
    mixer_block()
    block_done(2, 2)
    wave((0, 4), (1, 2), (2, 1))
    rows[0:ROWS, :] = tok[...].reshape(ROWS, MODEL)
    rows[ROWS:, :] = xm[at_seg]
    for copy in row_copies:
        copy.wait_recv()
    for i in range(4):
        for t in range(3):
            cut = slice(i * GROUP, (i + 1) * GROUP)
            part = slice(t * GROUP, (t + 1) * GROUP)
            triple[t, 0:BLOCK, cut] = drow0[i, :, part]
            triple[t, BLOCK:ROWS, cut] = drow[i, :, part]
            triple[t, ROWS:, cut] = dmall[at_seg, i, :, part] * keep
            wide[t, :, cut] = dmall[0, i, :, part]
    for t in range(3):
        g[t] = t_dot(rows[...], triple[t]).astype(LOW)
        block_done(3, t)
    wave((0, 5), (1, 3), (2, 2), (3, 1))
    for copy in fetched[8:]:
        copy.wait()
    d_rows = dot_t(wide[0], wq[...]) + dot_t(wide[1], wk[...]) + dot_t(wide[2], wv[...])
    write = d_rows[0:PAD] + dh1w[...]
    grad = write + d_rows[PAD:]
    norm = jnp.sum(jnp.sum(grad * grad, axis=0, keepdims=True), axis=1, keepdims=True)
    own_ext[0:8, :] = small[0:8, :] + sums[...]
    own_ext[8:16, :] = small[8:16, :] + jnp.concatenate(
        [inner_sum[:, i * MODEL : (i + 1) * MODEL] for i in range(4)]
        + [jnp.zeros((4, MODEL), F32)],
        axis=0,
    )
    own_ext[QUERY_B : QUERY_B + 1, :] += column_sum(triple[0])
    own_ext[VALUE_B : VALUE_B + 1, :] += column_sum(triple[2])
    row = lax.broadcasted_iota(jnp.int32, (24, MODEL), 0)
    own_ext[16:40, :] = small[16:40, :] + 0.25 * grad[0:24]
    own_ext[40:64, :] = small[40:64, :] + 0.25 * (
        write[0:24] + jnp.where(row >= SLOTS, jnp.broadcast_to(norm, (24, MODEL)), 0.0)
    )
    half = pl.ds(pl.multiple_of(core * 32, 8), 32)
    other = pl.ds(pl.multiple_of((1 - core) * 32, 8), 32)
    small_core = send(own_ext.at[other], ecore, t_s.at[0], t_r.at[0], "core", 1)
    wave((0, 6), (1, 4), (2, 3), (3, 2))
    small_core.wait_recv()
    ecore[...] = own_ext[half, :] + ecore[...]
    small_x = [
        send(
            ecore.at[pl.ds(pl.multiple_of(turn(at["x"], d) * 8, 8), 8)],
            ex.at[d - 1], t_s.at[d], t_r.at[d], "x", d,
        )
        for d in (1, 2, 3)
    ]
    input_grad[...] = (
        dh1[...]
        + dot_t(triple[0, 0:ROWS, :], wq[...])
        + dot_t(triple[1, 0:ROWS, :], wk[...])
        + dot_t(triple[2, 0:ROWS, :], wv[...])
    ).reshape(1, SEGS, BLOCK, MODEL)
    wave((0, 7), (1, 5), (2, 4), (3, 3))
    for copy in small_x:
        copy.wait_recv()
    ey[pl.ds(at["y"], 1)] = (
        ecore[pl.ds(pl.multiple_of(at["x"] * 8, 8), 8), :] + ex[0] + ex[1] + ex[2]
    )[None]
    small_y = [
        send(ey.at[at["y"]], ey.at[at["y"]], t_s.at[3 + d], t_r.at[3 + d], "y", d)
        for d in (1, 2, 3)
    ]
    wave((0, 8), (1, 6), (2, 5), (3, 4))
    for copy in small_y:
        copy.wait_recv()
    ez[pl.ds(at["z"], 1)] = (ey[0] + ey[1] + ey[2] + ey[3])[None]
    small_z = [
        send(ez.at[at["z"]], ez.at[at["z"]], t_s.at[6 + d], t_r.at[6 + d], "z", d)
        for d in (1, 2, 3)
    ]
    wave((1, 7), (2, 6), (3, 5))
    for copy in small_z:
        copy.wait_recv()
    mine = pl.ds(pl.multiple_of(core * 32 + at["x"] * 8, 8), 8)
    ext[mine, :] = ez[0] + ez[1] + ez[2] + ez[3]
    small_back = [
        send(ext.at[mine], ext.at[mine], t_s.at[9 + d], t_r.at[9 + d], "x", d) for d in (1, 2, 3)
    ]
    wave((1, 8), (2, 7), (3, 6), (0, 9))
    for copy in small_back:
        copy.wait_recv()
    small_last = send(ext.at[half], ext.at[half], t_s.at[13], t_r.at[13], "core", 1)
    wave((2, 8), (3, 7), (1, 9), (3, 8), (2, 9))
    small_last.wait_recv()
    wave((3, 9))
    for copy in started:
        copy.wait_send()
    for copy in stores:
        copy.wait()


def finish_all(near, far):
    def buffer(*dims):
        return pltpu.VMEM(dims, LOW)

    def wide_buffer(*dims):
        return pltpu.VMEM(dims, F32)

    pairs = [
        (3,), (3,), (4, 3), (4, 3, 2), (4, 3, 2), (4, 3, 3), (4, 3, 3), (4, 3, 3), None,
        (4, 3, 2), (4, 3, 2), (4, 3, 5), (14,),
    ]
    sems = [DMA((11,))]
    for dims in pairs:
        if dims is None:
            sems += [DMA((4, 3)), pltpu.SemaphoreType.REGULAR((4,))]
        else:
            sems += [DMA(dims), DMA(dims)]
    return pl.pallas_call(
        finish_kernel,
        out_shape=(
            shape((12 * MODEL, MODEL)),
            shape((1, SEGS, BLOCK, MODEL), F32),
            shape((64, MODEL), F32),
        ),
        in_specs=[VMEM] * len(near) + [ANY] * len(far),
        out_specs=(ANY, VMEM, VMEM),
        scratch_shapes=[
            buffer(KEYS, TRIPLE),
            buffer(MINE, QUERIES, KEYS),
            buffer(TOKENS, GROUP),
            buffer(MOST, MODEL),
            buffer(MOST, INNER),
            buffer(MOST, INNER),
            buffer(MOST, MODEL),
            buffer(MOST, MODEL),
            buffer(MODEL, MODEL),
            buffer(MODEL, MODEL),
            buffer(MODEL, MODEL),
            buffer(FULL, MODEL),
            buffer(3, FULL, MODEL),
            buffer(4, MOST, GROUP),
            wide_buffer(KEYS, 2 * GROUP),
            buffer(TOKENS, TRIPLE),
            buffer(MEMORY, TRIPLE),
            buffer(4, BLOCK, TRIPLE),
            buffer(SEGS, 4, MEMORY, TRIPLE),
            buffer(3, MEMORY, MODEL),
            buffer(12, MODEL, MODEL),
            buffer(4, 3, HALF, MODEL),
            buffer(4, 3, 2, SUB, MODEL),
            buffer(4, 3, 2, CHUNK, MODEL),
            buffer(4, 3, 3, SUB, SIDE),
            buffer(4, 3, 4, SUB, SIDE),
            wide_buffer(64, MODEL),
            wide_buffer(32, MODEL),
            wide_buffer(3, 8, MODEL),
            wide_buffer(4, 8, MODEL),
            wide_buffer(4, 8, MODEL),
        ]
        + sems,
        compiler_params=pltpu.CompilerParams(
            collective_id=3, has_side_effects=True, vmem_limit_bytes=62 << 20
        ),
        name="weights_and_sums",
    )(*near, *far)


def widen_kernel(
    count, packed, ext, grad_in,
    grad_out, query_w, key_w, value_w, mixer_w, inner_w, outer_w, query_b, value_b, mixer_b, gain_1, shift_1,
    inner_b, outer_b, gain_2, shift_2, init, offset, norm,
    low, wide, in_sem, out_sem,
):
    through = pltpu.make_async_copy(grad_in, grad_out, in_sem.at[12])
    through.start()
    def rows(i):
        return pl.ds(i * MODEL, MODEL)

    loads = [pltpu.make_async_copy(packed.at[rows(i)], low.at[i], in_sem.at[i]) for i in range(12)]
    for copy in loads:
        copy.start()
    targets = [query_w, key_w, value_w, mixer_w]
    targets += [inner_w.at[:, rows(i)] for i in range(4)]
    targets += [outer_w.at[rows(i)] for i in range(4)]
    stores = []
    for i in range(12):
        loads[i].wait()

        def body(j, carry):
            part = pl.ds(pl.multiple_of(j * 96, 96), 96)
            wide[i, part, :] = low[i, part, :].astype(F32)
            return carry

        lax.fori_loop(0, 8, body, 0)
        stores.append(pltpu.make_async_copy(wide.at[i], targets[i], out_sem.at[i]))
        stores[-1].start()
    singles = (
        (query_b, QUERY_B), (value_b, VALUE_B), (mixer_b, MIXER_B), (gain_1, GAIN_1),
        (shift_1, SHIFT_1), (outer_b, OUTER_B), (gain_2, GAIN_2), (shift_2, SHIFT_2),
    )
    for ref, row in singles:
        ref[...] = ext[row : row + 1, :].reshape(MODEL)
    inner_b[...] = jnp.concatenate([ext[8 + i : 9 + i, :] for i in range(4)], axis=1).reshape(INNER)
    init[...] = ext[16 : 16 + SLOTS, :]
    offset[...] = ext[40 : 40 + SLOTS, :]
    norm[...] = jnp.sqrt(ext[60:61, 0:1] * (1.0 / count))
    for copy in stores:
        copy.wait()
    through.wait()


def widen(packed, ext, input_grad, chains):
    square = shape((MODEL, MODEL), F32)
    line = shape((MODEL,), F32)
    slots = shape((SLOTS, MODEL), F32)
    return pl.pallas_call(
        functools.partial(widen_kernel, chains * SEGS * SLOTS * MODEL),
        out_shape=(
            shape((1, SEGS, BLOCK, MODEL), F32), square, square, square, square, shape((MODEL, INNER), F32), shape((INNER, MODEL), F32),
            line, line, line, line, line, shape((INNER,), F32), line, line, line, slots, slots,
            shape((1, 1), F32),
        ),
        in_specs=[ANY, VMEM, VMEM],
        out_specs=(ANY,) * 7 + (VMEM,) * 12,
        scratch_shapes=[
            pltpu.VMEM((12, MODEL, MODEL), LOW),
            pltpu.VMEM((12, MODEL, MODEL), F32),
            DMA((13,)),
            DMA((12,)),
        ],
        compiler_params=pltpu.CompilerParams(vmem_limit_bytes=60 << 20),
        name="widen",
    )(packed, ext, input_grad)


def shards(
    tokens, documents, resets, cotangent, query_weight, query_bias, key_weight, value_weight,
    value_bias, mixer_weight, mixer_bias, first_gain, first_shift, inner_weight, inner_bias,
    outer_weight, outer_bias, second_gain, second_shift, memory_init, write_offset,
):
    weights = (query_weight, key_weight, value_weight, mixer_weight, inner_weight, outer_weight)
    vectors = (
        query_bias, value_bias, mixer_bias, first_gain, first_shift, outer_bias, second_gain,
        second_shift,
    )
    tok = tokens[0]
    kv, probs, orow, ow, h1w, zw, h2w, xm, vec, inner_b = forward(
        resets, tok, documents[0], memory_init, write_offset, vectors, inner_bias, weights
    )
    layer_output, ub, act, dz, df, da, dh1, dout, sums, inner_sum = middle(
        tok, orow, cotangent[0], vec, inner_b, weights
    )
    drow, dmem, ubw, gw, dzw, dfw, daw, small, doh, dow, dh1w = backward(
        resets, dout, kv, probs, h1w, zw, h2w, vec, weights
    )
    packed, input_grad, ext = finish_all(
        (
            tok, xm, drow, dmem, orow, ow, dh1, sums, inner_sum, small, ubw, gw, dzw, dfw, daw,
            dow, dh1w,
        ),
        (kv, probs, doh, ub, act, dz, df, da) + weights[:3],
    )
    (
        input_grad, query_w, key_w, value_w, mixer_w, inner_w, outer_w, query_b, value_b, mixer_b, gain_1,
        shift_1, inner_b, outer_b, gain_2, shift_2, init, offset, memory_norm,
    ) = widen(packed, ext, input_grad, lax.axis_size("chain"))
    return (
        layer_output, input_grad, query_w, query_b, key_w, value_w, value_b, mixer_w, mixer_b,
        gain_1, shift_1, inner_w, inner_b, outer_w, outer_b, gain_2, shift_2, init, offset,
        memory_norm.reshape(()),
    )


def solution(mesh):
    tokens = P("chain", None, "seq", None)
    in_specs = (tokens, P("chain", None, "seq"), P("chain", None), tokens) + (P(),) * 17
    out_specs = (tokens, tokens) + (P(),) * 18
    return jax.shard_map(shards, mesh=mesh, in_specs=in_specs, out_specs=out_specs, check_vma=False)
```

```python
import functools

import jax
import jax.numpy as jnp
from jax import lax
from jax.experimental import pallas as pl
from jax.experimental.pallas import tpu as pltpu
from jax.sharding import PartitionSpec as P

MESH = pl.DeviceIdType.MESH
LOW = jnp.bfloat16
F32 = jnp.float32
SEGS = 3
BLOCK = 128
MODEL = 768
INNER = 3072
SLOTS = 20
PAD = 32
MEMORY = 2 * PAD
ROWS = SEGS * BLOCK
TOKENS = 512
KEYS = 640
QUERIES = TOKENS + PAD
HEAD = 64
MINE = 3
GROUP = MINE * HEAD
TRIPLE = 3 * GROUP
SCALE = HEAD ** (-0.5)
EPS = 1e-12
HIDDEN = -1e30


def dot(left, right):
    return jnp.dot(left, right, preferred_element_type=F32)


def dot_t(left, right):
    return lax.dot_general(left, right, (((1,), (1,)), ((), ())), preferred_element_type=F32)


def t_dot(left, right):
    return lax.dot_general(left, right, (((0,), (0,)), ((), ())), preferred_element_type=F32)


def norm_parts(hidden):
    centre = hidden - jnp.mean(hidden, axis=-1, keepdims=True)
    spread = jnp.mean(centre * centre, axis=-1, keepdims=True)
    inverse = lax.rsqrt(spread + EPS)
    return centre * inverse, inverse


def norm_back(upstream, unit, inverse, gain):
    scaled = upstream * gain
    first = jnp.mean(scaled, axis=-1, keepdims=True)
    second = jnp.mean(scaled * unit, axis=-1, keepdims=True)
    return (scaled - first - unit * second) * inverse


def gelu_parts(values):
    below = 0.5 * (1.0 + lax.erf(values * (0.5**0.5)))
    density = jnp.exp(-0.5 * values * values) * 0.3989422804014327
    return values * below, below + values * density


def column_sum(values):
    return jnp.sum(values.astype(F32), axis=0, keepdims=True)


def ring(off):
    return lax.rem(lax.axis_index("seq") + off + 4, 4)


def ring_barrier():
    barrier = pltpu.get_barrier_semaphore()
    for off in (1, 2, 3):
        pl.semaphore_signal(
            barrier, inc=1, device_id=(lax.axis_index("chain"), ring(off)), device_id_type=MESH
        )
    pl.semaphore_wait(barrier, 3)


def push(started, src, dst, s_sem, r_sem, off):
    copy = pltpu.make_async_remote_copy(
        src_ref=src,
        dst_ref=dst,
        send_sem=s_sem,
        recv_sem=r_sem,
        device_id=(lax.axis_index("chain"), ring(off)),
        device_id_type=MESH,
    )
    copy.start()
    started.append(copy)
    return copy


def fetch(pairs, sems):
    copies = [pltpu.make_async_copy(src, dst, sems.at[i]) for i, (src, dst) in enumerate(pairs)]
    for copy in copies:
        copy.start()
    return copies


QUERY_B, VALUE_B, MIXER_B, GAIN_1, SHIFT_1, OUTER_B, GAIN_2, SHIFT_2 = range(8)


def forward_kernel(
    resets, tok, docs, init_in, offset_in, query_b, value_b, mixer_b, gain_1, shift_1, outer_b,
    gain_2, shift_2, inner_in, wq_h, wk_h, wv_h, wm_h, wi_h, wo_h,
    kv, probs, orow, ow, h1w, zw, h2w, xm, vec, inner_b,
    wq, wk, wv, wm, wi, wo, wown, vown, sbuf, lab, bias, osend, owsend, init, offset,
    w_sem, q_s, q_r, o_s, o_r, m_s, m_r, l_s, l_r,
):
    z = lax.axis_index("seq")
    fetched = fetch(
        [(wq_h, wq), (wk_h, wk), (wv_h, wv), (wm_h, wm), (wi_h, wi), (wo_h, wo)], w_sem
    )
    started = []
    vectors = (query_b, value_b, mixer_b, gain_1, shift_1, outer_b, gain_2, shift_2)
    for i, ref in enumerate(vectors):
        vec[i : i + 1, :] = ref[...].astype(F32).reshape(1, MODEL)
    inner_b[...] = inner_in[...].astype(F32).reshape(1, INNER)
    for wide, ref in ((init, init_in), (offset, offset_in)):
        wide[...] = jnp.zeros((PAD, MODEL), LOW)
        wide[0:SLOTS, :] = ref[...]
    ring_barrier()
    lab[pl.ds(z, 1)] = docs[...][None]
    label_copies = [
        push(started, docs, lab.at[z], l_s.at[d - 1], l_r.at[d - 1], d) for d in (1, 2, 3)
    ]
    tokens = tok[...].reshape(ROWS, MODEL)
    fetched[0].wait()
    queries = ((dot(tokens, wq[...]) + vec[QUERY_B : QUERY_B + 1, :]) * SCALE).astype(LOW)
    for g in range(4):
        for s in range(SEGS):
            sbuf[g, s, :, 0:GROUP] = queries[
                s * BLOCK : (s + 1) * BLOCK, g * GROUP : (g + 1) * GROUP
            ]
    fetched[1].wait()
    keys = dot(tokens, wk[...]).astype(LOW)
    for g in range(4):
        for s in range(SEGS):
            sbuf[g, s, :, GROUP : 2 * GROUP] = keys[
                s * BLOCK : (s + 1) * BLOCK, g * GROUP : (g + 1) * GROUP
            ]
    fetched[2].wait()
    values = (dot(tokens, wv[...]) + vec[VALUE_B : VALUE_B + 1, :]).astype(LOW)
    for g in range(4):
        for s in range(SEGS):
            sbuf[g, s, :, 2 * GROUP :] = values[
                s * BLOCK : (s + 1) * BLOCK, g * GROUP : (g + 1) * GROUP
            ]
    here = pl.ds(pl.multiple_of(z * BLOCK, BLOCK), BLOCK)
    row_copies = {}

    def send_rows(s):
        row_copies[s] = [
            push(
                started, sbuf.at[ring(d), s], kv.at[s, here],
                q_s.at[s, d - 1], q_r.at[s, d - 1], d,
            )
            for d in (1, 2, 3)
        ]

    send_rows(0)
    send_rows(1)
    for s in range(SEGS):
        kv[s, here, :] = sbuf[z, s]
        kv[s, TOKENS + MEMORY :, :] = jnp.zeros((KEYS - TOKENS - MEMORY, TRIPLE), LOW)
    for g in range(4):

        @pl.when(z == g)
        def _():
            cut = slice(g * GROUP, (g + 1) * GROUP)
            wown[:, 0:GROUP] = wq[:, cut]
            wown[:, GROUP : 2 * GROUP] = wk[:, cut]
            wown[:, 2 * GROUP :] = wv[:, cut]
            vown[0:1, 0:GROUP] = vec[QUERY_B : QUERY_B + 1, cut]
            vown[0:1, GROUP : 2 * GROUP] = jnp.zeros((1, GROUP), F32)
            vown[0:1, 2 * GROUP :] = vec[VALUE_B : VALUE_B + 1, cut]

    lane = lax.broadcasted_iota(jnp.int32, (1, TRIPLE), 1)
    factor = jnp.where(lane < GROUP, SCALE, 1.0)
    slot = lax.broadcasted_iota(jnp.int32, (PAD, MODEL), 0)
    key_lane = lax.broadcasted_iota(jnp.int32, (PAD, KEYS), 1)
    filled = (key_lane < TOKENS + SLOTS) | (
        (key_lane >= TOKENS + PAD) & (key_lane < TOKENS + PAD + SLOTS)
    )
    write_bias = jnp.where(filled, 0.0, HIDDEN)

    def attend(query_rows, mask, s, row_at, rows):
        parts = []
        for h in range(MINE):
            key_head = kv[s, :, GROUP + h * HEAD : GROUP + (h + 1) * HEAD]
            value_head = kv[s, :, 2 * GROUP + h * HEAD : 2 * GROUP + (h + 1) * HEAD]
            scores = dot_t(query_rows[:, h * HEAD : (h + 1) * HEAD], key_head) + mask
            weights = jnp.exp(scores - jnp.max(scores, axis=-1, keepdims=True))
            total = jnp.sum(weights, axis=-1, keepdims=True)
            prob = (weights * (1.0 / total)).astype(LOW)
            probs[s, h, pl.ds(row_at, rows), :] = prob
            parts.append(dot(prob, value_head))
        return jnp.concatenate(parts, axis=1).astype(LOW)

    memory = init[...]
    for copy in label_copies:
        copy.wait_recv()
    for s in range(SEGS):
        for i in range(4):
            column = jnp.transpose(jnp.broadcast_to(lab[i, s : s + 1, :].astype(F32), (BLOCK, BLOCK)))
            for j in range(4):
                row = jnp.broadcast_to(lab[j, s : s + 1, :].astype(F32), (BLOCK, BLOCK))
                bias[s, i * BLOCK : (i + 1) * BLOCK, j * BLOCK : (j + 1) * BLOCK] = jnp.where(
                    column == row, 0.0, HIDDEN
                )
            bias[s, i * BLOCK : (i + 1) * BLOCK, TOKENS:] = jnp.broadcast_to(
                write_bias[0:1, TOKENS:], (BLOCK, BLOCK)
            )
    out_copies = []
    for s in range(SEGS):
        written_in = (memory.astype(F32) + offset[...].astype(F32)).astype(LOW)
        xm[s, 0:PAD, :] = written_in
        xm[s, PAD:, :] = memory
        kv[s, TOKENS : TOKENS + MEMORY, :] = (
            (dot(xm[s], wown[...]) + vown[0:1, :]) * factor
        ).astype(LOW)
        for copy in row_copies[s]:
            copy.wait_recv()
        if s < SEGS - 1:
            mixed = attend(kv[s, TOKENS : TOKENS + PAD, :], write_bias, s, TOKENS, PAD)
            owsend[s] = mixed
            ow[s, pl.ds(z, 1)] = mixed[None]
            write_copies = [
                push(started, owsend.at[s], ow.at[s, z], m_s.at[s, d - 1], m_r.at[s, d - 1], d)
                for d in (1, 2, 3)
            ]
            if s == 0:
                send_rows(2)

        def block(i, carry):
            row_at = pl.multiple_of(i * BLOCK, BLOCK)
            rows = pl.ds(row_at, BLOCK)
            osend[s, i] = attend(kv[s, rows, :], bias[s, rows, :], s, row_at, BLOCK)
            return carry

        lax.fori_loop(0, 4, block, 0)
        part = slice(s * BLOCK, (s + 1) * BLOCK)
        out_copies += [
            push(
                started, osend.at[s, ring(d)], orow.at[z, part],
                o_s.at[s, d - 1], o_r.at[s, d - 1], d,
            )
            for d in (1, 2, 3)
        ]
        orow[z, part, :] = osend[s, z]
        if s < SEGS - 1:
            if s == 0:
                for copy in fetched[3:]:
                    copy.wait()
            for copy in write_copies:
                copy.wait_recv()
            hidden = xm[s, 0:PAD, :].astype(F32) + vec[MIXER_B : MIXER_B + 1, :]
            for g in range(4):
                hidden = hidden + dot(ow[s, g], wm[g * GROUP : (g + 1) * GROUP, :])
            h1w[s] = hidden
            unit, _ = norm_parts(hidden)
            upper = unit * vec[GAIN_1 : GAIN_1 + 1, :] + vec[SHIFT_1 : SHIFT_1 + 1, :]
            inner = dot(upper.astype(LOW), wi[...]) + inner_b[...]
            zw[s] = inner
            active, _ = gelu_parts(inner)
            hidden = upper + dot(active.astype(LOW), wo[...]) + vec[OUTER_B : OUTER_B + 1, :]
            h2w[s] = hidden
            unit, _ = norm_parts(hidden)
            result = unit * vec[GAIN_2 : GAIN_2 + 1, :] + vec[SHIFT_2 : SHIFT_2 + 1, :]
            flag = jnp.full((PAD, MODEL), resets[0, s], jnp.int32)
            result = jnp.where(flag > 0, init[...].astype(F32), result)
            memory = jnp.where(slot < SLOTS, result, 0.0).astype(LOW)
    for copy in out_copies:
        copy.wait_recv()
    for copy in started:
        copy.wait_send()


def shape(dims, kind=LOW):
    return jax.ShapeDtypeStruct(dims, kind)


VMEM = pl.BlockSpec(memory_space=pltpu.VMEM)
ANY = pl.BlockSpec(memory_space=pl.ANY)
DMA = pltpu.SemaphoreType.DMA


def weight_buffers():
    return [pltpu.VMEM((MODEL, MODEL), LOW) for _ in range(4)] + [
        pltpu.VMEM((MODEL, INNER), LOW),
        pltpu.VMEM((INNER, MODEL), LOW),
    ]


def forward(resets, tok, docs, init, offset, vectors, inner_b, weights):
    return pl.pallas_call(
        forward_kernel,
        out_shape=(
            shape((SEGS, KEYS, TRIPLE)),
            shape((SEGS, MINE, QUERIES, KEYS)),
            shape((4, ROWS, GROUP)),
            shape((2, 4, PAD, GROUP)),
            shape((2, PAD, MODEL), F32),
            shape((2, PAD, INNER), F32),
            shape((2, PAD, MODEL), F32),
            shape((SEGS, MEMORY, MODEL)),
            shape((8, MODEL), F32),
            shape((1, INNER), F32),
        ),
        in_specs=[pl.BlockSpec(memory_space=pltpu.SMEM)] + [VMEM] * 13 + [ANY] * 6,
        out_specs=(VMEM,) * 10,
        scratch_shapes=weight_buffers()
        + [
            pltpu.VMEM((MODEL, TRIPLE), LOW),
            pltpu.VMEM((8, TRIPLE), F32),
            pltpu.VMEM((4, SEGS, BLOCK, TRIPLE), LOW),
            pltpu.VMEM((4, SEGS, BLOCK), jnp.int32),
            pltpu.VMEM((SEGS, TOKENS, KEYS), F32),
            pltpu.VMEM((SEGS, 4, BLOCK, GROUP), LOW),
            pltpu.VMEM((2, PAD, GROUP), LOW),
            pltpu.VMEM((PAD, MODEL), LOW),
            pltpu.VMEM((PAD, MODEL), LOW),
            DMA((6,)),
            DMA((SEGS, 3)),
            DMA((SEGS, 3)),
            DMA((SEGS, 3)),
            DMA((SEGS, 3)),
            DMA((2, 3)),
            DMA((2, 3)),
            DMA((3,)),
            DMA((3,)),
        ],
        compiler_params=pltpu.CompilerParams(
            collective_id=1, has_side_effects=True, vmem_limit_bytes=60 << 20
        ),
        name="forward_attention",
    )(resets, tok, docs, init, offset, *vectors, inner_b, *weights)


HALF = 384
CHUNK = 96
SUB = 48
SIDE = 384
ORDERS = (("x", "y", "z"), ("y", "z", "x"), ("z", "x", "y"))


def places():
    chain = lax.axis_index("chain")
    return {
        "x": chain // 8,
        "y": lax.rem(chain // 2, 4),
        "z": lax.axis_index("seq"),
        "core": lax.rem(chain, 2),
    }


def peer(at, axis, off):
    at = dict(at)
    size = 2 if axis == "core" else 4
    at[axis] = lax.rem(at[axis] + off + size, size)
    return ((at["x"] * 4 + at["y"]) * 2 + at["core"], at["z"])


def greet(at, peers):
    barrier = pltpu.get_barrier_semaphore()
    for axis, off in peers:
        pl.semaphore_signal(barrier, inc=1, device_id=peer(at, axis, off), device_id_type=MESH)
    pl.semaphore_wait(barrier, len(peers))


ALL_PEERS = [("core", 1)] + [(axis, off) for axis in "xyz" for off in (1, 2, 3)]


def add_rows(out, out_start, terms, rows, step=48):
    def body(i, carry):
        base = i * step
        total = None
        for ref, start in terms:
            term = ref[pl.ds(pl.multiple_of(start + base, 16), step), :].astype(jnp.float32)
            total = term if total is None else total + term
        out[pl.ds(pl.multiple_of(out_start + base, 16), step), :] = total.astype(out.dtype)
        return carry

    lax.fori_loop(0, rows // step, body, 0)


def middle_kernel(
    tok, orow, cot, vec, inner_b, wm_h, wi_h, wo_h,
    out, ub, act, dz, df, da, dh1, dout, sums, inner_sum,
    wm, wi, wo, slope, total, unit_1, inverse_1, w_sem,
):
    fetched = fetch([(wm_h, wm), (wi_h, wi), (wo_h, wo)], w_sem)
    gain_1 = vec[GAIN_1 : GAIN_1 + 1, :]
    gain_2 = vec[GAIN_2 : GAIN_2 + 1, :]
    hidden = tok[...].reshape(ROWS, MODEL).astype(F32) + vec[MIXER_B : MIXER_B + 1, :]
    fetched[0].wait()
    for g in range(4):
        hidden = hidden + dot(orow[g], wm[g * GROUP : (g + 1) * GROUP, :])
    unit, inverse = norm_parts(hidden)
    unit_1[...] = unit
    inverse_1[...] = inverse
    upper = unit * gain_1 + vec[SHIFT_1 : SHIFT_1 + 1, :]
    ub[...] = upper.astype(LOW)
    total[...] = upper + vec[OUTER_B : OUTER_B + 1, :]
    for copy in fetched[1:]:
        copy.wait()

    def ahead(j):
        cut = pl.ds(j * MODEL, MODEL)
        inner = dot(ub[...], wi[:, cut]) + inner_b[:, cut]
        active, slant = gelu_parts(inner)
        active = active.astype(LOW)
        act[:, cut] = active
        slope[:, cut] = slant
        total[...] += dot(active, wo[cut, :])

    for j in range(INNER // MODEL):
        ahead(j)
    unit, inverse = norm_parts(total[...])
    result = unit * gain_2 + vec[SHIFT_2 : SHIFT_2 + 1, :]
    out[...] = result.astype(LOW).reshape(1, SEGS, BLOCK, MODEL)
    upstream = cot[...].reshape(ROWS, MODEL).astype(F32)
    sums[GAIN_2 : GAIN_2 + 1, :] = column_sum(upstream * unit)
    sums[SHIFT_2 : SHIFT_2 + 1, :] = column_sum(upstream)
    d_hidden = norm_back(upstream, unit, inverse, gain_2)
    total[...] = d_hidden
    d_low = d_hidden.astype(LOW)
    df[...] = d_low
    sums[OUTER_B : OUTER_B + 1, :] = column_sum(d_low)

    def back(j):
        cut = pl.ds(j * MODEL, MODEL)
        d_inner = (dot_t(df[...], wo[cut, :]) * slope[:, cut]).astype(LOW)
        dz[:, cut] = d_inner
        inner_sum[:, cut] = column_sum(d_inner)
        total[...] += dot_t(d_inner, wi[:, cut])

    for j in range(INNER // MODEL):
        back(j)
    upstream = total[...]
    unit = unit_1[...]
    sums[GAIN_1 : GAIN_1 + 1, :] = column_sum(upstream * unit)
    sums[SHIFT_1 : SHIFT_1 + 1, :] = column_sum(upstream)
    d_hidden = norm_back(upstream, unit, inverse_1[...], gain_1)
    dh1[...] = d_hidden
    d_low = d_hidden.astype(LOW)
    da[...] = d_low
    sums[MIXER_B : MIXER_B + 1, :] = column_sum(d_low)
    sums[QUERY_B : QUERY_B + 2, :] = jnp.zeros((2, MODEL), F32)
    for g in range(4):
        dout[g] = dot_t(d_low, wm[g * GROUP : (g + 1) * GROUP, :]).astype(LOW)


def middle(tok, orow, cot, vec, inner_b, weights):
    return pl.pallas_call(
        middle_kernel,
        out_shape=(
            shape((1, SEGS, BLOCK, MODEL)),
            shape((ROWS, MODEL)),
            shape((ROWS, INNER)),
            shape((ROWS, INNER)),
            shape((ROWS, MODEL)),
            shape((ROWS, MODEL)),
            shape((ROWS, MODEL), F32),
            shape((4, ROWS, GROUP)),
            shape((8, MODEL), F32),
            shape((1, INNER), F32),
        ),
        in_specs=[VMEM] * 5 + [ANY] * 3,
        out_specs=(VMEM,) * 10,
        scratch_shapes=[
            pltpu.VMEM((MODEL, MODEL), LOW),
            pltpu.VMEM((MODEL, INNER), LOW),
            pltpu.VMEM((INNER, MODEL), LOW),
            pltpu.VMEM((ROWS, INNER), F32),
            pltpu.VMEM((ROWS, MODEL), F32),
            pltpu.VMEM((ROWS, MODEL), F32),
            pltpu.VMEM((ROWS, 1), F32),
            DMA((3,)),
        ],
        compiler_params=pltpu.CompilerParams(vmem_limit_bytes=60 << 20),
        name="token_layer",
    )(tok, orow, cot, vec, inner_b, *weights[3:])


def backward_kernel(
    resets, dout, kv, probs, h1w, zw, h2w, vec,
    wq_h, wk_h, wv_h, wm_h, wi_h, wo_h,
    drow, dmem, ubw, gw, dzw, dfw, daw, small, dlast, mlast, dh1w,
    wq, wk, wv, wm, wi, wo, doh, dow, acc, dsend, msend, wide,
    w_sem, d_s, d_r, x_s, x_r, m_s, m_r,
):
    z = lax.axis_index("seq")
    fetched = fetch(
        [(wq_h, wq), (wk_h, wk), (wv_h, wv), (wm_h, wm), (wi_h, wi), (wo_h, wo)], w_sem
    )
    started = []
    ring_barrier()
    here = pl.ds(pl.multiple_of(z * BLOCK, BLOCK), BLOCK)
    in_copies = {}
    for s in reversed(range(SEGS)):
        part = slice(s * BLOCK, (s + 1) * BLOCK)
        in_copies[s] = [
            push(
                started, dout.at[ring(d), part], doh.at[s, here],
                d_s.at[s, d - 1], d_r.at[s, d - 1], d,
            )
            for d in (1, 2, 3)
        ]
        doh[s, here, :] = dout[z, part, :]
    gain_1 = vec[GAIN_1 : GAIN_1 + 1, :]
    gain_2 = vec[GAIN_2 : GAIN_2 + 1, :]

    def head_back(s, h, d_rows, rows):
        cut = slice(h * HEAD, (h + 1) * HEAD)
        key_head = kv[s, :, GROUP + h * HEAD : GROUP + (h + 1) * HEAD]
        value_head = kv[s, :, 2 * GROUP + h * HEAD : 2 * GROUP + (h + 1) * HEAD]
        d_head = d_rows[:, cut]
        prob = probs[s, h, rows, :]
        wide_prob = prob.astype(F32)
        product = wide_prob * dot_t(d_head, value_head)
        delta = jnp.sum(product, axis=-1, keepdims=True)
        d_scores = (product - wide_prob * delta).astype(LOW)
        d_query = (dot(d_scores, key_head) * SCALE).astype(LOW)
        d_key = t_dot(d_scores, kv[s, rows, cut])
        d_value = t_dot(prob, d_head)
        return d_query, d_key, d_value

    def tokens_back(s):
        for copy in in_copies[s]:
            copy.wait_recv()
        rows = slice(0, TOKENS)
        for h in range(MINE):
            cut = slice(h * HEAD, (h + 1) * HEAD)
            d_query, d_key, d_value = head_back(s, h, doh[s], rows)
            dsend[s, :, cut] = d_query
            acc[s, :, cut] = d_key
            acc[s, :, GROUP + h * HEAD : GROUP + (h + 1) * HEAD] = d_value

    def writes_back(s):
        rows = slice(TOKENS, TOKENS + PAD)
        for h in range(MINE):
            cut = slice(h * HEAD, (h + 1) * HEAD)
            d_query, d_key, d_value = head_back(s, h, dow[...], rows)
            msend[s, 0:PAD, cut] = d_query
            acc[s, :, cut] += d_key
            acc[s, :, GROUP + h * HEAD : GROUP + (h + 1) * HEAD] += d_value

    mem_copies = {}
    row_copies = []

    def finish(s):
        if s == SEGS - 1:
            msend[s, :, 0:GROUP] = jnp.zeros((MEMORY, GROUP), LOW)
        else:
            msend[s, PAD:, 0:GROUP] = jnp.zeros((PAD, GROUP), LOW)
        msend[s, :, GROUP:] = acc[s, TOKENS : TOKENS + MEMORY, :].astype(LOW)
        mem_copies[s] = [
            push(started, msend.at[s], dmem.at[s - 1, z], m_s.at[s, d - 1], m_r.at[s, d - 1], d)
            for d in (1, 2, 3)
        ]
        dmem[s - 1, z] = msend[s]
        dsend[s, :, GROUP:] = acc[s, 0:TOKENS, :].astype(LOW)
        kept = slice((s - 1) * BLOCK, s * BLOCK)
        for d in (1, 2, 3):
            there = pl.ds(pl.multiple_of(ring(d) * BLOCK, BLOCK), BLOCK)
            row_copies.append(
                push(
                    started, dsend.at[s, there], drow.at[z, kept],
                    x_s.at[s, d - 1], x_r.at[s, d - 1], d,
                )
            )
        drow[z, kept, :] = dsend[s, here, :]

    sums = {}

    def add(name, value):
        sums[name] = value if name not in sums else sums[name] + value

    saved = {}

    def memory_back(s):
        for copy in mem_copies[s]:
            copy.wait_recv()
        for g in range(4):
            for t in range(3):
                wide[t, :, g * GROUP : (g + 1) * GROUP] = dmem[
                    s - 1, g, :, t * GROUP : (t + 1) * GROUP
                ]
        if s == SEGS - 1:
            for copy in fetched:
                copy.wait()
        d_rows = dot_t(wide[0], wq[...]) + dot_t(wide[1], wk[...]) + dot_t(wide[2], wv[...])
        write = d_rows[0:PAD]
        if s < SEGS - 1:
            write = write + saved[s]
        grad = write + d_rows[PAD:]
        add("offset", write)
        add("norm", jnp.sum(jnp.sum(grad * grad, axis=0, keepdims=True), axis=1, keepdims=True))
        flag = jnp.full((PAD, MODEL), resets[0, s - 1], jnp.int32) > 0
        add("init", jnp.where(flag, grad, 0.0))
        return jnp.where(flag, 0.0, grad)

    def layer_back(s, upstream):
        unit, inverse = norm_parts(h2w[s])
        add("gain_2", column_sum(upstream * unit))
        add("shift_2", column_sum(upstream))
        d_second = norm_back(upstream, unit, inverse, gain_2)
        d_low = d_second.astype(LOW)
        dfw[s] = d_low
        add("outer", column_sum(d_low))
        active, slant = gelu_parts(zw[s])
        gw[s] = active.astype(LOW)
        d_inner = (dot_t(d_low, wo[...]) * slant).astype(LOW)
        dzw[s] = d_inner
        add("inner", column_sum(d_inner))
        unit, inverse = norm_parts(h1w[s])
        ubw[s] = (unit * gain_1 + vec[SHIFT_1 : SHIFT_1 + 1, :]).astype(LOW)
        d_upper = dot_t(d_inner, wi[...]) + d_second
        add("gain_1", column_sum(d_upper * unit))
        add("shift_1", column_sum(d_upper))
        d_first = norm_back(d_upper, unit, inverse, gain_1)
        saved[s] = d_first
        if s == 0:
            dh1w[...] = d_first
        d_low = d_first.astype(LOW)
        daw[s] = d_low
        add("mixer", column_sum(d_low))
        own = pl.ds(pl.multiple_of(z * GROUP, HEAD), GROUP)
        dow[...] = dot_t(d_low, wm[own, :]).astype(LOW)

    tokens_back(2)
    finish(2)
    tokens_back(1)
    layer_back(1, memory_back(2))
    writes_back(1)
    finish(1)
    tokens_back(0)
    layer_back(0, memory_back(1))
    writes_back(0)
    msend[0, PAD:, 0:GROUP] = jnp.zeros((PAD, GROUP), LOW)
    msend[0, :, GROUP:] = acc[0, TOKENS : TOKENS + MEMORY, :].astype(LOW)
    dsend[0, :, GROUP:] = acc[0, 0:TOKENS, :].astype(LOW)
    dlast[...] = dsend[0]
    mlast[...] = msend[0]
    quarter = 0.25
    row = lax.broadcasted_iota(jnp.int32, (24, MODEL), 0)
    zero = jnp.zeros((1, MODEL), F32)
    small[0:8, :] = quarter * jnp.concatenate(
        [zero, zero]
        + [sums[n] for n in ("mixer", "gain_1", "shift_1", "outer", "gain_2", "shift_2")],
        axis=0,
    )
    small[8:16, :] = quarter * jnp.concatenate(
        [sums["inner"][:, i * MODEL : (i + 1) * MODEL] for i in range(4)] + [zero] * 4, axis=0
    )
    small[16:40, :] = quarter * sums["init"][0:24]
    small[40:64, :] = quarter * (
        sums["offset"][0:24]
        + jnp.where(row >= SLOTS, jnp.broadcast_to(sums["norm"], (24, MODEL)), 0.0)
    )
    for copy in row_copies:
        copy.wait_recv()
    for copy in started:
        copy.wait_send()


def backward(resets, dout, kv, probs, h1w, zw, h2w, vec, weights):
    return pl.pallas_call(
        backward_kernel,
        out_shape=(
            shape((4, ROWS - BLOCK, TRIPLE)),
            shape((SEGS - 1, 4, MEMORY, TRIPLE)),
            shape((2, PAD, MODEL)),
            shape((2, PAD, INNER)),
            shape((2, PAD, INNER)),
            shape((2, PAD, MODEL)),
            shape((2, PAD, MODEL)),
            shape((64, MODEL), F32),
            shape((TOKENS, TRIPLE)),
            shape((MEMORY, TRIPLE)),
            shape((PAD, MODEL), F32),
        ),
        in_specs=[pl.BlockSpec(memory_space=pltpu.SMEM)] + [VMEM] * 7 + [ANY] * 6,
        out_specs=(VMEM,) * 11,
        scratch_shapes=weight_buffers()
        + [
            pltpu.VMEM((SEGS, TOKENS, GROUP), LOW),
            pltpu.VMEM((PAD, GROUP), LOW),
            pltpu.VMEM((SEGS, KEYS, 2 * GROUP), F32),
            pltpu.VMEM((SEGS, TOKENS, TRIPLE), LOW),
            pltpu.VMEM((SEGS, MEMORY, TRIPLE), LOW),
            pltpu.VMEM((3, MEMORY, MODEL), LOW),
            DMA((6,)),
            DMA((SEGS, 3)),
            DMA((SEGS, 3)),
            DMA((SEGS, 3)),
            DMA((SEGS, 3)),
            DMA((SEGS, 3)),
            DMA((SEGS, 3)),
        ],
        compiler_params=pltpu.CompilerParams(
            collective_id=2, has_side_effects=True, vmem_limit_bytes=60 << 20
        ),
        name="backward_attention",
    )(resets, dout, kv, probs, h1w, zw, h2w, vec, *weights)


FULL = ROWS + MEMORY
MOST = ROWS + PAD
UNITS = ((4, 5, 6), (7, 8, 9), (0, 1, 2), (10, 11, 3))


def finish_kernel(
    tok, xm, drow, dmem, orow, ow, dh1, sums, inner_sum, small, ubw, gw, dzw, dfw, daw, dsend, msend, dh1w,
    ub_h, act_h, dz_h, df_h, da_h, wq_h, wk_h, wv_h,
    packed, input_grad, ext,
    ub, act, dz, df, da, wq, wk, wv, rows, triple, mixed,
    drow0, dmall, wide, g, crecv, r1, r2, r3, slots, own_ext, ecore, ex, ey, ez,
    w_sem, x_s, x_r, m_s, m_r, c_s, c_r, a_s, a_r, b_s, b_r, d_s, d_r, e_s, e_r, f_s, f_r,
    loc, free, n_s, n_r, o_s, o_r, gc_s, gc_r, t_s, t_r,
):
    at = places()
    z = at["z"]
    core = at["core"]
    top = pl.ds(0, ROWS)
    fetched = fetch(
        [
            (ub_h, ub.at[top]), (dz_h, dz.at[top]), (act_h, act.at[top]), (df_h, df.at[top]), (da_h, da.at[top]),
            (wq_h, wq), (wk_h, wk), (wv_h, wv),
        ],
        w_sem,
    )
    started = []

    def send(src, dst, s_sem, r_sem, axis, off):
        copy = pltpu.make_async_remote_copy(
            src_ref=src, dst_ref=dst, send_sem=s_sem, recv_sem=r_sem,
            device_id=peer(at, axis, off), device_id_type=MESH,
        )
        copy.start()
        started.append(copy)
        return copy

    def turn(value, off):
        return lax.rem(value + off + 4, 4)

    def ds(start, size):
        return pl.ds(pl.multiple_of(start, 16), size)

    place1 = [at[order[0]] for order in ORDERS]
    place2 = [at[order[1]] for order in ORDERS]
    place3 = [at[order[2]] for order in ORDERS]
    live = {}

    def sub_of(ref, start, n):
        side = pl.ds(pl.multiple_of(lax.rem(n, 2) * SIDE, 128), SIDE)
        return ref.at[ds(start + (n // 2) * SUB, SUB), side]

    def home(p, off):
        return core * HALF + turn(place1[p], off) * CHUNK

    def block_done(u, p):
        b = UNITS[u][p]
        live["core", u, p] = send(
            g.at[b, ds((1 - core) * HALF, HALF)], crecv.at[u, p],
            c_s.at[u, p], c_r.at[u, p], "core", 1,
        )
        started.pop()

    def stage1(u):
        for p in range(3):
            b = UNITS[u][p]
            live["core", u, p].wait_recv()
            held = crecv.at[u, p]
            start = turn(place1[p], 2) * CHUNK
            add_rows(held, start, [(g.at[b], core * HALF + start), (held, start)], CHUNK)
            live["a", u, p] = [
                send(
                    held.at[ds(start + i * SUB, SUB)], r1.at[u, p, i],
                    a_s.at[u, p, i], a_r.at[u, p, i], ORDERS[p][0], 1 + 2 * i,
                )
                for i in range(2)
            ]
        for p in range(3):
            b = UNITS[u][p]
            held = crecv.at[u, p]
            for off in (1, 3, 0):
                start = turn(place1[p], off) * CHUNK
                add_rows(held, start, [(g.at[b], core * HALF + start), (held, start)], CHUNK)
            live["core", u, p].wait_send()
        pl.semaphore_signal(
            free.at[u], inc=1, device_id=peer(at, "core", 1), device_id_type=MESH
        )

    def stage2(u):
        for p in range(3):
            held = crecv.at[u, p]
            live["b", u, p] = []
            for i in range(2):
                start = turn(place1[p], 1 + 2 * i) * CHUNK
                live["a", u, p][i].wait_recv()
                half = start + i * SUB
                add_rows(held, half, [(held, half), (r1.at[u, p, i], 0)], SUB)
                live["b", u, p].append(
                    send(
                        held.at[ds(start, CHUNK)], r2.at[u, p, i],
                        b_s.at[u, p, i], b_r.at[u, p, i], ORDERS[p][0], 1 + 2 * i,
                    )
                )

    def stage3(u):
        for p in range(3):
            held = crecv.at[u, p]
            start = place1[p] * CHUNK
            for copy in live["b", u, p]:
                copy.wait_recv()
            add_rows(held, start, [(held, start), (r2.at[u, p, 0], 0), (r2.at[u, p, 1], 0)], CHUNK)
            live["d", u, p] = [
                send(
                    sub_of(held, start, turn(place2[p], d)), r3.at[u, p, d - 1],
                    d_s.at[u, p, d - 1], d_r.at[u, p, d - 1], ORDERS[p][1], d,
                )
                for d in (1, 2, 3)
            ]

    def stage4(u):
        for p in range(3):
            for copy in live["d", u, p]:
                copy.wait_recv()
            total = sub_of(crecv.at[u, p], place1[p] * CHUNK, place2[p])[...].astype(F32)
            for d in range(3):
                total = total + r3[u, p, d].astype(F32)
            slots[u, p, pl.ds(place3[p], 1)] = total.astype(LOW)[None]
            live["e", u, p] = [
                send(
                    slots.at[u, p, place3[p]], slots.at[u, p, place3[p]],
                    e_s.at[u, p, d - 1], e_r.at[u, p, d - 1], ORDERS[p][2], d,
                )
                for d in (1, 2, 3)
            ]

    def stage5(u):
        for p in range(3):
            for copy in live["e", u, p]:
                copy.wait_recv()
            total = slots[u, p, 0].astype(F32)
            for i in range(1, 4):
                total = total + slots[u, p, i].astype(F32)
            target = sub_of(g.at[UNITS[u][p]], home(p, 0), place2[p])
            target[...] = total.astype(LOW)
            live["f", u, p] = [
                send(target, target, f_s.at[u, p, d - 1], f_r.at[u, p, d - 1], ORDERS[p][1], d)
                for d in (1, 2, 3)
            ]

    def across(u, p, j, start, count):
        piece = g.at[UNITS[u][p], ds(start, count)]
        live["gc", u, p, j] = send(piece, piece, gc_s.at[u, p, j], gc_r.at[u, p, j], "core", 1)

    def stage6(u):
        pl.semaphore_wait(free.at[u], 1)
        for p in range(3):
            for copy in live["f", u, p]:
                copy.wait_recv()
            piece = g.at[UNITS[u][p], ds(home(p, 0), CHUNK)]
            live["n", u, p] = [
                send(piece, piece, n_s.at[u, p, i], n_r.at[u, p, i], ORDERS[p][0], 1 + 2 * i)
                for i in range(2)
            ]
            across(u, p, 0, home(p, 0), CHUNK)

    def stage7(u):
        for p in range(3):
            live["o", u, p] = []
            for i in range(2):
                live["n", u, p][i].wait_recv()
                start = home(p, 3 - 2 * i)
                piece = g.at[UNITS[u][p], ds(start + i * SUB, SUB)]
                live["o", u, p].append(
                    send(piece, piece, o_s.at[u, p, i], o_r.at[u, p, i], ORDERS[p][0], 1 + 2 * i)
                )
                across(u, p, 1 + i, start, CHUNK)

    def stage8(u):
        for p in range(3):
            for i in range(2):
                live["o", u, p][i].wait_recv()
                across(u, p, 3 + i, home(p, 2) + i * SUB, SUB)

    stores = []

    def stage9(u):
        for p in range(3):
            for j in range(5):
                live["gc", u, p, j].wait_recv()
            b = UNITS[u][p]
            stores.append(
                pltpu.make_async_copy(
                    g.at[b], packed.at[pl.ds(b * MODEL, MODEL)], loc.at[u, p]
                )
            )
            stores[-1].start()

    stages = {
        1: stage1, 2: stage2, 3: stage3, 4: stage4, 5: stage5, 6: stage6, 7: stage7, 8: stage8,
        9: stage9,
    }

    def wave(*pairs):
        for u, k in pairs:
            stages[k](u)

    low_at = jnp.minimum(z, 1)
    low_keep = (z < 2).astype(F32).astype(LOW)
    at_seg = jnp.minimum(z, 2)
    keep = (z < SEGS).astype(F32).astype(LOW)

    def inner_block(j):
        g[4 + j] = t_dot(ub[...], dz[:, j * MODEL : (j + 1) * MODEL]).astype(LOW)

    def outer_block(j):
        g[8 + j] = t_dot(act[:, j * MODEL : (j + 1) * MODEL], df[...]).astype(LOW)

    def mixer_block():
        for i in range(4):
            mixed[i, 0:ROWS, :] = orow[i]
            mixed[i, ROWS:, :] = ow[low_at, i]
        for i in range(4):
            g[3, i * GROUP : (i + 1) * GROUP, :] = t_dot(mixed[i], da[...]).astype(LOW)

    greet(at, ALL_PEERS)
    row_copies = []
    for d in (1, 2, 3):
        there = ds(ring(d) * BLOCK, BLOCK)
        row_copies.append(
            send(dsend.at[there], drow0.at[z], x_s.at[d - 1], x_r.at[d - 1], "z", d)
        )
        row_copies.append(
            send(msend, dmall.at[0, z], m_s.at[d - 1], m_r.at[d - 1], "z", d)
        )
    drow0[z] = dsend[ds(z * BLOCK, BLOCK), :]
    dmall[0, z] = msend[...]
    dmall[1:] = dmem[...]
    ub[ROWS:, :] = ubw[low_at]
    act[ROWS:, :] = gw[low_at]
    dz[ROWS:, :] = dzw[low_at] * low_keep
    df[ROWS:, :] = dfw[low_at] * low_keep
    da[ROWS:, :] = daw[low_at] * low_keep
    for copy in fetched[:2]:
        copy.wait()
    for j in range(3):
        inner_block(j)
        block_done(0, j)
    inner_block(3)
    block_done(1, 0)
    wave((0, 1))
    for copy in fetched[2:4]:
        copy.wait()
    for j in range(2):
        outer_block(j)
        block_done(1, 1 + j)
    wave((0, 2), (1, 1))
    rows[0:ROWS, :] = tok[...].reshape(ROWS, MODEL)
    rows[ROWS:, :] = xm[at_seg]
    for copy in row_copies:
        copy.wait_recv()
    for i in range(4):
        for t in range(3):
            cut = slice(i * GROUP, (i + 1) * GROUP)
            part = slice(t * GROUP, (t + 1) * GROUP)
            triple[t, 0:BLOCK, cut] = drow0[i, :, part]
            triple[t, BLOCK:ROWS, cut] = drow[i, :, part]
            triple[t, ROWS:, cut] = dmall[at_seg, i, :, part] * keep
            wide[t, :, cut] = dmall[0, i, :, part]
    for t in range(3):
        g[t] = t_dot(rows[...], triple[t]).astype(LOW)
        block_done(2, t)
    wave((0, 3), (1, 2), (2, 1))
    for j in range(2, 4):
        outer_block(j)
        block_done(3, j - 2)
    fetched[4].wait()
    mixer_block()
    block_done(3, 2)
    wave((0, 4), (1, 3), (2, 2), (3, 1))
    for copy in fetched[5:]:
        copy.wait()
    d_rows = dot_t(wide[0], wq[...]) + dot_t(wide[1], wk[...]) + dot_t(wide[2], wv[...])
    write = d_rows[0:PAD] + dh1w[...]
    grad = write + d_rows[PAD:]
    norm = jnp.sum(jnp.sum(grad * grad, axis=0, keepdims=True), axis=1, keepdims=True)
    own_ext[0:8, :] = small[0:8, :] + sums[...]
    own_ext[8:16, :] = small[8:16, :] + jnp.concatenate(
        [inner_sum[:, i * MODEL : (i + 1) * MODEL] for i in range(4)]
        + [jnp.zeros((4, MODEL), F32)],
        axis=0,
    )
    own_ext[QUERY_B : QUERY_B + 1, :] += column_sum(triple[0])
    own_ext[VALUE_B : VALUE_B + 1, :] += column_sum(triple[2])
    row = lax.broadcasted_iota(jnp.int32, (24, MODEL), 0)
    own_ext[16:40, :] = small[16:40, :] + 0.25 * grad[0:24]
    own_ext[40:64, :] = small[40:64, :] + 0.25 * (
        write[0:24] + jnp.where(row >= SLOTS, jnp.broadcast_to(norm, (24, MODEL)), 0.0)
    )
    half = pl.ds(pl.multiple_of(core * 32, 8), 32)
    other = pl.ds(pl.multiple_of((1 - core) * 32, 8), 32)
    small_core = send(own_ext.at[other], ecore, t_s.at[0], t_r.at[0], "core", 1)
    wave((0, 5), (1, 4), (2, 3), (3, 2))
    small_core.wait_recv()
    ecore[...] = own_ext[half, :] + ecore[...]
    small_x = [
        send(
            ecore.at[pl.ds(pl.multiple_of(turn(at["x"], d) * 8, 8), 8)],
            ex.at[d - 1], t_s.at[d], t_r.at[d], "x", d,
        )
        for d in (1, 2, 3)
    ]
    input_grad[...] = (
        dh1[...]
        + dot_t(triple[0, 0:ROWS, :], wq[...])
        + dot_t(triple[1, 0:ROWS, :], wk[...])
        + dot_t(triple[2, 0:ROWS, :], wv[...])
    ).reshape(1, SEGS, BLOCK, MODEL)
    wave((0, 6), (1, 5), (2, 4), (3, 3))
    for copy in small_x:
        copy.wait_recv()
    ey[pl.ds(at["y"], 1)] = (
        ecore[pl.ds(pl.multiple_of(at["x"] * 8, 8), 8), :] + ex[0] + ex[1] + ex[2]
    )[None]
    small_y = [
        send(ey.at[at["y"]], ey.at[at["y"]], t_s.at[3 + d], t_r.at[3 + d], "y", d)
        for d in (1, 2, 3)
    ]
    wave((0, 7), (1, 6), (2, 5), (3, 4))
    for copy in small_y:
        copy.wait_recv()
    ez[pl.ds(at["z"], 1)] = (ey[0] + ey[1] + ey[2] + ey[3])[None]
    small_z = [
        send(ez.at[at["z"]], ez.at[at["z"]], t_s.at[6 + d], t_r.at[6 + d], "z", d)
        for d in (1, 2, 3)
    ]
    wave((0, 8), (1, 7), (2, 6), (3, 5))
    for copy in small_z:
        copy.wait_recv()
    mine = pl.ds(pl.multiple_of(core * 32 + at["x"] * 8, 8), 8)
    ext[mine, :] = ez[0] + ez[1] + ez[2] + ez[3]
    small_back = [
        send(ext.at[mine], ext.at[mine], t_s.at[9 + d], t_r.at[9 + d], "x", d) for d in (1, 2, 3)
    ]
    wave((1, 8), (2, 7), (3, 6), (0, 9))
    for copy in small_back:
        copy.wait_recv()
    small_last = send(ext.at[half], ext.at[half], t_s.at[13], t_r.at[13], "core", 1)
    wave((2, 8), (3, 7), (1, 9), (3, 8), (2, 9))
    small_last.wait_recv()
    wave((3, 9))
    for copy in started:
        copy.wait_send()
    for copy in stores:
        copy.wait()


def finish_all(near, far):
    def buffer(*dims):
        return pltpu.VMEM(dims, LOW)

    def wide_buffer(*dims):
        return pltpu.VMEM(dims, F32)

    pairs = [
        (3,), (3,), (4, 3), (4, 3, 2), (4, 3, 2), (4, 3, 3), (4, 3, 3), (4, 3, 3), None,
        (4, 3, 2), (4, 3, 2), (4, 3, 5), (14,),
    ]
    sems = [DMA((8,))]
    for dims in pairs:
        if dims is None:
            sems += [DMA((4, 3)), pltpu.SemaphoreType.REGULAR((4,))]
        else:
            sems += [DMA(dims), DMA(dims)]
    return pl.pallas_call(
        finish_kernel,
        out_shape=(
            shape((12 * MODEL, MODEL)),
            shape((1, SEGS, BLOCK, MODEL), F32),
            shape((64, MODEL), F32),
        ),
        in_specs=[VMEM] * len(near) + [ANY] * len(far),
        out_specs=(ANY, VMEM, VMEM),
        scratch_shapes=[
            buffer(MOST, MODEL),
            buffer(MOST, INNER),
            buffer(MOST, INNER),
            buffer(MOST, MODEL),
            buffer(MOST, MODEL),
            buffer(MODEL, MODEL),
            buffer(MODEL, MODEL),
            buffer(MODEL, MODEL),
            buffer(FULL, MODEL),
            buffer(3, FULL, MODEL),
            buffer(4, MOST, GROUP),
            buffer(4, BLOCK, TRIPLE),
            buffer(SEGS, 4, MEMORY, TRIPLE),
            buffer(3, MEMORY, MODEL),
            buffer(12, MODEL, MODEL),
            buffer(4, 3, HALF, MODEL),
            buffer(4, 3, 2, SUB, MODEL),
            buffer(4, 3, 2, CHUNK, MODEL),
            buffer(4, 3, 3, SUB, SIDE),
            buffer(4, 3, 4, SUB, SIDE),
            wide_buffer(64, MODEL),
            wide_buffer(32, MODEL),
            wide_buffer(3, 8, MODEL),
            wide_buffer(4, 8, MODEL),
            wide_buffer(4, 8, MODEL),
        ]
        + sems,
        compiler_params=pltpu.CompilerParams(
            collective_id=3, has_side_effects=True, vmem_limit_bytes=62 << 20
        ),
        name="weights_and_sums",
    )(*near, *far)


def widen_kernel(
    count, packed, ext, grad_in,
    grad_out, query_w, key_w, value_w, mixer_w, inner_w, outer_w, query_b, value_b, mixer_b, gain_1, shift_1,
    inner_b, outer_b, gain_2, shift_2, init, offset, norm,
    low, wide, in_sem, out_sem,
):
    through = pltpu.make_async_copy(grad_in, grad_out, in_sem.at[12])
    through.start()
    def rows(i):
        return pl.ds(i * MODEL, MODEL)

    loads = [pltpu.make_async_copy(packed.at[rows(i)], low.at[i], in_sem.at[i]) for i in range(12)]
    for copy in loads:
        copy.start()
    targets = [query_w, key_w, value_w, mixer_w]
    targets += [inner_w.at[:, rows(i)] for i in range(4)]
    targets += [outer_w.at[rows(i)] for i in range(4)]
    stores = []
    for i in range(12):
        loads[i].wait()

        def body(j, carry):
            part = pl.ds(pl.multiple_of(j * 96, 96), 96)
            wide[i, part, :] = low[i, part, :].astype(F32)
            return carry

        lax.fori_loop(0, 8, body, 0)
        stores.append(pltpu.make_async_copy(wide.at[i], targets[i], out_sem.at[i]))
        stores[-1].start()
    singles = (
        (query_b, QUERY_B), (value_b, VALUE_B), (mixer_b, MIXER_B), (gain_1, GAIN_1),
        (shift_1, SHIFT_1), (outer_b, OUTER_B), (gain_2, GAIN_2), (shift_2, SHIFT_2),
    )
    for ref, row in singles:
        ref[...] = ext[row : row + 1, :].reshape(MODEL)
    inner_b[...] = jnp.concatenate([ext[8 + i : 9 + i, :] for i in range(4)], axis=1).reshape(INNER)
    init[...] = ext[16 : 16 + SLOTS, :]
    offset[...] = ext[40 : 40 + SLOTS, :]
    norm[...] = jnp.sqrt(ext[60:61, 0:1] * (1.0 / count))
    for copy in stores:
        copy.wait()
    through.wait()


def widen(packed, ext, input_grad, chains):
    square = shape((MODEL, MODEL), F32)
    line = shape((MODEL,), F32)
    slots = shape((SLOTS, MODEL), F32)
    return pl.pallas_call(
        functools.partial(widen_kernel, chains * SEGS * SLOTS * MODEL),
        out_shape=(
            shape((1, SEGS, BLOCK, MODEL), F32), square, square, square, square, shape((MODEL, INNER), F32), shape((INNER, MODEL), F32),
            line, line, line, line, line, shape((INNER,), F32), line, line, line, slots, slots,
            shape((1, 1), F32),
        ),
        in_specs=[ANY, VMEM, VMEM],
        out_specs=(ANY,) * 7 + (VMEM,) * 12,
        scratch_shapes=[
            pltpu.VMEM((12, MODEL, MODEL), LOW),
            pltpu.VMEM((12, MODEL, MODEL), F32),
            DMA((13,)),
            DMA((12,)),
        ],
        compiler_params=pltpu.CompilerParams(vmem_limit_bytes=60 << 20),
        name="widen",
    )(packed, ext, input_grad)


def shards(
    tokens, documents, resets, cotangent, query_weight, query_bias, key_weight, value_weight,
    value_bias, mixer_weight, mixer_bias, first_gain, first_shift, inner_weight, inner_bias,
    outer_weight, outer_bias, second_gain, second_shift, memory_init, write_offset,
):
    weights = (query_weight, key_weight, value_weight, mixer_weight, inner_weight, outer_weight)
    vectors = (
        query_bias, value_bias, mixer_bias, first_gain, first_shift, outer_bias, second_gain,
        second_shift,
    )
    tok = tokens[0]
    kv, probs, orow, ow, h1w, zw, h2w, xm, vec, inner_b = forward(
        resets, tok, documents[0], memory_init, write_offset, vectors, inner_bias, weights
    )
    layer_output, ub, act, dz, df, da, dh1, dout, sums, inner_sum = middle(
        tok, orow, cotangent[0], vec, inner_b, weights
    )
    drow, dmem, ubw, gw, dzw, dfw, daw, small, dlast, mlast, dh1w = backward(
        resets, dout, kv, probs, h1w, zw, h2w, vec, weights
    )
    packed, input_grad, ext = finish_all(
        (
            tok, xm, drow, dmem, orow, ow, dh1, sums, inner_sum, small, ubw, gw, dzw, dfw, daw,
            dlast, mlast, dh1w,
        ),
        (ub, act, dz, df, da) + weights[:3],
    )
    (
        input_grad, query_w, key_w, value_w, mixer_w, inner_w, outer_w, query_b, value_b, mixer_b, gain_1,
        shift_1, inner_b, outer_b, gain_2, shift_2, init, offset, memory_norm,
    ) = widen(packed, ext, input_grad, lax.axis_size("chain"))
    return (
        layer_output, input_grad, query_w, query_b, key_w, value_w, value_b, mixer_w, mixer_b,
        gain_1, shift_1, inner_w, inner_b, outer_w, outer_b, gain_2, shift_2, init, offset,
        memory_norm.reshape(()),
    )


def solution(mesh):
    tokens = P("chain", None, "seq", None)
    in_specs = (tokens, P("chain", None, "seq"), P("chain", None), tokens) + (P(),) * 17
    out_specs = (tokens, tokens) + (P(),) * 18
    return jax.shard_map(shards, mesh=mesh, in_specs=in_specs, out_specs=out_specs, check_vma=False)
```

```python
import functools

import jax
import jax.numpy as jnp
from jax import lax
from jax.experimental import pallas as pl
from jax.experimental.pallas import tpu as pltpu
from jax.sharding import PartitionSpec as P

MESH = pl.DeviceIdType.MESH
LOW = jnp.bfloat16
F32 = jnp.float32
SEGS = 3
BLOCK = 128
MODEL = 768
INNER = 3072
SLOTS = 20
PAD = 32
MEMORY = 2 * PAD
ROWS = SEGS * BLOCK
TOKENS = 512
KEYS = 640
QUERIES = TOKENS + PAD
HEAD = 64
MINE = 3
GROUP = MINE * HEAD
TRIPLE = 3 * GROUP
SCALE = HEAD ** (-0.5)
EPS = 1e-12
HIDDEN = -1e30


def dot(left, right):
    return jnp.dot(left, right, preferred_element_type=F32)


def dot_t(left, right):
    return lax.dot_general(left, right, (((1,), (1,)), ((), ())), preferred_element_type=F32)


def t_dot(left, right):
    return lax.dot_general(left, right, (((0,), (0,)), ((), ())), preferred_element_type=F32)


def norm_parts(hidden):
    centre = hidden - jnp.mean(hidden, axis=-1, keepdims=True)
    spread = jnp.mean(centre * centre, axis=-1, keepdims=True)
    inverse = lax.rsqrt(spread + EPS)
    return centre * inverse, inverse


def norm_back(upstream, unit, inverse, gain):
    scaled = upstream * gain
    first = jnp.mean(scaled, axis=-1, keepdims=True)
    second = jnp.mean(scaled * unit, axis=-1, keepdims=True)
    return (scaled - first - unit * second) * inverse


def gelu_parts(values):
    below = 0.5 * (1.0 + lax.erf(values * (0.5**0.5)))
    density = jnp.exp(-0.5 * values * values) * 0.3989422804014327
    return values * below, below + values * density


def column_sum(values):
    return jnp.sum(values.astype(F32), axis=0, keepdims=True)


def ring(off):
    return lax.rem(lax.axis_index("seq") + off + 4, 4)


def ring_barrier():
    barrier = pltpu.get_barrier_semaphore()
    for off in (1, 2, 3):
        pl.semaphore_signal(
            barrier, inc=1, device_id=(lax.axis_index("chain"), ring(off)), device_id_type=MESH
        )
    pl.semaphore_wait(barrier, 3)


def push(started, src, dst, s_sem, r_sem, off):
    copy = pltpu.make_async_remote_copy(
        src_ref=src,
        dst_ref=dst,
        send_sem=s_sem,
        recv_sem=r_sem,
        device_id=(lax.axis_index("chain"), ring(off)),
        device_id_type=MESH,
    )
    copy.start()
    started.append(copy)
    return copy


def fetch(pairs, sems):
    copies = [pltpu.make_async_copy(src, dst, sems.at[i]) for i, (src, dst) in enumerate(pairs)]
    for copy in copies:
        copy.start()
    return copies


QUERY_B, VALUE_B, MIXER_B, GAIN_1, SHIFT_1, OUTER_B, GAIN_2, SHIFT_2 = range(8)


def shape(dims, kind=LOW):
    return jax.ShapeDtypeStruct(dims, kind)


VMEM = pl.BlockSpec(memory_space=pltpu.VMEM)
ANY = pl.BlockSpec(memory_space=pl.ANY)
DMA = pltpu.SemaphoreType.DMA


def weight_buffers():
    return [pltpu.VMEM((MODEL, MODEL), LOW) for _ in range(4)] + [
        pltpu.VMEM((MODEL, INNER), LOW),
        pltpu.VMEM((INNER, MODEL), LOW),
    ]


HALF = 384
CHUNK = 96
SUB = 48
SIDE = 384
ORDERS = (("x", "y", "z"), ("y", "z", "x"), ("z", "x", "y"))


def places():
    chain = lax.axis_index("chain")
    return {
        "x": chain // 8,
        "y": lax.rem(chain // 2, 4),
        "z": lax.axis_index("seq"),
        "core": lax.rem(chain, 2),
    }


def peer(at, axis, off):
    at = dict(at)
    size = 2 if axis == "core" else 4
    at[axis] = lax.rem(at[axis] + off + size, size)
    return ((at["x"] * 4 + at["y"]) * 2 + at["core"], at["z"])


def greet(at, peers):
    barrier = pltpu.get_barrier_semaphore()
    for axis, off in peers:
        pl.semaphore_signal(barrier, inc=1, device_id=peer(at, axis, off), device_id_type=MESH)
    pl.semaphore_wait(barrier, len(peers))


ALL_PEERS = [("core", 1)] + [(axis, off) for axis in "xyz" for off in (1, 2, 3)]


def add_rows(out, out_start, terms, rows, step=48):
    def body(i, carry):
        base = i * step
        total = None
        for ref, start in terms:
            term = ref[pl.ds(pl.multiple_of(start + base, 16), step), :].astype(jnp.float32)
            total = term if total is None else total + term
        out[pl.ds(pl.multiple_of(out_start + base, 16), step), :] = total.astype(out.dtype)
        return carry

    lax.fori_loop(0, rows // step, body, 0)


def layer_kernel(
    resets, tok, cot, docs, init_in, offset_in, query_b, value_b, mixer_b, gain_1, shift_1, outer_b,
    gain_2, shift_2, inner_in, wq_h, wk_h, wv_h, wm_h, wi_h, wo_h,
    out, orow, ow, xm, ub, act, dz, df, da, dh1, sums, inner_sum,
    drow, dmem, ubw, gw, dzw, dfw, daw, small, dlast, mlast, dh1w,
    kv, probs, h1w, zw, h2w, vec, inner_b,
    wq, wk, wv, wm, wi, wo, wown, vown, sbuf, lab, bias, osend, owsend, init, offset,
    slope, total, unit_1, inverse_1, dout, doh, dow, acc, dsend, msend, wide,
    w_sem, q_s, q_r, o_s, o_r, m_s, m_r, l_s, l_r, d_s, d_r, x_s, x_r, mm_s, mm_r,
):
    z = lax.axis_index("seq")
    fetched = fetch(
        [(wq_h, wq), (wk_h, wk), (wv_h, wv), (wm_h, wm), (wi_h, wi), (wo_h, wo)], w_sem
    )
    started = []
    vectors = (query_b, value_b, mixer_b, gain_1, shift_1, outer_b, gain_2, shift_2)
    for i, ref in enumerate(vectors):
        vec[i : i + 1, :] = ref[...].astype(F32).reshape(1, MODEL)
    inner_b[...] = inner_in[...].astype(F32).reshape(1, INNER)
    for padded, ref in ((init, init_in), (offset, offset_in)):
        padded[...] = jnp.zeros((PAD, MODEL), LOW)
        padded[0:SLOTS, :] = ref[...]
    ring_barrier()
    lab[pl.ds(z, 1)] = docs[...][None]
    label_copies = [
        push(started, docs, lab.at[z], l_s.at[d - 1], l_r.at[d - 1], d) for d in (1, 2, 3)
    ]
    tokens = tok[...].reshape(ROWS, MODEL)
    fetched[0].wait()
    queries = ((dot(tokens, wq[...]) + vec[QUERY_B : QUERY_B + 1, :]) * SCALE).astype(LOW)
    for g in range(4):
        for s in range(SEGS):
            sbuf[g, s, :, 0:GROUP] = queries[
                s * BLOCK : (s + 1) * BLOCK, g * GROUP : (g + 1) * GROUP
            ]
    fetched[1].wait()
    keys = dot(tokens, wk[...]).astype(LOW)
    for g in range(4):
        for s in range(SEGS):
            sbuf[g, s, :, GROUP : 2 * GROUP] = keys[
                s * BLOCK : (s + 1) * BLOCK, g * GROUP : (g + 1) * GROUP
            ]
    fetched[2].wait()
    values = (dot(tokens, wv[...]) + vec[VALUE_B : VALUE_B + 1, :]).astype(LOW)
    for g in range(4):
        for s in range(SEGS):
            sbuf[g, s, :, 2 * GROUP :] = values[
                s * BLOCK : (s + 1) * BLOCK, g * GROUP : (g + 1) * GROUP
            ]
    here = pl.ds(pl.multiple_of(z * BLOCK, BLOCK), BLOCK)
    row_copies = {}

    def send_rows(s):
        row_copies[s] = [
            push(
                started, sbuf.at[ring(d), s], kv.at[s, here],
                q_s.at[s, d - 1], q_r.at[s, d - 1], d,
            )
            for d in (1, 2, 3)
        ]

    send_rows(0)
    send_rows(1)
    for s in range(SEGS):
        kv[s, here, :] = sbuf[z, s]
        kv[s, TOKENS + MEMORY :, :] = jnp.zeros((KEYS - TOKENS - MEMORY, TRIPLE), LOW)
    for g in range(4):

        @pl.when(z == g)
        def _():
            cut = slice(g * GROUP, (g + 1) * GROUP)
            wown[:, 0:GROUP] = wq[:, cut]
            wown[:, GROUP : 2 * GROUP] = wk[:, cut]
            wown[:, 2 * GROUP :] = wv[:, cut]
            vown[0:1, 0:GROUP] = vec[QUERY_B : QUERY_B + 1, cut]
            vown[0:1, GROUP : 2 * GROUP] = jnp.zeros((1, GROUP), F32)
            vown[0:1, 2 * GROUP :] = vec[VALUE_B : VALUE_B + 1, cut]

    lane = lax.broadcasted_iota(jnp.int32, (1, TRIPLE), 1)
    factor = jnp.where(lane < GROUP, SCALE, 1.0)
    slot = lax.broadcasted_iota(jnp.int32, (PAD, MODEL), 0)
    key_lane = lax.broadcasted_iota(jnp.int32, (PAD, KEYS), 1)
    filled = (key_lane < TOKENS + SLOTS) | (
        (key_lane >= TOKENS + PAD) & (key_lane < TOKENS + PAD + SLOTS)
    )
    write_bias = jnp.where(filled, 0.0, HIDDEN)

    def attend(query_rows, mask, s, row_at, rows):
        parts = []
        for h in range(MINE):
            key_head = kv[s, :, GROUP + h * HEAD : GROUP + (h + 1) * HEAD]
            value_head = kv[s, :, 2 * GROUP + h * HEAD : 2 * GROUP + (h + 1) * HEAD]
            scores = dot_t(query_rows[:, h * HEAD : (h + 1) * HEAD], key_head) + mask
            weights = jnp.exp(scores - jnp.max(scores, axis=-1, keepdims=True))
            total = jnp.sum(weights, axis=-1, keepdims=True)
            prob = (weights * (1.0 / total)).astype(LOW)
            probs[s, h, pl.ds(row_at, rows), :] = prob
            parts.append(dot(prob, value_head))
        return jnp.concatenate(parts, axis=1).astype(LOW)

    memory = init[...]
    for copy in label_copies:
        copy.wait_recv()
    for s in range(SEGS):
        for i in range(4):
            column = jnp.transpose(jnp.broadcast_to(lab[i, s : s + 1, :].astype(F32), (BLOCK, BLOCK)))
            for j in range(4):
                row = jnp.broadcast_to(lab[j, s : s + 1, :].astype(F32), (BLOCK, BLOCK))
                bias[s, i * BLOCK : (i + 1) * BLOCK, j * BLOCK : (j + 1) * BLOCK] = jnp.where(
                    column == row, 0.0, HIDDEN
                ).astype(LOW)
            bias[s, i * BLOCK : (i + 1) * BLOCK, TOKENS:] = jnp.broadcast_to(
                write_bias[0:1, TOKENS:], (BLOCK, BLOCK)
            ).astype(LOW)
    out_copies = []
    for s in range(SEGS):
        written_in = (memory.astype(F32) + offset[...].astype(F32)).astype(LOW)
        xm[s, 0:PAD, :] = written_in
        xm[s, PAD:, :] = memory
        kv[s, TOKENS : TOKENS + MEMORY, :] = (
            (dot(xm[s], wown[...]) + vown[0:1, :]) * factor
        ).astype(LOW)
        for copy in row_copies[s]:
            copy.wait_recv()
        if s < SEGS - 1:
            mixed = attend(kv[s, TOKENS : TOKENS + PAD, :], write_bias, s, TOKENS, PAD)
            owsend[s] = mixed
            ow[s, pl.ds(z, 1)] = mixed[None]
            write_copies = [
                push(started, owsend.at[s], ow.at[s, z], m_s.at[s, d - 1], m_r.at[s, d - 1], d)
                for d in (1, 2, 3)
            ]
            if s == 0:
                send_rows(2)

        def block(i, carry):
            row_at = pl.multiple_of(i * BLOCK, BLOCK)
            rows = pl.ds(row_at, BLOCK)
            osend[s, i] = attend(kv[s, rows, :], bias[s, rows, :].astype(F32), s, row_at, BLOCK)
            return carry

        lax.fori_loop(0, 4, block, 0)
        part = slice(s * BLOCK, (s + 1) * BLOCK)
        out_copies += [
            push(
                started, osend.at[s, ring(d)], orow.at[z, part],
                o_s.at[s, d - 1], o_r.at[s, d - 1], d,
            )
            for d in (1, 2, 3)
        ]
        orow[z, part, :] = osend[s, z]
        if s < SEGS - 1:
            if s == 0:
                for copy in fetched[3:]:
                    copy.wait()
            for copy in write_copies:
                copy.wait_recv()
            hidden = xm[s, 0:PAD, :].astype(F32) + vec[MIXER_B : MIXER_B + 1, :]
            for g in range(4):
                hidden = hidden + dot(ow[s, g], wm[g * GROUP : (g + 1) * GROUP, :])
            h1w[s] = hidden
            unit, _ = norm_parts(hidden)
            upper = unit * vec[GAIN_1 : GAIN_1 + 1, :] + vec[SHIFT_1 : SHIFT_1 + 1, :]
            inner = dot(upper.astype(LOW), wi[...]) + inner_b[...]
            zw[s] = inner
            active, _ = gelu_parts(inner)
            hidden = upper + dot(active.astype(LOW), wo[...]) + vec[OUTER_B : OUTER_B + 1, :]
            h2w[s] = hidden
            unit, _ = norm_parts(hidden)
            result = unit * vec[GAIN_2 : GAIN_2 + 1, :] + vec[SHIFT_2 : SHIFT_2 + 1, :]
            flag = jnp.full((PAD, MODEL), resets[0, s], jnp.int32)
            result = jnp.where(flag > 0, init[...].astype(F32), result)
            memory = jnp.where(slot < SLOTS, result, 0.0).astype(LOW)
    for copy in out_copies:
        copy.wait_recv()
    first_gain = vec[GAIN_1 : GAIN_1 + 1, :]
    second_gain = vec[GAIN_2 : GAIN_2 + 1, :]
    hidden = tok[...].reshape(ROWS, MODEL).astype(F32) + vec[MIXER_B : MIXER_B + 1, :]
    for g in range(4):
        hidden = hidden + dot(orow[g], wm[g * GROUP : (g + 1) * GROUP, :])
    unit, inverse = norm_parts(hidden)
    unit_1[...] = unit
    inverse_1[...] = inverse
    upper = unit * first_gain + vec[SHIFT_1 : SHIFT_1 + 1, :]
    ub[...] = upper.astype(LOW)
    total[...] = upper + vec[OUTER_B : OUTER_B + 1, :]

    def ahead(j):
        cut = pl.ds(j * MODEL, MODEL)
        inner = dot(ub[...], wi[:, cut]) + inner_b[:, cut]
        active, slant = gelu_parts(inner)
        active = active.astype(LOW)
        act[:, cut] = active
        slope[:, cut] = slant.astype(LOW)
        total[...] += dot(active, wo[cut, :])

    for j in range(INNER // MODEL):
        ahead(j)
    unit, inverse = norm_parts(total[...])
    result = unit * second_gain + vec[SHIFT_2 : SHIFT_2 + 1, :]
    out[...] = result.astype(LOW).reshape(1, SEGS, BLOCK, MODEL)
    upstream = cot[...].reshape(ROWS, MODEL).astype(F32)
    sums[GAIN_2 : GAIN_2 + 1, :] = column_sum(upstream * unit)
    sums[SHIFT_2 : SHIFT_2 + 1, :] = column_sum(upstream)
    d_hidden = norm_back(upstream, unit, inverse, second_gain)
    total[...] = d_hidden
    d_low = d_hidden.astype(LOW)
    df[...] = d_low
    sums[OUTER_B : OUTER_B + 1, :] = column_sum(d_low)

    def back(j):
        cut = pl.ds(j * MODEL, MODEL)
        d_inner = (dot_t(df[...], wo[cut, :]) * slope[:, cut].astype(F32)).astype(LOW)
        dz[:, cut] = d_inner
        inner_sum[:, cut] = column_sum(d_inner)
        total[...] += dot_t(d_inner, wi[:, cut])

    for j in range(INNER // MODEL):
        back(j)
    upstream = total[...]
    unit = unit_1[...]
    sums[GAIN_1 : GAIN_1 + 1, :] = column_sum(upstream * unit)
    sums[SHIFT_1 : SHIFT_1 + 1, :] = column_sum(upstream)
    d_hidden = norm_back(upstream, unit, inverse_1[...], first_gain)
    dh1[...] = d_hidden
    d_low = d_hidden.astype(LOW)
    da[...] = d_low
    sums[MIXER_B : MIXER_B + 1, :] = column_sum(d_low)
    sums[QUERY_B : QUERY_B + 2, :] = jnp.zeros((2, MODEL), F32)
    for g in range(4):
        dout[g] = dot_t(d_low, wm[g * GROUP : (g + 1) * GROUP, :]).astype(LOW)
    in_copies = {}
    for s in reversed(range(SEGS)):
        part = slice(s * BLOCK, (s + 1) * BLOCK)
        in_copies[s] = [
            push(
                started, dout.at[ring(d), part], doh.at[s, here],
                d_s.at[s, d - 1], d_r.at[s, d - 1], d,
            )
            for d in (1, 2, 3)
        ]
        doh[s, here, :] = dout[z, part, :]

    def head_back(s, h, d_rows, rows):
        cut = slice(h * HEAD, (h + 1) * HEAD)
        key_head = kv[s, :, GROUP + h * HEAD : GROUP + (h + 1) * HEAD]
        value_head = kv[s, :, 2 * GROUP + h * HEAD : 2 * GROUP + (h + 1) * HEAD]
        d_head = d_rows[:, cut]
        prob = probs[s, h, rows, :]
        wide_prob = prob.astype(F32)
        product = wide_prob * dot_t(d_head, value_head)
        delta = jnp.sum(product, axis=-1, keepdims=True)
        d_scores = (product - wide_prob * delta).astype(LOW)
        d_query = (dot(d_scores, key_head) * SCALE).astype(LOW)
        d_key = t_dot(d_scores, kv[s, rows, cut])
        d_value = t_dot(prob, d_head)
        return d_query, d_key, d_value

    def tokens_back(s):
        for copy in in_copies[s]:
            copy.wait_recv()
        rows = slice(0, TOKENS)
        for h in range(MINE):
            cut = slice(h * HEAD, (h + 1) * HEAD)
            d_query, d_key, d_value = head_back(s, h, doh[s], rows)
            dsend[s, :, cut] = d_query
            acc[:, cut] = d_key
            acc[:, GROUP + h * HEAD : GROUP + (h + 1) * HEAD] = d_value

    def writes_back(s):
        rows = slice(TOKENS, TOKENS + PAD)
        for h in range(MINE):
            cut = slice(h * HEAD, (h + 1) * HEAD)
            d_query, d_key, d_value = head_back(s, h, dow[...], rows)
            msend[s, 0:PAD, cut] = d_query
            acc[:, cut] += d_key
            acc[:, GROUP + h * HEAD : GROUP + (h + 1) * HEAD] += d_value

    mem_copies = {}
    back_copies = []

    def finish(s):
        if s == SEGS - 1:
            msend[s, :, 0:GROUP] = jnp.zeros((MEMORY, GROUP), LOW)
        else:
            msend[s, PAD:, 0:GROUP] = jnp.zeros((PAD, GROUP), LOW)
        msend[s, :, GROUP:] = acc[TOKENS : TOKENS + MEMORY, :].astype(LOW)
        mem_copies[s] = [
            push(started, msend.at[s], dmem.at[s - 1, z], mm_s.at[s, d - 1], mm_r.at[s, d - 1], d)
            for d in (1, 2, 3)
        ]
        dmem[s - 1, z] = msend[s]
        dsend[s, :, GROUP:] = acc[0:TOKENS, :].astype(LOW)
        kept = slice((s - 1) * BLOCK, s * BLOCK)
        for d in (1, 2, 3):
            there = pl.ds(pl.multiple_of(ring(d) * BLOCK, BLOCK), BLOCK)
            back_copies.append(
                push(
                    started, dsend.at[s, there], drow.at[z, kept],
                    x_s.at[s, d - 1], x_r.at[s, d - 1], d,
                )
            )
        drow[z, kept, :] = dsend[s, here, :]

    parts = {}

    def add(name, value):
        parts[name] = value if name not in parts else parts[name] + value

    saved = {}

    def memory_back(s):
        for copy in mem_copies[s]:
            copy.wait_recv()
        for g in range(4):
            for t in range(3):
                wide[t, :, g * GROUP : (g + 1) * GROUP] = dmem[
                    s - 1, g, :, t * GROUP : (t + 1) * GROUP
                ]
        d_rows = dot_t(wide[0], wq[...]) + dot_t(wide[1], wk[...]) + dot_t(wide[2], wv[...])
        write = d_rows[0:PAD]
        if s < SEGS - 1:
            write = write + saved[s]
        grad = write + d_rows[PAD:]
        add("offset", write)
        add("norm", jnp.sum(jnp.sum(grad * grad, axis=0, keepdims=True), axis=1, keepdims=True))
        flag = jnp.full((PAD, MODEL), resets[0, s - 1], jnp.int32) > 0
        add("init", jnp.where(flag, grad, 0.0))
        return jnp.where(flag, 0.0, grad)

    def layer_back(s, upstream):
        unit, inverse = norm_parts(h2w[s])
        add("gain_2", column_sum(upstream * unit))
        add("shift_2", column_sum(upstream))
        d_second = norm_back(upstream, unit, inverse, second_gain)
        d_low = d_second.astype(LOW)
        dfw[s] = d_low
        add("outer", column_sum(d_low))
        active, slant = gelu_parts(zw[s])
        gw[s] = active.astype(LOW)
        d_inner = (dot_t(d_low, wo[...]) * slant).astype(LOW)
        dzw[s] = d_inner
        add("inner", column_sum(d_inner))
        unit, inverse = norm_parts(h1w[s])
        ubw[s] = (unit * first_gain + vec[SHIFT_1 : SHIFT_1 + 1, :]).astype(LOW)
        d_upper = dot_t(d_inner, wi[...]) + d_second
        add("gain_1", column_sum(d_upper * unit))
        add("shift_1", column_sum(d_upper))
        d_first = norm_back(d_upper, unit, inverse, first_gain)
        saved[s] = d_first
        if s == 0:
            dh1w[...] = d_first
        d_low = d_first.astype(LOW)
        daw[s] = d_low
        add("mixer", column_sum(d_low))
        own = pl.ds(pl.multiple_of(z * GROUP, HEAD), GROUP)
        dow[...] = dot_t(d_low, wm[own, :]).astype(LOW)

    tokens_back(2)
    finish(2)
    tokens_back(1)
    layer_back(1, memory_back(2))
    writes_back(1)
    finish(1)
    tokens_back(0)
    layer_back(0, memory_back(1))
    writes_back(0)
    msend[0, PAD:, 0:GROUP] = jnp.zeros((PAD, GROUP), LOW)
    msend[0, :, GROUP:] = acc[TOKENS : TOKENS + MEMORY, :].astype(LOW)
    dsend[0, :, GROUP:] = acc[0:TOKENS, :].astype(LOW)
    dlast[...] = dsend[0]
    mlast[...] = msend[0]
    quarter = 0.25
    row = lax.broadcasted_iota(jnp.int32, (24, MODEL), 0)
    zero = jnp.zeros((1, MODEL), F32)
    small[0:8, :] = quarter * jnp.concatenate(
        [zero, zero]
        + [parts[n] for n in ("mixer", "gain_1", "shift_1", "outer", "gain_2", "shift_2")],
        axis=0,
    )
    small[8:16, :] = quarter * jnp.concatenate(
        [parts["inner"][:, i * MODEL : (i + 1) * MODEL] for i in range(4)] + [zero] * 4, axis=0
    )
    small[16:40, :] = quarter * parts["init"][0:24]
    small[40:64, :] = quarter * (
        parts["offset"][0:24]
        + jnp.where(row >= SLOTS, jnp.broadcast_to(parts["norm"], (24, MODEL)), 0.0)
    )
    for copy in back_copies:
        copy.wait_recv()
    for copy in started:
        copy.wait_send()
def layer(resets, tok, cot, docs, init, offset, vectors, inner_b, weights):
    def buffer(*dims):
        return pltpu.VMEM(dims, LOW)

    def wide_buffer(*dims):
        return pltpu.VMEM(dims, F32)

    by_segment = [DMA((SEGS, 3)), DMA((SEGS, 3))]
    return pl.pallas_call(
        layer_kernel,
        out_shape=(
            shape((1, SEGS, BLOCK, MODEL)),
            shape((4, ROWS, GROUP)),
            shape((2, 4, PAD, GROUP)),
            shape((SEGS, MEMORY, MODEL)),
            shape((ROWS, MODEL)),
            shape((ROWS, INNER)),
            shape((ROWS, INNER)),
            shape((ROWS, MODEL)),
            shape((ROWS, MODEL)),
            shape((ROWS, MODEL), F32),
            shape((8, MODEL), F32),
            shape((1, INNER), F32),
            shape((4, ROWS - BLOCK, TRIPLE)),
            shape((SEGS - 1, 4, MEMORY, TRIPLE)),
            shape((2, PAD, MODEL)),
            shape((2, PAD, INNER)),
            shape((2, PAD, INNER)),
            shape((2, PAD, MODEL)),
            shape((2, PAD, MODEL)),
            shape((64, MODEL), F32),
            shape((TOKENS, TRIPLE)),
            shape((MEMORY, TRIPLE)),
            shape((PAD, MODEL), F32),
        ),
        in_specs=[pl.BlockSpec(memory_space=pltpu.SMEM)] + [VMEM] * 14 + [ANY] * 6,
        out_specs=(VMEM,) * 23,
        scratch_shapes=[
            buffer(SEGS, KEYS, TRIPLE),
            buffer(SEGS, MINE, QUERIES, KEYS),
            wide_buffer(2, PAD, MODEL),
            wide_buffer(2, PAD, INNER),
            wide_buffer(2, PAD, MODEL),
            wide_buffer(8, MODEL),
            wide_buffer(1, INNER),
        ]
        + weight_buffers()
        + [
            buffer(MODEL, TRIPLE),
            wide_buffer(8, TRIPLE),
            buffer(4, SEGS, BLOCK, TRIPLE),
            pltpu.VMEM((4, SEGS, BLOCK), jnp.int32),
            buffer(SEGS, TOKENS, KEYS),
            buffer(SEGS, 4, BLOCK, GROUP),
            buffer(2, PAD, GROUP),
            buffer(PAD, MODEL),
            buffer(PAD, MODEL),
            buffer(ROWS, INNER),
            wide_buffer(ROWS, MODEL),
            wide_buffer(ROWS, MODEL),
            wide_buffer(ROWS, 1),
            buffer(4, ROWS, GROUP),
            buffer(SEGS, TOKENS, GROUP),
            buffer(PAD, GROUP),
            wide_buffer(KEYS, 2 * GROUP),
            buffer(SEGS, TOKENS, TRIPLE),
            buffer(SEGS, MEMORY, TRIPLE),
            buffer(3, MEMORY, MODEL),
            DMA((6,)),
        ]
        + by_segment * 2
        + [DMA((2, 3)), DMA((2, 3)), DMA((3,)), DMA((3,))]
        + by_segment * 3,
        compiler_params=pltpu.CompilerParams(
            collective_id=1, has_side_effects=True, vmem_limit_bytes=62 << 20
        ),
        name="layer",
    )(resets, tok, cot, docs, init, offset, *vectors, inner_b, *weights)


FULL = ROWS + MEMORY
MOST = ROWS + PAD
UNITS = ((4, 5, 6), (7, 8, 9), (0, 1, 2), (10, 11, 3))


def finish_kernel(
    tok, xm, drow, dmem, orow, ow, dh1, sums, inner_sum, small, ubw, gw, dzw, dfw, daw, dsend, msend, dh1w,
    ub_h, act_h, dz_h, df_h, da_h, wq_h, wk_h, wv_h,
    packed, input_grad, ext,
    ub, act, dz, df, da, wq, wk, wv, rows, triple, mixed,
    drow0, dmall, wide, g, crecv, r1, r2, r3, slots, own_ext, ecore, ex, ey, ez,
    w_sem, x_s, x_r, m_s, m_r, c_s, c_r, a_s, a_r, b_s, b_r, d_s, d_r, e_s, e_r, f_s, f_r,
    loc, free, n_s, n_r, o_s, o_r, gc_s, gc_r, t_s, t_r,
):
    at = places()
    z = at["z"]
    core = at["core"]
    top = pl.ds(0, ROWS)
    fetched = fetch(
        [
            (ub_h, ub.at[top]), (dz_h, dz.at[top]), (act_h, act.at[top]), (df_h, df.at[top]), (da_h, da.at[top]),
            (wq_h, wq), (wk_h, wk), (wv_h, wv),
        ],
        w_sem,
    )
    started = []

    def send(src, dst, s_sem, r_sem, axis, off):
        copy = pltpu.make_async_remote_copy(
            src_ref=src, dst_ref=dst, send_sem=s_sem, recv_sem=r_sem,
            device_id=peer(at, axis, off), device_id_type=MESH,
        )
        copy.start()
        started.append(copy)
        return copy

    def turn(value, off):
        return lax.rem(value + off + 4, 4)

    def ds(start, size):
        return pl.ds(pl.multiple_of(start, 16), size)

    place1 = [at[order[0]] for order in ORDERS]
    place2 = [at[order[1]] for order in ORDERS]
    place3 = [at[order[2]] for order in ORDERS]
    live = {}

    def sub_of(ref, start, n):
        side = pl.ds(pl.multiple_of(lax.rem(n, 2) * SIDE, 128), SIDE)
        return ref.at[ds(start + (n // 2) * SUB, SUB), side]

    def home(p, off):
        return core * HALF + turn(place1[p], off) * CHUNK

    def block_done(u, p):
        b = UNITS[u][p]
        live["core", u, p] = send(
            g.at[b, ds((1 - core) * HALF, HALF)], crecv.at[u, p],
            c_s.at[u, p], c_r.at[u, p], "core", 1,
        )
        started.pop()

    def stage1(u):
        for p in range(3):
            b = UNITS[u][p]
            live["core", u, p].wait_recv()
            held = crecv.at[u, p]
            start = turn(place1[p], 2) * CHUNK
            add_rows(held, start, [(g.at[b], core * HALF + start), (held, start)], CHUNK)
            live["a", u, p] = [
                send(
                    held.at[ds(start + i * SUB, SUB)], r1.at[u, p, i],
                    a_s.at[u, p, i], a_r.at[u, p, i], ORDERS[p][0], 1 + 2 * i,
                )
                for i in range(2)
            ]
        for p in range(3):
            b = UNITS[u][p]
            held = crecv.at[u, p]
            for off in (1, 3, 0):
                start = turn(place1[p], off) * CHUNK
                add_rows(held, start, [(g.at[b], core * HALF + start), (held, start)], CHUNK)
            live["core", u, p].wait_send()
        pl.semaphore_signal(
            free.at[u], inc=1, device_id=peer(at, "core", 1), device_id_type=MESH
        )

    def stage2(u):
        for p in range(3):
            held = crecv.at[u, p]
            live["b", u, p] = []
            for i in range(2):
                start = turn(place1[p], 1 + 2 * i) * CHUNK
                live["a", u, p][i].wait_recv()
                half = start + i * SUB
                add_rows(held, half, [(held, half), (r1.at[u, p, i], 0)], SUB)
                live["b", u, p].append(
                    send(
                        held.at[ds(start, CHUNK)], r2.at[u, p, i],
                        b_s.at[u, p, i], b_r.at[u, p, i], ORDERS[p][0], 1 + 2 * i,
                    )
                )

    def stage3(u):
        for p in range(3):
            held = crecv.at[u, p]
            start = place1[p] * CHUNK
            for copy in live["b", u, p]:
                copy.wait_recv()
            add_rows(held, start, [(held, start), (r2.at[u, p, 0], 0), (r2.at[u, p, 1], 0)], CHUNK)
            live["d", u, p] = [
                send(
                    sub_of(held, start, turn(place2[p], d)), r3.at[u, p, d - 1],
                    d_s.at[u, p, d - 1], d_r.at[u, p, d - 1], ORDERS[p][1], d,
                )
                for d in (1, 2, 3)
            ]

    def stage4(u):
        for p in range(3):
            for copy in live["d", u, p]:
                copy.wait_recv()
            total = sub_of(crecv.at[u, p], place1[p] * CHUNK, place2[p])[...].astype(F32)
            for d in range(3):
                total = total + r3[u, p, d].astype(F32)
            slots[u, p, pl.ds(place3[p], 1)] = total.astype(LOW)[None]
            live["e", u, p] = [
                send(
                    slots.at[u, p, place3[p]], slots.at[u, p, place3[p]],
                    e_s.at[u, p, d - 1], e_r.at[u, p, d - 1], ORDERS[p][2], d,
                )
                for d in (1, 2, 3)
            ]

    def stage5(u):
        for p in range(3):
            for copy in live["e", u, p]:
                copy.wait_recv()
            total = slots[u, p, 0].astype(F32)
            for i in range(1, 4):
                total = total + slots[u, p, i].astype(F32)
            target = sub_of(g.at[UNITS[u][p]], home(p, 0), place2[p])
            target[...] = total.astype(LOW)
            live["f", u, p] = [
                send(target, target, f_s.at[u, p, d - 1], f_r.at[u, p, d - 1], ORDERS[p][1], d)
                for d in (1, 2, 3)
            ]

    def across(u, p, j, start, count):
        piece = g.at[UNITS[u][p], ds(start, count)]
        live["gc", u, p, j] = send(piece, piece, gc_s.at[u, p, j], gc_r.at[u, p, j], "core", 1)

    def stage6(u):
        pl.semaphore_wait(free.at[u], 1)
        for p in range(3):
            for copy in live["f", u, p]:
                copy.wait_recv()
            piece = g.at[UNITS[u][p], ds(home(p, 0), CHUNK)]
            live["n", u, p] = [
                send(piece, piece, n_s.at[u, p, i], n_r.at[u, p, i], ORDERS[p][0], 1 + 2 * i)
                for i in range(2)
            ]
            across(u, p, 0, home(p, 0), CHUNK)

    def stage7(u):
        for p in range(3):
            live["o", u, p] = []
            for i in range(2):
                live["n", u, p][i].wait_recv()
                start = home(p, 3 - 2 * i)
                piece = g.at[UNITS[u][p], ds(start + i * SUB, SUB)]
                live["o", u, p].append(
                    send(piece, piece, o_s.at[u, p, i], o_r.at[u, p, i], ORDERS[p][0], 1 + 2 * i)
                )
                across(u, p, 1 + i, start, CHUNK)

    def stage8(u):
        for p in range(3):
            for i in range(2):
                live["o", u, p][i].wait_recv()
                across(u, p, 3 + i, home(p, 2) + i * SUB, SUB)

    stores = []

    def stage9(u):
        for p in range(3):
            for j in range(5):
                live["gc", u, p, j].wait_recv()
            b = UNITS[u][p]
            stores.append(
                pltpu.make_async_copy(
                    g.at[b], packed.at[pl.ds(b * MODEL, MODEL)], loc.at[u, p]
                )
            )
            stores[-1].start()

    stages = {
        1: stage1, 2: stage2, 3: stage3, 4: stage4, 5: stage5, 6: stage6, 7: stage7, 8: stage8,
        9: stage9,
    }

    def wave(*pairs):
        for u, k in pairs:
            stages[k](u)

    low_at = jnp.minimum(z, 1)
    low_keep = (z < 2).astype(F32).astype(LOW)
    at_seg = jnp.minimum(z, 2)
    keep = (z < SEGS).astype(F32).astype(LOW)

    def inner_block(j):
        g[4 + j] = t_dot(ub[...], dz[:, j * MODEL : (j + 1) * MODEL]).astype(LOW)

    def outer_block(j):
        g[8 + j] = t_dot(act[:, j * MODEL : (j + 1) * MODEL], df[...]).astype(LOW)

    def mixer_block():
        for i in range(4):
            mixed[i, 0:ROWS, :] = orow[i]
            mixed[i, ROWS:, :] = ow[low_at, i]
        for i in range(4):
            g[3, i * GROUP : (i + 1) * GROUP, :] = t_dot(mixed[i], da[...]).astype(LOW)

    greet(at, ALL_PEERS)
    row_copies = []
    for d in (1, 2, 3):
        there = ds(ring(d) * BLOCK, BLOCK)
        row_copies.append(
            send(dsend.at[there], drow0.at[z], x_s.at[d - 1], x_r.at[d - 1], "z", d)
        )
        row_copies.append(
            send(msend, dmall.at[0, z], m_s.at[d - 1], m_r.at[d - 1], "z", d)
        )
    drow0[z] = dsend[ds(z * BLOCK, BLOCK), :]
    dmall[0, z] = msend[...]
    dmall[1:] = dmem[...]
    ub[ROWS:, :] = ubw[low_at]
    act[ROWS:, :] = gw[low_at]
    dz[ROWS:, :] = dzw[low_at] * low_keep
    df[ROWS:, :] = dfw[low_at] * low_keep
    da[ROWS:, :] = daw[low_at] * low_keep
    for copy in fetched[:2]:
        copy.wait()
    for j in range(3):
        inner_block(j)
        block_done(0, j)
    inner_block(3)
    block_done(1, 0)
    wave((0, 1))
    for copy in fetched[2:4]:
        copy.wait()
    for j in range(2):
        outer_block(j)
        block_done(1, 1 + j)
    wave((0, 2), (1, 1))
    rows[0:ROWS, :] = tok[...].reshape(ROWS, MODEL)
    rows[ROWS:, :] = xm[at_seg]
    for copy in row_copies:
        copy.wait_recv()
    for i in range(4):
        for t in range(3):
            cut = slice(i * GROUP, (i + 1) * GROUP)
            part = slice(t * GROUP, (t + 1) * GROUP)
            triple[t, 0:BLOCK, cut] = drow0[i, :, part]
            triple[t, BLOCK:ROWS, cut] = drow[i, :, part]
            triple[t, ROWS:, cut] = dmall[at_seg, i, :, part] * keep
            wide[t, :, cut] = dmall[0, i, :, part]
    for t in range(3):
        g[t] = t_dot(rows[...], triple[t]).astype(LOW)
        block_done(2, t)
    wave((0, 3), (1, 2), (2, 1))
    for j in range(2, 4):
        outer_block(j)
        block_done(3, j - 2)
    fetched[4].wait()
    mixer_block()
    block_done(3, 2)
    wave((0, 4), (1, 3), (2, 2), (3, 1))
    for copy in fetched[5:]:
        copy.wait()
    d_rows = dot_t(wide[0], wq[...]) + dot_t(wide[1], wk[...]) + dot_t(wide[2], wv[...])
    write = d_rows[0:PAD] + dh1w[...]
    grad = write + d_rows[PAD:]
    norm = jnp.sum(jnp.sum(grad * grad, axis=0, keepdims=True), axis=1, keepdims=True)
    own_ext[0:8, :] = small[0:8, :] + sums[...]
    own_ext[8:16, :] = small[8:16, :] + jnp.concatenate(
        [inner_sum[:, i * MODEL : (i + 1) * MODEL] for i in range(4)]
        + [jnp.zeros((4, MODEL), F32)],
        axis=0,
    )
    own_ext[QUERY_B : QUERY_B + 1, :] += column_sum(triple[0])
    own_ext[VALUE_B : VALUE_B + 1, :] += column_sum(triple[2])
    row = lax.broadcasted_iota(jnp.int32, (24, MODEL), 0)
    own_ext[16:40, :] = small[16:40, :] + 0.25 * grad[0:24]
    own_ext[40:64, :] = small[40:64, :] + 0.25 * (
        write[0:24] + jnp.where(row >= SLOTS, jnp.broadcast_to(norm, (24, MODEL)), 0.0)
    )
    half = pl.ds(pl.multiple_of(core * 32, 8), 32)
    other = pl.ds(pl.multiple_of((1 - core) * 32, 8), 32)
    small_core = send(own_ext.at[other], ecore, t_s.at[0], t_r.at[0], "core", 1)
    wave((0, 5), (1, 4), (2, 3), (3, 2))
    small_core.wait_recv()
    ecore[...] = own_ext[half, :] + ecore[...]
    small_x = [
        send(
            ecore.at[pl.ds(pl.multiple_of(turn(at["x"], d) * 8, 8), 8)],
            ex.at[d - 1], t_s.at[d], t_r.at[d], "x", d,
        )
        for d in (1, 2, 3)
    ]
    input_grad[...] = (
        dh1[...]
        + dot_t(triple[0, 0:ROWS, :], wq[...])
        + dot_t(triple[1, 0:ROWS, :], wk[...])
        + dot_t(triple[2, 0:ROWS, :], wv[...])
    ).reshape(1, SEGS, BLOCK, MODEL)
    wave((0, 6), (1, 5), (2, 4), (3, 3))
    for copy in small_x:
        copy.wait_recv()
    ey[pl.ds(at["y"], 1)] = (
        ecore[pl.ds(pl.multiple_of(at["x"] * 8, 8), 8), :] + ex[0] + ex[1] + ex[2]
    )[None]
    small_y = [
        send(ey.at[at["y"]], ey.at[at["y"]], t_s.at[3 + d], t_r.at[3 + d], "y", d)
        for d in (1, 2, 3)
    ]
    wave((0, 7), (1, 6), (2, 5), (3, 4))
    for copy in small_y:
        copy.wait_recv()
    ez[pl.ds(at["z"], 1)] = (ey[0] + ey[1] + ey[2] + ey[3])[None]
    small_z = [
        send(ez.at[at["z"]], ez.at[at["z"]], t_s.at[6 + d], t_r.at[6 + d], "z", d)
        for d in (1, 2, 3)
    ]
    wave((0, 8), (1, 7), (2, 6), (3, 5))
    for copy in small_z:
        copy.wait_recv()
    mine = pl.ds(pl.multiple_of(core * 32 + at["x"] * 8, 8), 8)
    ext[mine, :] = ez[0] + ez[1] + ez[2] + ez[3]
    small_back = [
        send(ext.at[mine], ext.at[mine], t_s.at[9 + d], t_r.at[9 + d], "x", d) for d in (1, 2, 3)
    ]
    wave((1, 8), (2, 7), (3, 6), (0, 9))
    for copy in small_back:
        copy.wait_recv()
    small_last = send(ext.at[half], ext.at[half], t_s.at[13], t_r.at[13], "core", 1)
    wave((2, 8), (3, 7), (1, 9), (3, 8), (2, 9))
    small_last.wait_recv()
    wave((3, 9))
    for copy in started:
        copy.wait_send()
    for copy in stores:
        copy.wait()


def finish_all(near, far):
    def buffer(*dims):
        return pltpu.VMEM(dims, LOW)

    def wide_buffer(*dims):
        return pltpu.VMEM(dims, F32)

    pairs = [
        (3,), (3,), (4, 3), (4, 3, 2), (4, 3, 2), (4, 3, 3), (4, 3, 3), (4, 3, 3), None,
        (4, 3, 2), (4, 3, 2), (4, 3, 5), (14,),
    ]
    sems = [DMA((8,))]
    for dims in pairs:
        if dims is None:
            sems += [DMA((4, 3)), pltpu.SemaphoreType.REGULAR((4,))]
        else:
            sems += [DMA(dims), DMA(dims)]
    return pl.pallas_call(
        finish_kernel,
        out_shape=(
            shape((12 * MODEL, MODEL)),
            shape((1, SEGS, BLOCK, MODEL), F32),
            shape((64, MODEL), F32),
        ),
        in_specs=[VMEM] * len(near) + [ANY] * len(far),
        out_specs=(ANY, VMEM, VMEM),
        scratch_shapes=[
            buffer(MOST, MODEL),
            buffer(MOST, INNER),
            buffer(MOST, INNER),
            buffer(MOST, MODEL),
            buffer(MOST, MODEL),
            buffer(MODEL, MODEL),
            buffer(MODEL, MODEL),
            buffer(MODEL, MODEL),
            buffer(FULL, MODEL),
            buffer(3, FULL, MODEL),
            buffer(4, MOST, GROUP),
            buffer(4, BLOCK, TRIPLE),
            buffer(SEGS, 4, MEMORY, TRIPLE),
            buffer(3, MEMORY, MODEL),
            buffer(12, MODEL, MODEL),
            buffer(4, 3, HALF, MODEL),
            buffer(4, 3, 2, SUB, MODEL),
            buffer(4, 3, 2, CHUNK, MODEL),
            buffer(4, 3, 3, SUB, SIDE),
            buffer(4, 3, 4, SUB, SIDE),
            wide_buffer(64, MODEL),
            wide_buffer(32, MODEL),
            wide_buffer(3, 8, MODEL),
            wide_buffer(4, 8, MODEL),
            wide_buffer(4, 8, MODEL),
        ]
        + sems,
        compiler_params=pltpu.CompilerParams(
            collective_id=3, has_side_effects=True, vmem_limit_bytes=62 << 20
        ),
        name="weights_and_sums",
    )(*near, *far)


def widen_kernel(
    count, packed, ext, grad_in, layer_in,
    layer_out, grad_out, query_w, key_w, value_w, mixer_w, inner_w, outer_w, query_b, value_b, mixer_b, gain_1, shift_1,
    inner_b, outer_b, gain_2, shift_2, init, offset, norm,
    low, wide, in_sem, out_sem,
):
    through = pltpu.make_async_copy(grad_in, grad_out, in_sem.at[12])
    through.start()
    layer_through = pltpu.make_async_copy(layer_in, layer_out, in_sem.at[13])
    layer_through.start()
    def rows(i):
        return pl.ds(i * MODEL, MODEL)

    loads = [pltpu.make_async_copy(packed.at[rows(i)], low.at[i], in_sem.at[i]) for i in range(12)]
    for copy in loads:
        copy.start()
    targets = [query_w, key_w, value_w, mixer_w]
    targets += [inner_w.at[:, rows(i)] for i in range(4)]
    targets += [outer_w.at[rows(i)] for i in range(4)]
    stores = []
    for i in range(12):
        loads[i].wait()

        def body(j, carry):
            part = pl.ds(pl.multiple_of(j * 96, 96), 96)
            wide[i, part, :] = low[i, part, :].astype(F32)
            return carry

        lax.fori_loop(0, 8, body, 0)
        stores.append(pltpu.make_async_copy(wide.at[i], targets[i], out_sem.at[i]))
        stores[-1].start()
    singles = (
        (query_b, QUERY_B), (value_b, VALUE_B), (mixer_b, MIXER_B), (gain_1, GAIN_1),
        (shift_1, SHIFT_1), (outer_b, OUTER_B), (gain_2, GAIN_2), (shift_2, SHIFT_2),
    )
    for ref, row in singles:
        ref[...] = ext[row : row + 1, :].reshape(MODEL)
    inner_b[...] = jnp.concatenate([ext[8 + i : 9 + i, :] for i in range(4)], axis=1).reshape(INNER)
    init[...] = ext[16 : 16 + SLOTS, :]
    offset[...] = ext[40 : 40 + SLOTS, :]
    norm[...] = jnp.sqrt(ext[60:61, 0:1] * (1.0 / count))
    for copy in stores:
        copy.wait()
    through.wait()
    layer_through.wait()


def widen(packed, ext, input_grad, layer_output, chains):
    square = shape((MODEL, MODEL), F32)
    line = shape((MODEL,), F32)
    slots = shape((SLOTS, MODEL), F32)
    return pl.pallas_call(
        functools.partial(widen_kernel, chains * SEGS * SLOTS * MODEL),
        out_shape=(
            shape((1, SEGS, BLOCK, MODEL)), shape((1, SEGS, BLOCK, MODEL), F32), square, square, square, square, shape((MODEL, INNER), F32), shape((INNER, MODEL), F32),
            line, line, line, line, line, shape((INNER,), F32), line, line, line, slots, slots,
            shape((1, 1), F32),
        ),
        in_specs=[ANY, VMEM, VMEM, VMEM],
        out_specs=(ANY,) * 8 + (VMEM,) * 12,
        scratch_shapes=[
            pltpu.VMEM((12, MODEL, MODEL), LOW),
            pltpu.VMEM((12, MODEL, MODEL), F32),
            DMA((14,)),
            DMA((12,)),
        ],
        compiler_params=pltpu.CompilerParams(vmem_limit_bytes=60 << 20),
        name="widen",
    )(packed, ext, input_grad, layer_output)


def shards(
    tokens, documents, resets, cotangent, query_weight, query_bias, key_weight, value_weight,
    value_bias, mixer_weight, mixer_bias, first_gain, first_shift, inner_weight, inner_bias,
    outer_weight, outer_bias, second_gain, second_shift, memory_init, write_offset,
):
    weights = (query_weight, key_weight, value_weight, mixer_weight, inner_weight, outer_weight)
    vectors = (
        query_bias, value_bias, mixer_bias, first_gain, first_shift, outer_bias, second_gain,
        second_shift,
    )
    tok = tokens[0]
    (
        layer_output, orow, ow, xm, ub, act, dz, df, da, dh1, sums, inner_sum,
        drow, dmem, ubw, gw, dzw, dfw, daw, small, dlast, mlast, dh1w,
    ) = layer(
        resets, tok, cotangent[0], documents[0], memory_init, write_offset, vectors, inner_bias,
        weights,
    )
    packed, input_grad, ext = finish_all(
        (
            tok, xm, drow, dmem, orow, ow, dh1, sums, inner_sum, small, ubw, gw, dzw, dfw, daw,
            dlast, mlast, dh1w,
        ),
        (ub, act, dz, df, da) + weights[:3],
    )
    (
        layer_output, input_grad, query_w, key_w, value_w, mixer_w, inner_w, outer_w, query_b, value_b, mixer_b, gain_1,
        shift_1, inner_b, outer_b, gain_2, shift_2, init, offset, memory_norm,
    ) = widen(packed, ext, input_grad, layer_output, lax.axis_size("chain"))
    return (
        layer_output, input_grad, query_w, query_b, key_w, value_w, value_b, mixer_w, mixer_b,
        gain_1, shift_1, inner_w, inner_b, outer_w, outer_b, gain_2, shift_2, init, offset,
        memory_norm.reshape(()),
    )


def solution(mesh):
    tokens = P("chain", None, "seq", None)
    in_specs = (tokens, P("chain", None, "seq"), P("chain", None), tokens) + (P(),) * 17
    out_specs = (tokens, tokens) + (P(),) * 18
    return jax.shard_map(shards, mesh=mesh, in_specs=in_specs, out_specs=out_specs, check_vma=False)
```

```python
import functools

import jax
import jax.numpy as jnp
from jax import lax
from jax.experimental import pallas as pl
from jax.experimental.pallas import tpu as pltpu
from jax.sharding import PartitionSpec as P

MESH = pl.DeviceIdType.MESH
LOW = jnp.bfloat16
F32 = jnp.float32
SEGS = 3
BLOCK = 128
MODEL = 768
INNER = 3072
SLOTS = 20
PAD = 32
MEMORY = 2 * PAD
ROWS = SEGS * BLOCK
TOKENS = 512
KEYS = 640
QUERIES = TOKENS + PAD
HEAD = 64
MINE = 3
GROUP = MINE * HEAD
TRIPLE = 3 * GROUP
SCALE = HEAD ** (-0.5)
EPS = 1e-12
HIDDEN = -1e30


def dot(left, right):
    return jnp.dot(left, right, preferred_element_type=F32)


def dot_t(left, right):
    return lax.dot_general(left, right, (((1,), (1,)), ((), ())), preferred_element_type=F32)


def t_dot(left, right):
    return lax.dot_general(left, right, (((0,), (0,)), ((), ())), preferred_element_type=F32)


def norm_parts(hidden):
    centre = hidden - jnp.mean(hidden, axis=-1, keepdims=True)
    spread = jnp.mean(centre * centre, axis=-1, keepdims=True)
    inverse = lax.rsqrt(spread + EPS)
    return centre * inverse, inverse


def norm_back(upstream, unit, inverse, gain):
    scaled = upstream * gain
    first = jnp.mean(scaled, axis=-1, keepdims=True)
    second = jnp.mean(scaled * unit, axis=-1, keepdims=True)
    return (scaled - first - unit * second) * inverse


def gelu_parts(values):
    below = 0.5 * (1.0 + lax.erf(values * (0.5**0.5)))
    density = jnp.exp(-0.5 * values * values) * 0.3989422804014327
    return values * below, below + values * density


def column_sum(values):
    return jnp.sum(values.astype(F32), axis=0, keepdims=True)


def ring(off):
    return lax.rem(lax.axis_index("seq") + off + 4, 4)


def ring_signal():
    for off in (1, 2, 3):
        pl.semaphore_signal(
            pltpu.get_barrier_semaphore(),
            inc=1,
            device_id=(lax.axis_index("chain"), ring(off)),
            device_id_type=MESH,
        )


def push(started, src, dst, s_sem, r_sem, off):
    copy = pltpu.make_async_remote_copy(
        src_ref=src,
        dst_ref=dst,
        send_sem=s_sem,
        recv_sem=r_sem,
        device_id=(lax.axis_index("chain"), ring(off)),
        device_id_type=MESH,
    )
    copy.start()
    started.append(copy)
    return copy


def fetch(pairs, sems):
    copies = [pltpu.make_async_copy(src, dst, sems.at[i]) for i, (src, dst) in enumerate(pairs)]
    for copy in copies:
        copy.start()
    return copies


QUERY_B, VALUE_B, MIXER_B, GAIN_1, SHIFT_1, OUTER_B, GAIN_2, SHIFT_2 = range(8)


def shape(dims, kind=LOW):
    return jax.ShapeDtypeStruct(dims, kind)


VMEM = pl.BlockSpec(memory_space=pltpu.VMEM)
ANY = pl.BlockSpec(memory_space=pl.ANY)
DMA = pltpu.SemaphoreType.DMA


def weight_buffers():
    return [pltpu.VMEM((MODEL, MODEL), LOW) for _ in range(4)] + [
        pltpu.VMEM((MODEL, INNER), LOW),
        pltpu.VMEM((INNER, MODEL), LOW),
    ]


HALF = 384
CHUNK = 96
SUB = 48
SIDE = 384
ORDERS = (("x", "y", "z"), ("y", "z", "x"), ("z", "x", "y"))


def places():
    chain = lax.axis_index("chain")
    return {
        "x": chain // 8,
        "y": lax.rem(chain // 2, 4),
        "z": lax.axis_index("seq"),
        "core": lax.rem(chain, 2),
    }


def peer(at, axis, off):
    at = dict(at)
    size = 2 if axis == "core" else 4
    at[axis] = lax.rem(at[axis] + off + size, size)
    return ((at["x"] * 4 + at["y"]) * 2 + at["core"], at["z"])


def greet(at, peers):
    barrier = pltpu.get_barrier_semaphore()
    for axis, off in peers:
        pl.semaphore_signal(barrier, inc=1, device_id=peer(at, axis, off), device_id_type=MESH)


ALL_PEERS = [("core", 1)] + [(axis, off) for axis in "xyz" for off in (1, 2, 3)]


def add_rows(out, out_start, terms, rows, step=48):
    def body(i, carry):
        base = i * step
        total = None
        for ref, start in terms:
            term = ref[pl.ds(pl.multiple_of(start + base, 16), step), :].astype(jnp.float32)
            total = term if total is None else total + term
        out[pl.ds(pl.multiple_of(out_start + base, 16), step), :] = total.astype(out.dtype)
        return carry

    lax.fori_loop(0, rows // step, body, 0)


def layer_kernel(
    resets, tok, cot, docs, init_in, offset_in, query_b, value_b, mixer_b, gain_1, shift_1, outer_b,
    gain_2, shift_2, inner_in, wq_h, wk_h, wv_h, wm_h, wi_h, wo_h,
    out_h, orow, ow, xm, ub_h, act_h, dz_h, df_h, da_h, dh1_h, sums, inner_sum,
    drow, dmem, ubw, gw, dzw, dfw, daw, small, dlast, mlast, dh1w,
    out, ub, act, dz, df, da, dh1, kv, probs, h1w, zw, h2w, vec, inner_b,
    wq, wk, wv, wm, wi, wo, wown, vown, sbuf, lab, bias, osend, owsend, init, offset,
    slope, total, unit_1, inverse_1, dout, doh, dow, acc, dsend, msend, wide,
    w_sem, h_sem, q_s, q_r, o_s, o_r, m_s, m_r, l_s, l_r, d_s, d_r, x_s, x_r, mm_s, mm_r,
):
    z = lax.axis_index("seq")
    fetched = fetch(
        [(wq_h, wq), (wk_h, wk), (wv_h, wv), (wm_h, wm), (wi_h, wi), (wo_h, wo)], w_sem
    )
    started = []
    ring_signal()
    vectors = (query_b, value_b, mixer_b, gain_1, shift_1, outer_b, gain_2, shift_2)
    for i, ref in enumerate(vectors):
        vec[i : i + 1, :] = ref[...].astype(F32).reshape(1, MODEL)
    inner_b[...] = inner_in[...].astype(F32).reshape(1, INNER)
    for padded, ref in ((init, init_in), (offset, offset_in)):
        padded[...] = jnp.zeros((PAD, MODEL), LOW)
        padded[0:SLOTS, :] = ref[...]
    lab[pl.ds(z, 1)] = docs[...][None]
    tokens = tok[...].reshape(ROWS, MODEL)
    fetched[0].wait()
    queries = ((dot(tokens, wq[...]) + vec[QUERY_B : QUERY_B + 1, :]) * SCALE).astype(LOW)
    for g in range(4):
        for s in range(SEGS):
            sbuf[g, s, :, 0:GROUP] = queries[
                s * BLOCK : (s + 1) * BLOCK, g * GROUP : (g + 1) * GROUP
            ]
    fetched[1].wait()
    keys = dot(tokens, wk[...]).astype(LOW)
    for g in range(4):
        for s in range(SEGS):
            sbuf[g, s, :, GROUP : 2 * GROUP] = keys[
                s * BLOCK : (s + 1) * BLOCK, g * GROUP : (g + 1) * GROUP
            ]
    fetched[2].wait()
    values = (dot(tokens, wv[...]) + vec[VALUE_B : VALUE_B + 1, :]).astype(LOW)
    for g in range(4):
        for s in range(SEGS):
            sbuf[g, s, :, 2 * GROUP :] = values[
                s * BLOCK : (s + 1) * BLOCK, g * GROUP : (g + 1) * GROUP
            ]
    here = pl.ds(pl.multiple_of(z * BLOCK, BLOCK), BLOCK)
    row_copies = {}

    def send_rows(s):
        row_copies[s] = [
            push(
                started, sbuf.at[ring(d), s], kv.at[s, here],
                q_s.at[s, d - 1], q_r.at[s, d - 1], d,
            )
            for d in (1, 2, 3)
        ]

    pl.semaphore_wait(pltpu.get_barrier_semaphore(), 3)
    label_copies = [
        push(started, docs, lab.at[z], l_s.at[d - 1], l_r.at[d - 1], d) for d in (1, 2, 3)
    ]
    send_rows(0)
    send_rows(1)
    for s in range(SEGS):
        kv[s, here, :] = sbuf[z, s]
        kv[s, TOKENS + MEMORY :, :] = jnp.zeros((KEYS - TOKENS - MEMORY, TRIPLE), LOW)
    for g in range(4):

        @pl.when(z == g)
        def _():
            cut = slice(g * GROUP, (g + 1) * GROUP)
            wown[:, 0:GROUP] = wq[:, cut]
            wown[:, GROUP : 2 * GROUP] = wk[:, cut]
            wown[:, 2 * GROUP :] = wv[:, cut]
            vown[0:1, 0:GROUP] = vec[QUERY_B : QUERY_B + 1, cut]
            vown[0:1, GROUP : 2 * GROUP] = jnp.zeros((1, GROUP), F32)
            vown[0:1, 2 * GROUP :] = vec[VALUE_B : VALUE_B + 1, cut]

    lane = lax.broadcasted_iota(jnp.int32, (1, TRIPLE), 1)
    factor = jnp.where(lane < GROUP, SCALE, 1.0)
    slot = lax.broadcasted_iota(jnp.int32, (PAD, MODEL), 0)
    key_lane = lax.broadcasted_iota(jnp.int32, (PAD, KEYS), 1)
    filled = (key_lane < TOKENS + SLOTS) | (
        (key_lane >= TOKENS + PAD) & (key_lane < TOKENS + PAD + SLOTS)
    )
    write_bias = jnp.where(filled, 0.0, HIDDEN)

    head_lane = lax.broadcasted_iota(jnp.int32, (1, GROUP), 1)
    in_head = [(head_lane >= h * HEAD) & (head_lane < (h + 1) * HEAD) for h in range(MINE)]

    def spread(block):
        none = jnp.zeros_like(block)
        return jnp.concatenate([jnp.where(own, block, none) for own in in_head], axis=0)

    def gather_heads(stacked, rows):
        picked = stacked[0:rows]
        for h in range(1, MINE):
            picked = jnp.where(in_head[h], stacked[h * rows : (h + 1) * rows], picked)
        return picked

    def attend(query_rows, mask, s, row_at, rows):
        scores = dot_t(spread(query_rows), kv[s, :, GROUP : 2 * GROUP])
        scores = scores + jnp.concatenate([mask] * MINE, axis=0)
        weights = jnp.exp(scores - jnp.max(scores, axis=-1, keepdims=True))
        total = jnp.sum(weights, axis=-1, keepdims=True)
        prob = (weights * (1.0 / total)).astype(LOW)
        for h in range(MINE):
            probs[s, h, pl.ds(row_at, rows), :] = prob[h * rows : (h + 1) * rows]
        return gather_heads(dot(prob, kv[s, :, 2 * GROUP :]), rows).astype(LOW)

    memory = init[...]
    for copy in label_copies:
        copy.wait_recv()
    for s in range(SEGS):
        for i in range(4):
            column = jnp.transpose(jnp.broadcast_to(lab[i, s : s + 1, :].astype(F32), (BLOCK, BLOCK)))
            for j in range(4):
                row = jnp.broadcast_to(lab[j, s : s + 1, :].astype(F32), (BLOCK, BLOCK))
                bias[s, i * BLOCK : (i + 1) * BLOCK, j * BLOCK : (j + 1) * BLOCK] = jnp.where(
                    column == row, 0.0, HIDDEN
                ).astype(LOW)
            bias[s, i * BLOCK : (i + 1) * BLOCK, TOKENS:] = jnp.broadcast_to(
                write_bias[0:1, TOKENS:], (BLOCK, BLOCK)
            ).astype(LOW)
    out_copies = []
    for s in range(SEGS):
        written_in = (memory.astype(F32) + offset[...].astype(F32)).astype(LOW)
        xm[s, 0:PAD, :] = written_in
        xm[s, PAD:, :] = memory
        kv[s, TOKENS : TOKENS + MEMORY, :] = (
            (dot(xm[s], wown[...]) + vown[0:1, :]) * factor
        ).astype(LOW)
        for copy in row_copies[s]:
            copy.wait_recv()
        if s < SEGS - 1:
            mixed = attend(kv[s, TOKENS : TOKENS + PAD, 0:GROUP], write_bias, s, TOKENS, PAD)
            owsend[s] = mixed
            ow[s, pl.ds(z, 1)] = mixed[None]
            write_copies = [
                push(started, owsend.at[s], ow.at[s, z], m_s.at[s, d - 1], m_r.at[s, d - 1], d)
                for d in (1, 2, 3)
            ]
            if s == 0:
                send_rows(2)

        def block(i, carry):
            row_at = pl.multiple_of(i * BLOCK, BLOCK)
            rows = pl.ds(row_at, BLOCK)
            osend[s, i] = attend(kv[s, rows, 0:GROUP], bias[s, rows, :].astype(F32), s, row_at, BLOCK)
            return carry

        lax.fori_loop(0, 4, block, 0)
        part = slice(s * BLOCK, (s + 1) * BLOCK)
        out_copies += [
            push(
                started, osend.at[s, ring(d)], orow.at[z, part],
                o_s.at[s, d - 1], o_r.at[s, d - 1], d,
            )
            for d in (1, 2, 3)
        ]
        orow[z, part, :] = osend[s, z]
        if s < SEGS - 1:
            if s == 0:
                for copy in fetched[3:]:
                    copy.wait()
            for copy in write_copies:
                copy.wait_recv()
            hidden = xm[s, 0:PAD, :].astype(F32) + vec[MIXER_B : MIXER_B + 1, :]
            for g in range(4):
                hidden = hidden + dot(ow[s, g], wm[g * GROUP : (g + 1) * GROUP, :])
            h1w[s] = hidden
            unit, _ = norm_parts(hidden)
            upper = unit * vec[GAIN_1 : GAIN_1 + 1, :] + vec[SHIFT_1 : SHIFT_1 + 1, :]
            inner = dot(upper.astype(LOW), wi[...]) + inner_b[...]
            zw[s] = inner
            active, _ = gelu_parts(inner)
            hidden = upper + dot(active.astype(LOW), wo[...]) + vec[OUTER_B : OUTER_B + 1, :]
            h2w[s] = hidden
            unit, _ = norm_parts(hidden)
            result = unit * vec[GAIN_2 : GAIN_2 + 1, :] + vec[SHIFT_2 : SHIFT_2 + 1, :]
            flag = jnp.broadcast_to(resets[0:1, s : s + 1], (PAD, MODEL))
            result = jnp.where(flag > 0, init[...].astype(F32), result)
            memory = jnp.where(slot < SLOTS, result, 0.0).astype(LOW)
    for copy in out_copies:
        copy.wait_recv()
    first_gain = vec[GAIN_1 : GAIN_1 + 1, :]
    second_gain = vec[GAIN_2 : GAIN_2 + 1, :]
    hidden = tok[...].reshape(ROWS, MODEL).astype(F32) + vec[MIXER_B : MIXER_B + 1, :]
    for g in range(4):
        hidden = hidden + dot(orow[g], wm[g * GROUP : (g + 1) * GROUP, :])
    unit, inverse = norm_parts(hidden)
    unit_1[...] = unit
    inverse_1[...] = inverse
    upper = unit * first_gain + vec[SHIFT_1 : SHIFT_1 + 1, :]
    ub[...] = upper.astype(LOW)
    total[...] = upper + vec[OUTER_B : OUTER_B + 1, :]

    def ahead(j):
        cut = pl.ds(j * MODEL, MODEL)
        inner = dot(ub[...], wi[:, cut]) + inner_b[:, cut]
        active, slant = gelu_parts(inner)
        active = active.astype(LOW)
        act[:, cut] = active
        slope[:, cut] = slant.astype(LOW)
        total[...] += dot(active, wo[cut, :])

    for j in range(INNER // MODEL):
        ahead(j)
    unit, inverse = norm_parts(total[...])
    result = unit * second_gain + vec[SHIFT_2 : SHIFT_2 + 1, :]
    out[...] = result.astype(LOW).reshape(1, SEGS, BLOCK, MODEL)
    upstream = cot[...].reshape(ROWS, MODEL).astype(F32)
    sums[GAIN_2 : GAIN_2 + 1, :] = column_sum(upstream * unit)
    sums[SHIFT_2 : SHIFT_2 + 1, :] = column_sum(upstream)
    d_hidden = norm_back(upstream, unit, inverse, second_gain)
    total[...] = d_hidden
    d_low = d_hidden.astype(LOW)
    df[...] = d_low
    sums[OUTER_B : OUTER_B + 1, :] = column_sum(d_low)

    def back(j):
        cut = pl.ds(j * MODEL, MODEL)
        d_inner = (dot_t(df[...], wo[cut, :]) * slope[:, cut].astype(F32)).astype(LOW)
        dz[:, cut] = d_inner
        inner_sum[:, cut] = column_sum(d_inner)
        total[...] += dot_t(d_inner, wi[:, cut])

    for j in range(INNER // MODEL):
        back(j)
    upstream = total[...]
    unit = unit_1[...]
    sums[GAIN_1 : GAIN_1 + 1, :] = column_sum(upstream * unit)
    sums[SHIFT_1 : SHIFT_1 + 1, :] = column_sum(upstream)
    d_hidden = norm_back(upstream, unit, inverse_1[...], first_gain)
    dh1[...] = d_hidden
    d_low = d_hidden.astype(LOW)
    da[...] = d_low
    sums[MIXER_B : MIXER_B + 1, :] = column_sum(d_low)
    sums[QUERY_B : QUERY_B + 2, :] = jnp.zeros((2, MODEL), F32)
    for g in range(4):
        dout[g] = dot_t(d_low, wm[g * GROUP : (g + 1) * GROUP, :]).astype(LOW)
    leaving = fetch(
        [
            (out, out_h), (ub, ub_h), (act, act_h), (dz, dz_h), (df, df_h), (da, da_h),
            (dh1, dh1_h),
        ],
        h_sem,
    )
    in_copies = {}
    for s in reversed(range(SEGS)):
        part = slice(s * BLOCK, (s + 1) * BLOCK)
        in_copies[s] = [
            push(
                started, dout.at[ring(d), part], doh.at[s, here],
                d_s.at[s, d - 1], d_r.at[s, d - 1], d,
            )
            for d in (1, 2, 3)
        ]
        doh[s, here, :] = dout[z, part, :]

    def rows_back(s, d_rows, row_at, rows):
        part = slice(row_at, row_at + rows)
        key_rows = kv[s, :, GROUP : 2 * GROUP]
        d_spread = spread(d_rows)
        prob = jnp.concatenate([probs[s, h, part, :] for h in range(MINE)], axis=0)
        wide_prob = prob.astype(F32)
        product = wide_prob * dot_t(d_spread, kv[s, :, 2 * GROUP :])
        delta = jnp.sum(product, axis=-1, keepdims=True)
        d_scores = (product - wide_prob * delta).astype(LOW)
        d_query = gather_heads(dot(d_scores, key_rows) * SCALE, rows).astype(LOW)
        d_key = t_dot(d_scores, spread(kv[s, part, 0:GROUP]))
        return d_query, d_key, t_dot(prob, d_spread)

    def tokens_back(s):
        for copy in in_copies[s]:
            copy.wait_recv()
        half = TOKENS // 2
        for i in range(2):
            part = slice(i * half, (i + 1) * half)
            d_query, d_key, d_value = rows_back(s, doh[s, part, :], i * half, half)
            dsend[s, part, 0:GROUP] = d_query
            if i == 0:
                acc[:, 0:GROUP] = d_key
                acc[:, GROUP:] = d_value
            else:
                acc[:, 0:GROUP] += d_key
                acc[:, GROUP:] += d_value

    def writes_back(s):
        d_query, d_key, d_value = rows_back(s, dow[...], TOKENS, PAD)
        msend[s, 0:PAD, 0:GROUP] = d_query
        acc[:, 0:GROUP] += d_key
        acc[:, GROUP:] += d_value

    mem_copies = {}
    back_copies = []

    def finish(s):
        if s == SEGS - 1:
            msend[s, :, 0:GROUP] = jnp.zeros((MEMORY, GROUP), LOW)
        else:
            msend[s, PAD:, 0:GROUP] = jnp.zeros((PAD, GROUP), LOW)
        msend[s, :, GROUP:] = acc[TOKENS : TOKENS + MEMORY, :].astype(LOW)
        mem_copies[s] = [
            push(started, msend.at[s], dmem.at[s - 1, z], mm_s.at[s, d - 1], mm_r.at[s, d - 1], d)
            for d in (1, 2, 3)
        ]
        dmem[s - 1, z] = msend[s]
        dsend[s, :, GROUP:] = acc[0:TOKENS, :].astype(LOW)
        kept = slice((s - 1) * BLOCK, s * BLOCK)
        for d in (1, 2, 3):
            there = pl.ds(pl.multiple_of(ring(d) * BLOCK, BLOCK), BLOCK)
            back_copies.append(
                push(
                    started, dsend.at[s, there], drow.at[z, kept],
                    x_s.at[s, d - 1], x_r.at[s, d - 1], d,
                )
            )
        drow[z, kept, :] = dsend[s, here, :]

    parts = {}

    def add(name, value):
        parts[name] = value if name not in parts else parts[name] + value

    saved = {}

    def memory_back(s):
        for copy in mem_copies[s]:
            copy.wait_recv()
        for g in range(4):
            for t in range(3):
                wide[t, :, g * GROUP : (g + 1) * GROUP] = dmem[
                    s - 1, g, :, t * GROUP : (t + 1) * GROUP
                ]
        d_rows = dot_t(wide[0], wq[...]) + dot_t(wide[1], wk[...]) + dot_t(wide[2], wv[...])
        write = d_rows[0:PAD]
        if s < SEGS - 1:
            write = write + saved[s]
        grad = write + d_rows[PAD:]
        add("offset", write)
        add("norm", jnp.sum(jnp.sum(grad * grad, axis=0, keepdims=True), axis=1, keepdims=True))
        flag = jnp.broadcast_to(resets[0:1, s - 1 : s], (PAD, MODEL)) > 0
        add("init", jnp.where(flag, grad, 0.0))
        return jnp.where(flag, 0.0, grad)

    def layer_back(s, upstream):
        unit, inverse = norm_parts(h2w[s])
        add("gain_2", column_sum(upstream * unit))
        add("shift_2", column_sum(upstream))
        d_second = norm_back(upstream, unit, inverse, second_gain)
        d_low = d_second.astype(LOW)
        dfw[s] = d_low
        add("outer", column_sum(d_low))
        active, slant = gelu_parts(zw[s])
        gw[s] = active.astype(LOW)
        d_inner = (dot_t(d_low, wo[...]) * slant).astype(LOW)
        dzw[s] = d_inner
        add("inner", column_sum(d_inner))
        unit, inverse = norm_parts(h1w[s])
        ubw[s] = (unit * first_gain + vec[SHIFT_1 : SHIFT_1 + 1, :]).astype(LOW)
        d_upper = dot_t(d_inner, wi[...]) + d_second
        add("gain_1", column_sum(d_upper * unit))
        add("shift_1", column_sum(d_upper))
        d_first = norm_back(d_upper, unit, inverse, first_gain)
        saved[s] = d_first
        if s == 0:
            dh1w[...] = d_first
        d_low = d_first.astype(LOW)
        daw[s] = d_low
        add("mixer", column_sum(d_low))
        own = pl.ds(pl.multiple_of(z * GROUP, HEAD), GROUP)
        dow[...] = dot_t(d_low, wm[own, :]).astype(LOW)

    tokens_back(2)
    finish(2)
    tokens_back(1)
    layer_back(1, memory_back(2))
    writes_back(1)
    finish(1)
    tokens_back(0)
    layer_back(0, memory_back(1))
    writes_back(0)
    msend[0, PAD:, 0:GROUP] = jnp.zeros((PAD, GROUP), LOW)
    msend[0, :, GROUP:] = acc[TOKENS : TOKENS + MEMORY, :].astype(LOW)
    dsend[0, :, GROUP:] = acc[0:TOKENS, :].astype(LOW)
    dlast[...] = dsend[0]
    mlast[...] = msend[0]
    quarter = 0.25
    row = lax.broadcasted_iota(jnp.int32, (24, MODEL), 0)
    zero = jnp.zeros((1, MODEL), F32)
    small[0:8, :] = quarter * jnp.concatenate(
        [zero, zero]
        + [parts[n] for n in ("mixer", "gain_1", "shift_1", "outer", "gain_2", "shift_2")],
        axis=0,
    )
    small[8:16, :] = quarter * jnp.concatenate(
        [parts["inner"][:, i * MODEL : (i + 1) * MODEL] for i in range(4)] + [zero] * 4, axis=0
    )
    small[16:40, :] = quarter * parts["init"][0:24]
    small[40:64, :] = quarter * (
        parts["offset"][0:24]
        + jnp.where(row >= SLOTS, jnp.broadcast_to(parts["norm"], (24, MODEL)), 0.0)
    )
    for copy in back_copies:
        copy.wait_recv()
    for copy in leaving:
        copy.wait()
    for copy in started:
        copy.wait_send()
def layer(resets, tok, cot, docs, init, offset, vectors, inner_b, weights):
    def buffer(*dims):
        return pltpu.VMEM(dims, LOW)

    def wide_buffer(*dims):
        return pltpu.VMEM(dims, F32)

    by_segment = [DMA((SEGS, 3)), DMA((SEGS, 3))]
    return pl.pallas_call(
        layer_kernel,
        out_shape=(
            shape((1, SEGS, BLOCK, MODEL)),
            shape((4, ROWS, GROUP)),
            shape((2, 4, PAD, GROUP)),
            shape((SEGS, MEMORY, MODEL)),
            shape((ROWS, MODEL)),
            shape((ROWS, INNER)),
            shape((ROWS, INNER)),
            shape((ROWS, MODEL)),
            shape((ROWS, MODEL)),
            shape((ROWS, MODEL), F32),
            shape((8, MODEL), F32),
            shape((1, INNER), F32),
            shape((4, ROWS - BLOCK, TRIPLE)),
            shape((SEGS - 1, 4, MEMORY, TRIPLE)),
            shape((2, PAD, MODEL)),
            shape((2, PAD, INNER)),
            shape((2, PAD, INNER)),
            shape((2, PAD, MODEL)),
            shape((2, PAD, MODEL)),
            shape((64, MODEL), F32),
            shape((TOKENS, TRIPLE)),
            shape((MEMORY, TRIPLE)),
            shape((PAD, MODEL), F32),
        ),
        in_specs=[VMEM] * 15 + [ANY] * 6,
        out_specs=(ANY, VMEM, VMEM, VMEM) + (ANY,) * 6 + (VMEM,) * 13,
        scratch_shapes=[
            buffer(1, SEGS, BLOCK, MODEL),
            buffer(ROWS, MODEL),
            buffer(ROWS, INNER),
            buffer(ROWS, INNER),
            buffer(ROWS, MODEL),
            buffer(ROWS, MODEL),
            wide_buffer(ROWS, MODEL),
            buffer(SEGS, KEYS, TRIPLE),
            buffer(SEGS, MINE, QUERIES, KEYS),
            wide_buffer(2, PAD, MODEL),
            wide_buffer(2, PAD, INNER),
            wide_buffer(2, PAD, MODEL),
            wide_buffer(8, MODEL),
            wide_buffer(1, INNER),
        ]
        + weight_buffers()
        + [
            buffer(MODEL, TRIPLE),
            wide_buffer(8, TRIPLE),
            buffer(4, SEGS, BLOCK, TRIPLE),
            pltpu.VMEM((4, SEGS, BLOCK), jnp.int32),
            buffer(SEGS, TOKENS, KEYS),
            buffer(SEGS, 4, BLOCK, GROUP),
            buffer(2, PAD, GROUP),
            buffer(PAD, MODEL),
            buffer(PAD, MODEL),
            buffer(ROWS, INNER),
            wide_buffer(ROWS, MODEL),
            wide_buffer(ROWS, MODEL),
            wide_buffer(ROWS, 1),
            buffer(4, ROWS, GROUP),
            buffer(SEGS, TOKENS, GROUP),
            buffer(PAD, GROUP),
            wide_buffer(KEYS, 2 * GROUP),
            buffer(SEGS, TOKENS, TRIPLE),
            buffer(SEGS, MEMORY, TRIPLE),
            buffer(3, MEMORY, MODEL),
            DMA((6,)),
            DMA((7,)),
        ]
        + by_segment * 2
        + [DMA((2, 3)), DMA((2, 3)), DMA((3,)), DMA((3,))]
        + by_segment * 3,
        compiler_params=pltpu.CompilerParams(
            collective_id=1, has_side_effects=True, vmem_limit_bytes=62 << 20
        ),
        name="layer",
    )(resets, tok, cot, docs, init, offset, *vectors, inner_b, *weights)


FULL = ROWS + MEMORY
MOST = ROWS + PAD
UNITS = ((4, 5, 6), (7, 8, 9), (0, 1, 2), (10, 11, 3))


def finish_kernel(
    sums, inner_sum, small, ubw, gw, dzw, dfw, daw, dsend, msend, dh1w,
    ub_h, act_h, dz_h, df_h, da_h, wq_h, wk_h, wv_h, tok_h, xm_h, drow_h, dmem_h, orow_h, ow_h, dh1_h,
    packed, input_grad, ext,
    tok, xm, drow, orow, ow, dh1, ub, act, dz, df, da, wq, wk, wv, rows, triple, mixed,
    drow0, dmall, wide, g, crecv, r1, r2, r3, slots, own_ext, ecore, ex, ey, ez,
    w_sem, x_s, x_r, m_s, m_r, c_s, c_r, a_s, a_r, b_s, b_r, d_s, d_r, e_s, e_r, f_s, f_r,
    loc, free, n_s, n_r, o_s, o_r, gc_s, gc_r, t_s, t_r,
):
    at = places()
    z = at["z"]
    core = at["core"]
    top = pl.ds(0, ROWS)
    fetched = fetch(
        [
            (ub_h, ub.at[top]), (dz_h, dz.at[top]), (act_h, act.at[top]), (df_h, df.at[top]),
            (da_h, da.at[top]), (wq_h, wq), (wk_h, wk), (wv_h, wv), (tok_h, tok), (xm_h, xm),
            (drow_h, drow), (dmem_h, dmall.at[pl.ds(1, 2)]), (orow_h, orow), (ow_h, ow),
            (dh1_h, dh1),
        ],
        w_sem,
    )
    greet(at, ALL_PEERS)
    started = []

    def send(src, dst, s_sem, r_sem, axis, off):
        copy = pltpu.make_async_remote_copy(
            src_ref=src, dst_ref=dst, send_sem=s_sem, recv_sem=r_sem,
            device_id=peer(at, axis, off), device_id_type=MESH,
        )
        copy.start()
        started.append(copy)
        return copy

    def turn(value, off):
        return lax.rem(value + off + 4, 4)

    def ds(start, size):
        return pl.ds(pl.multiple_of(start, 16), size)

    place1 = [at[order[0]] for order in ORDERS]
    place2 = [at[order[1]] for order in ORDERS]
    place3 = [at[order[2]] for order in ORDERS]
    live = {}

    def sub_of(ref, start, n):
        side = pl.ds(pl.multiple_of(lax.rem(n, 2) * SIDE, 128), SIDE)
        return ref.at[ds(start + (n // 2) * SUB, SUB), side]

    def home(p, off):
        return core * HALF + turn(place1[p], off) * CHUNK

    def block_done(u, p):
        b = UNITS[u][p]
        live["core", u, p] = send(
            g.at[b, ds((1 - core) * HALF, HALF)], crecv.at[u, p],
            c_s.at[u, p], c_r.at[u, p], "core", 1,
        )
        started.pop()

    def stage1(u):
        for p in range(3):
            b = UNITS[u][p]
            live["core", u, p].wait_recv()
            held = crecv.at[u, p]
            start = turn(place1[p], 2) * CHUNK
            add_rows(held, start, [(g.at[b], core * HALF + start), (held, start)], CHUNK)
            live["a", u, p] = [
                send(
                    held.at[ds(start + i * SUB, SUB)], r1.at[u, p, i],
                    a_s.at[u, p, i], a_r.at[u, p, i], ORDERS[p][0], 1 + 2 * i,
                )
                for i in range(2)
            ]
        for p in range(3):
            b = UNITS[u][p]
            held = crecv.at[u, p]
            for off in (1, 3, 0):
                start = turn(place1[p], off) * CHUNK
                add_rows(held, start, [(g.at[b], core * HALF + start), (held, start)], CHUNK)
            live["core", u, p].wait_send()
        pl.semaphore_signal(
            free.at[u], inc=1, device_id=peer(at, "core", 1), device_id_type=MESH
        )

    def stage2(u):
        for p in range(3):
            held = crecv.at[u, p]
            live["b", u, p] = []
            for i in range(2):
                start = turn(place1[p], 1 + 2 * i) * CHUNK
                live["a", u, p][i].wait_recv()
                half = start + i * SUB
                add_rows(held, half, [(held, half), (r1.at[u, p, i], 0)], SUB)
                live["b", u, p].append(
                    send(
                        held.at[ds(start, CHUNK)], r2.at[u, p, i],
                        b_s.at[u, p, i], b_r.at[u, p, i], ORDERS[p][0], 1 + 2 * i,
                    )
                )

    def stage3(u):
        for p in range(3):
            held = crecv.at[u, p]
            start = place1[p] * CHUNK
            for copy in live["b", u, p]:
                copy.wait_recv()
            add_rows(held, start, [(held, start), (r2.at[u, p, 0], 0), (r2.at[u, p, 1], 0)], CHUNK)
            live["d", u, p] = [
                send(
                    sub_of(held, start, turn(place2[p], d)), r3.at[u, p, d - 1],
                    d_s.at[u, p, d - 1], d_r.at[u, p, d - 1], ORDERS[p][1], d,
                )
                for d in (1, 2, 3)
            ]

    def stage4(u):
        for p in range(3):
            for copy in live["d", u, p]:
                copy.wait_recv()
            total = sub_of(crecv.at[u, p], place1[p] * CHUNK, place2[p])[...].astype(F32)
            for d in range(3):
                total = total + r3[u, p, d].astype(F32)
            slots[u, p, pl.ds(place3[p], 1)] = total.astype(LOW)[None]
            live["e", u, p] = [
                send(
                    slots.at[u, p, place3[p]], slots.at[u, p, place3[p]],
                    e_s.at[u, p, d - 1], e_r.at[u, p, d - 1], ORDERS[p][2], d,
                )
                for d in (1, 2, 3)
            ]

    def stage5(u):
        for p in range(3):
            for copy in live["e", u, p]:
                copy.wait_recv()
            total = slots[u, p, 0].astype(F32)
            for i in range(1, 4):
                total = total + slots[u, p, i].astype(F32)
            target = sub_of(g.at[UNITS[u][p]], home(p, 0), place2[p])
            target[...] = total.astype(LOW)
            live["f", u, p] = [
                send(target, target, f_s.at[u, p, d - 1], f_r.at[u, p, d - 1], ORDERS[p][1], d)
                for d in (1, 2, 3)
            ]

    def across(u, p, j, start, count):
        piece = g.at[UNITS[u][p], ds(start, count)]
        live["gc", u, p, j] = send(piece, piece, gc_s.at[u, p, j], gc_r.at[u, p, j], "core", 1)

    def stage6(u):
        pl.semaphore_wait(free.at[u], 1)
        for p in range(3):
            for copy in live["f", u, p]:
                copy.wait_recv()
            piece = g.at[UNITS[u][p], ds(home(p, 0), CHUNK)]
            live["n", u, p] = [
                send(piece, piece, n_s.at[u, p, i], n_r.at[u, p, i], ORDERS[p][0], 1 + 2 * i)
                for i in range(2)
            ]
            across(u, p, 0, home(p, 0), CHUNK)

    def stage7(u):
        for p in range(3):
            live["o", u, p] = []
            for i in range(2):
                live["n", u, p][i].wait_recv()
                start = home(p, 3 - 2 * i)
                piece = g.at[UNITS[u][p], ds(start + i * SUB, SUB)]
                live["o", u, p].append(
                    send(piece, piece, o_s.at[u, p, i], o_r.at[u, p, i], ORDERS[p][0], 1 + 2 * i)
                )
                across(u, p, 1 + i, start, CHUNK)

    def stage8(u):
        for p in range(3):
            for i in range(2):
                live["o", u, p][i].wait_recv()
                across(u, p, 3 + i, home(p, 2) + i * SUB, SUB)

    stores = []

    def stage9(u):
        for p in range(3):
            for j in range(5):
                live["gc", u, p, j].wait_recv()
            b = UNITS[u][p]
            stores.append(
                pltpu.make_async_copy(
                    g.at[b], packed.at[pl.ds(b * MODEL, MODEL)], loc.at[u, p]
                )
            )
            stores[-1].start()

    stages = {
        1: stage1, 2: stage2, 3: stage3, 4: stage4, 5: stage5, 6: stage6, 7: stage7, 8: stage8,
        9: stage9,
    }

    def wave(*pairs):
        for u, k in pairs:
            stages[k](u)

    low_at = jnp.minimum(z, 1)
    low_keep = (z < 2).astype(F32).astype(LOW)
    at_seg = jnp.minimum(z, 2)
    keep = (z < SEGS).astype(F32).astype(LOW)

    def inner_block(j):
        g[4 + j] = t_dot(ub[...], dz[:, j * MODEL : (j + 1) * MODEL]).astype(LOW)

    def outer_block(j):
        g[8 + j] = t_dot(act[:, j * MODEL : (j + 1) * MODEL], df[...]).astype(LOW)

    def mixer_block():
        for i in range(4):
            mixed[i, 0:ROWS, :] = orow[i]
            mixed[i, ROWS:, :] = ow[low_at, i]
        for i in range(4):
            g[3, i * GROUP : (i + 1) * GROUP, :] = t_dot(mixed[i], da[...]).astype(LOW)

    drow0[z] = dsend[ds(z * BLOCK, BLOCK), :]
    dmall[0, z] = msend[...]
    ub[ROWS:, :] = ubw[low_at]
    act[ROWS:, :] = gw[low_at]
    dz[ROWS:, :] = dzw[low_at] * low_keep
    df[ROWS:, :] = dfw[low_at] * low_keep
    da[ROWS:, :] = daw[low_at] * low_keep
    for copy in fetched[:2]:
        copy.wait()
    inner_block(0)
    pl.semaphore_wait(pltpu.get_barrier_semaphore(), len(ALL_PEERS))
    block_done(0, 0)
    row_copies = []
    for d in (1, 2, 3):
        there = ds(ring(d) * BLOCK, BLOCK)
        row_copies.append(
            send(dsend.at[there], drow0.at[z], x_s.at[d - 1], x_r.at[d - 1], "z", d)
        )
        row_copies.append(
            send(msend, dmall.at[0, z], m_s.at[d - 1], m_r.at[d - 1], "z", d)
        )
    for j in (1, 2):
        inner_block(j)
        block_done(0, j)
    inner_block(3)
    block_done(1, 0)
    wave((0, 1))
    for copy in fetched[2:4]:
        copy.wait()
    for j in range(2):
        outer_block(j)
        block_done(1, 1 + j)
    wave((0, 2), (1, 1))
    for copy in fetched[8:]:
        copy.wait()
    rows[0:ROWS, :] = tok[...].reshape(ROWS, MODEL)
    rows[ROWS:, :] = xm[at_seg]
    for copy in row_copies:
        copy.wait_recv()
    for i in range(4):
        for t in range(3):
            cut = slice(i * GROUP, (i + 1) * GROUP)
            part = slice(t * GROUP, (t + 1) * GROUP)
            triple[t, 0:BLOCK, cut] = drow0[i, :, part]
            triple[t, BLOCK:ROWS, cut] = drow[i, :, part]
            triple[t, ROWS:, cut] = dmall[at_seg, i, :, part] * keep
            wide[t, :, cut] = dmall[0, i, :, part]
    for t in range(3):
        g[t] = t_dot(rows[...], triple[t]).astype(LOW)
        block_done(2, t)
    wave((0, 3), (1, 2), (2, 1))
    for j in range(2, 4):
        outer_block(j)
        block_done(3, j - 2)
    fetched[4].wait()
    mixer_block()
    block_done(3, 2)
    wave((0, 4), (1, 3), (2, 2), (3, 1))
    for copy in fetched[5:8]:
        copy.wait()
    d_rows = dot_t(wide[0], wq[...]) + dot_t(wide[1], wk[...]) + dot_t(wide[2], wv[...])
    write = d_rows[0:PAD] + dh1w[...]
    grad = write + d_rows[PAD:]
    norm = jnp.sum(jnp.sum(grad * grad, axis=0, keepdims=True), axis=1, keepdims=True)
    own_ext[0:8, :] = small[0:8, :] + sums[...]
    own_ext[8:16, :] = small[8:16, :] + jnp.concatenate(
        [inner_sum[:, i * MODEL : (i + 1) * MODEL] for i in range(4)]
        + [jnp.zeros((4, MODEL), F32)],
        axis=0,
    )
    own_ext[QUERY_B : QUERY_B + 1, :] += column_sum(triple[0])
    own_ext[VALUE_B : VALUE_B + 1, :] += column_sum(triple[2])
    row = lax.broadcasted_iota(jnp.int32, (24, MODEL), 0)
    own_ext[16:40, :] = small[16:40, :] + 0.25 * grad[0:24]
    own_ext[40:64, :] = small[40:64, :] + 0.25 * (
        write[0:24] + jnp.where(row >= SLOTS, jnp.broadcast_to(norm, (24, MODEL)), 0.0)
    )
    half = pl.ds(pl.multiple_of(core * 32, 8), 32)
    other = pl.ds(pl.multiple_of((1 - core) * 32, 8), 32)
    small_core = send(own_ext.at[other], ecore, t_s.at[0], t_r.at[0], "core", 1)
    wave((0, 5), (1, 4), (2, 3), (3, 2))
    small_core.wait_recv()
    ecore[...] = own_ext[half, :] + ecore[...]
    small_x = [
        send(
            ecore.at[pl.ds(pl.multiple_of(turn(at["x"], d) * 8, 8), 8)],
            ex.at[d - 1], t_s.at[d], t_r.at[d], "x", d,
        )
        for d in (1, 2, 3)
    ]
    input_grad[...] = (
        dh1[...]
        + dot_t(triple[0, 0:ROWS, :], wq[...])
        + dot_t(triple[1, 0:ROWS, :], wk[...])
        + dot_t(triple[2, 0:ROWS, :], wv[...])
    ).reshape(1, SEGS, BLOCK, MODEL)
    wave((0, 6), (1, 5), (2, 4), (3, 3))
    for copy in small_x:
        copy.wait_recv()
    ey[pl.ds(at["y"], 1)] = (
        ecore[pl.ds(pl.multiple_of(at["x"] * 8, 8), 8), :] + ex[0] + ex[1] + ex[2]
    )[None]
    small_y = [
        send(ey.at[at["y"]], ey.at[at["y"]], t_s.at[3 + d], t_r.at[3 + d], "y", d)
        for d in (1, 2, 3)
    ]
    wave((0, 7), (1, 6), (2, 5), (3, 4))
    for copy in small_y:
        copy.wait_recv()
    ez[pl.ds(at["z"], 1)] = (ey[0] + ey[1] + ey[2] + ey[3])[None]
    small_z = [
        send(ez.at[at["z"]], ez.at[at["z"]], t_s.at[6 + d], t_r.at[6 + d], "z", d)
        for d in (1, 2, 3)
    ]
    wave((0, 8), (1, 7), (2, 6), (3, 5))
    for copy in small_z:
        copy.wait_recv()
    mine = pl.ds(pl.multiple_of(core * 32 + at["x"] * 8, 8), 8)
    ext[mine, :] = ez[0] + ez[1] + ez[2] + ez[3]
    small_back = [
        send(ext.at[mine], ext.at[mine], t_s.at[9 + d], t_r.at[9 + d], "x", d) for d in (1, 2, 3)
    ]
    wave((1, 8), (2, 7), (3, 6), (0, 9))
    for copy in small_back:
        copy.wait_recv()
    small_last = send(ext.at[half], ext.at[half], t_s.at[13], t_r.at[13], "core", 1)
    wave((2, 8), (3, 7), (1, 9), (3, 8), (2, 9))
    small_last.wait_recv()
    wave((3, 9))
    for copy in started:
        copy.wait_send()
    for copy in stores:
        copy.wait()


def finish_all(near, far):
    def buffer(*dims):
        return pltpu.VMEM(dims, LOW)

    def wide_buffer(*dims):
        return pltpu.VMEM(dims, F32)

    pairs = [
        (3,), (3,), (4, 3), (4, 3, 2), (4, 3, 2), (4, 3, 3), (4, 3, 3), (4, 3, 3), None,
        (4, 3, 2), (4, 3, 2), (4, 3, 5), (14,),
    ]
    sems = [DMA((15,))]
    for dims in pairs:
        if dims is None:
            sems += [DMA((4, 3)), pltpu.SemaphoreType.REGULAR((4,))]
        else:
            sems += [DMA(dims), DMA(dims)]
    return pl.pallas_call(
        finish_kernel,
        out_shape=(
            shape((12 * MODEL, MODEL)),
            shape((1, SEGS, BLOCK, MODEL), F32),
            shape((64, MODEL), F32),
        ),
        in_specs=[VMEM] * len(near) + [ANY] * len(far),
        out_specs=(ANY, VMEM, VMEM),
        scratch_shapes=[
            buffer(SEGS, BLOCK, MODEL),
            buffer(SEGS, MEMORY, MODEL),
            buffer(4, ROWS - BLOCK, TRIPLE),
            buffer(4, ROWS, GROUP),
            buffer(2, 4, PAD, GROUP),
            wide_buffer(ROWS, MODEL),
            buffer(MOST, MODEL),
            buffer(MOST, INNER),
            buffer(MOST, INNER),
            buffer(MOST, MODEL),
            buffer(MOST, MODEL),
            buffer(MODEL, MODEL),
            buffer(MODEL, MODEL),
            buffer(MODEL, MODEL),
            buffer(FULL, MODEL),
            buffer(3, FULL, MODEL),
            buffer(4, MOST, GROUP),
            buffer(4, BLOCK, TRIPLE),
            buffer(SEGS, 4, MEMORY, TRIPLE),
            buffer(3, MEMORY, MODEL),
            buffer(12, MODEL, MODEL),
            buffer(4, 3, HALF, MODEL),
            buffer(4, 3, 2, SUB, MODEL),
            buffer(4, 3, 2, CHUNK, MODEL),
            buffer(4, 3, 3, SUB, SIDE),
            buffer(4, 3, 4, SUB, SIDE),
            wide_buffer(64, MODEL),
            wide_buffer(32, MODEL),
            wide_buffer(3, 8, MODEL),
            wide_buffer(4, 8, MODEL),
            wide_buffer(4, 8, MODEL),
        ]
        + sems,
        compiler_params=pltpu.CompilerParams(
            collective_id=3, has_side_effects=True, vmem_limit_bytes=62 << 20
        ),
        name="weights_and_sums",
    )(*near, *far)


def widen_kernel(
    count, packed, ext, grad_in, layer_in,
    layer_out, grad_out, query_w, key_w, value_w, mixer_w, inner_w, outer_w, query_b, value_b, mixer_b, gain_1, shift_1,
    inner_b, outer_b, gain_2, shift_2, init, offset, norm,
    low, wide, in_sem, out_sem,
):
    through = pltpu.make_async_copy(grad_in, grad_out, in_sem.at[12])
    through.start()
    layer_through = pltpu.make_async_copy(layer_in, layer_out, in_sem.at[13])
    layer_through.start()
    def rows(i):
        return pl.ds(i * MODEL, MODEL)

    loads = [pltpu.make_async_copy(packed.at[rows(i)], low.at[i], in_sem.at[i]) for i in range(12)]
    for copy in loads:
        copy.start()
    targets = [query_w, key_w, value_w, mixer_w]
    targets += [inner_w.at[:, rows(i)] for i in range(4)]
    targets += [outer_w.at[rows(i)] for i in range(4)]
    stores = []
    for i in range(12):
        loads[i].wait()

        def body(j, carry):
            part = pl.ds(pl.multiple_of(j * 96, 96), 96)
            wide[i, part, :] = low[i, part, :].astype(F32)
            return carry

        lax.fori_loop(0, 8, body, 0)
        stores.append(pltpu.make_async_copy(wide.at[i], targets[i], out_sem.at[i]))
        stores[-1].start()
    singles = (
        (query_b, QUERY_B), (value_b, VALUE_B), (mixer_b, MIXER_B), (gain_1, GAIN_1),
        (shift_1, SHIFT_1), (outer_b, OUTER_B), (gain_2, GAIN_2), (shift_2, SHIFT_2),
    )
    for ref, row in singles:
        ref[...] = ext[row : row + 1, :].reshape(MODEL)
    inner_b[...] = jnp.concatenate([ext[8 + i : 9 + i, :] for i in range(4)], axis=1).reshape(INNER)
    init[...] = ext[16 : 16 + SLOTS, :]
    offset[...] = ext[40 : 40 + SLOTS, :]
    norm[...] = jnp.sqrt(ext[60:61, 0:1] * (1.0 / count))
    for copy in stores:
        copy.wait()
    through.wait()
    layer_through.wait()


def widen(packed, ext, input_grad, layer_output, chains):
    square = shape((MODEL, MODEL), F32)
    line = shape((MODEL,), F32)
    slots = shape((SLOTS, MODEL), F32)
    return pl.pallas_call(
        functools.partial(widen_kernel, chains * SEGS * SLOTS * MODEL),
        out_shape=(
            shape((1, SEGS, BLOCK, MODEL)), shape((1, SEGS, BLOCK, MODEL), F32), square, square, square, square, shape((MODEL, INNER), F32), shape((INNER, MODEL), F32),
            line, line, line, line, line, shape((INNER,), F32), line, line, line, slots, slots,
            shape((1, 1), F32),
        ),
        in_specs=[ANY, VMEM, VMEM, VMEM],
        out_specs=(ANY,) * 8 + (VMEM,) * 12,
        scratch_shapes=[
            pltpu.VMEM((12, MODEL, MODEL), LOW),
            pltpu.VMEM((12, MODEL, MODEL), F32),
            DMA((14,)),
            DMA((12,)),
        ],
        compiler_params=pltpu.CompilerParams(vmem_limit_bytes=60 << 20),
        name="widen",
    )(packed, ext, input_grad, layer_output)


def shards(
    tokens, documents, resets, cotangent, query_weight, query_bias, key_weight, value_weight,
    value_bias, mixer_weight, mixer_bias, first_gain, first_shift, inner_weight, inner_bias,
    outer_weight, outer_bias, second_gain, second_shift, memory_init, write_offset,
):
    weights = (query_weight, key_weight, value_weight, mixer_weight, inner_weight, outer_weight)
    vectors = (
        query_bias, value_bias, mixer_bias, first_gain, first_shift, outer_bias, second_gain,
        second_shift,
    )
    tok = tokens[0]
    (
        layer_output, orow, ow, xm, ub, act, dz, df, da, dh1, sums, inner_sum,
        drow, dmem, ubw, gw, dzw, dfw, daw, small, dlast, mlast, dh1w,
    ) = layer(
        resets, tok, cotangent[0], documents[0], memory_init, write_offset, vectors, inner_bias,
        weights,
    )
    packed, input_grad, ext = finish_all(
        (sums, inner_sum, small, ubw, gw, dzw, dfw, daw, dlast, mlast, dh1w),
        (ub, act, dz, df, da) + weights[:3] + (tok, xm, drow, dmem, orow, ow, dh1),
    )
    (
        layer_output, input_grad, query_w, key_w, value_w, mixer_w, inner_w, outer_w, query_b, value_b, mixer_b, gain_1,
        shift_1, inner_b, outer_b, gain_2, shift_2, init, offset, memory_norm,
    ) = widen(packed, ext, input_grad, layer_output, lax.axis_size("chain"))
    return (
        layer_output, input_grad, query_w, query_b, key_w, value_w, value_b, mixer_w, mixer_b,
        gain_1, shift_1, inner_w, inner_b, outer_w, outer_b, gain_2, shift_2, init, offset,
        memory_norm.reshape(()),
    )


def solution(mesh):
    tokens = P("chain", None, "seq", None)
    in_specs = (tokens, P("chain", None, "seq"), P("chain", None), tokens) + (P(),) * 17
    out_specs = (tokens, tokens) + (P(),) * 18
    return jax.shard_map(shards, mesh=mesh, in_specs=in_specs, out_specs=out_specs, check_vma=False)
```
